128 devices in a mesh: fsdp: 2 (over z_lo), ctx: 64 (over x, y, z_hi, core).
Axes of the slice: x: 4, y: 4, z: 4 (z_hi: 2, z_lo: 2; z = z_hi * 2 + z_lo), core: 2. Of those that a mesh axis runs over, the one named last changes fastest.
Arguments:
- tokens: bfloat16 [2, 8192, 896], P('fsdp', 'ctx'), may hold values from -16 to 16
- block_index: int32 [2, 128], P('fsdp'), may hold values from 0 to 127, as said below
- positions: int32 [2, 8192], P('fsdp', 'ctx'), may hold values from 0 to 12287, as said below
- cotangent: bfloat16 [2, 8192, 896], P('fsdp', 'ctx'), may hold values from -6 to 6
- norm_attn: bfloat16 [896], replicated, may hold values from 0.099609375 to 1.8984375
- w_q: bfloat16 [896, 896], P('fsdp'), may hold values from -0.1875 to 0.1875
- b_q: bfloat16 [896], replicated, may hold values from -3 to 3
- w_k: bfloat16 [896, 128], P('fsdp'), may hold values from -0.1875 to 0.1875
- b_k: bfloat16 [128], replicated, may hold values from -3 to 3
- w_v: bfloat16 [896, 128], P('fsdp'), may hold values from -0.1875 to 0.1875
- b_v: bfloat16 [128], replicated, may hold values from -3 to 3
- w_o: bfloat16 [896, 896], P('fsdp'), may hold values from -3 to 3
- norm_mlp: bfloat16 [896], replicated, may hold values from 0.099609375 to 1.8984375
- w_gate: bfloat16 [896, 4864], P('fsdp'), may hold values from -0.1875 to 0.1875
- w_up: bfloat16 [896, 4864], P('fsdp'), may hold values from -0.1875 to 0.1875
- w_down: bfloat16 [4864, 896], P('fsdp'), may hold values from -0.078125 to 0.078125
Outputs:
- mixed_out: bfloat16 [2, 8192, 896], P('fsdp', 'ctx')
- d_tokens: float32 [2, 8192, 896], P('fsdp', 'ctx')
- grad_w_q: float32 [896, 896], P(('fsdp', 'ctx'))
- grad_w_k: float32 [896, 128], P(('fsdp', 'ctx'))
- grad_w_v: float32 [896, 128], P(('fsdp', 'ctx'))
- grad_w_o: float32 [896, 896], P(('fsdp', 'ctx'))
- grad_w_gate: float32 [896, 4864], P(('fsdp', 'ctx'))
- grad_w_up: float32 [896, 4864], P(('fsdp', 'ctx'))
- grad_w_down: float32 [4864, 896], P(('fsdp', 'ctx'))
- grad_norm_attn: float32 [896], replicated
- grad_norm_mlp: float32 [896], replicated
- grad_b_q: float32 [896], replicated
- grad_b_k: float32 [128], replicated
- grad_b_v: float32 [128], replicated
The draws below stay inside these ranges and needn't reach their ends.
Inputs may be any that keep to these rules, and one draw needn't show every extreme that they name: `block_index`: each row is a permutation in which entries 2 c and 2 c + 1 add up to 127. Taken in the order of places, each sequence's positions start at 0 and rise by 1 or 2 from token to token, by 2 at exactly 4096 of the steps, so the last place holds the most.
All inputs are finite; a program needn't handle non-finite values.
Results may differ from the reference program's by a relative error of at most 0.025.
Values may be sent and summed in bfloat16 or wider, within the bound.
A program may use at most 192 MiB of HBM per device.

```python
import jax
import jax.numpy as jnp
from jax import lax

D = 896
H = 14
KVH = 2
HD = 64
FF = 4864
QW = 896
KW = 128
SEQS = 2
BLOCKS = 128
SEQ_LEN = 8192


def paired_order(key):

    def one_sequence(seq_key):
        perm_key, flip_key = jax.random.split(seq_key)
        pairs = jax.random.permutation(perm_key, BLOCKS // 2)
        flips = jax.random.randint(flip_key, (BLOCKS // 2,), 0, 2)
        leading = jnp.where(flips == 1, BLOCKS - 1 - pairs, pairs)
        return jnp.stack([leading, BLOCKS - 1 - leading], 1).reshape(BLOCKS)
    return jax.vmap(one_sequence)(jax.random.split(key, SEQS)).astype(jnp.int32)


def draw_block_index(key, part):
    order = paired_order(key)
    return order


def draw_positions(key, part):
    order = paired_order(key)
    key = jax.random.fold_in(key, 2)

    def step_row(row_key):
        shuffled = jax.random.permutation(row_key, SEQ_LEN - 1)
        doubled = (shuffled < SEQ_LEN // 2).astype(jnp.int32)
        return jnp.concatenate([jnp.zeros((1,), jnp.int32), 1 + doubled])
    steps = jax.vmap(step_row)(jax.random.split(key, SEQS))
    natural = jnp.cumsum(steps, axis=1).astype(jnp.int32)
    width = SEQ_LEN // BLOCKS

    def one_sequence(row, picks):
        return row.reshape(BLOCKS, width)[picks].reshape(SEQ_LEN)
    return jax.vmap(one_sequence)(natural, order).astype(jnp.int32)


def spiked(values, stream_key, source, target, shards_of, factor):
    def block_of(position):
        return (jnp.arange(values.shape[position]) // (values.shape[position] // shards_of)).reshape((-1,) + (1,) * (values.ndim - 1 - position))

    one_side = jax.random.permutation(stream_key, shards_of)[block_of(target)]
    far = (block_of(target) + shards_of // 2) % shards_of
    return jnp.where((block_of(source) == one_side) | (block_of(source) == far), factor * values, values)


def steps_of(rng, shape, cuts, least, top_value):
    level = 1.0
    for axis_at, shards_of in cuts:
        steps = jax.random.uniform(jax.random.fold_in(jax.random.fold_in(rng, 6), axis_at), (shards_of,), jnp.float32, least / len(cuts), top_value / len(cuts))
        level = level * jnp.repeat(jnp.exp(steps), shape[axis_at] // shards_of).reshape((-1,) + (1,) * (len(shape) - 1 - axis_at))
    return level


def gaussian(own_key, shape, scale, most, cuts=(), held_as=jnp.bfloat16):
    loudness = steps_of(own_key, shape, cuts, -0.22, 0.18) if cuts else 1.0
    array = jax.random.normal(own_key, shape, jnp.float32) * scale * loudness
    return jnp.minimum(jnp.maximum(array, -most), most).astype(held_as)


def noise_with(rng, dims, scale, limit, cuts, heavy, kind=jnp.bfloat16):
    drawn = scale * jax.random.normal(rng, dims, jnp.float32)
    if cuts:
        drawn = drawn * steps_of(rng, dims, cuts, -0.22, 0.18)
    return jnp.clip(spiked(drawn, jax.random.fold_in(rng, 3), *heavy), -limit, limit).astype(kind)


def setup_inputs(seed: int = 0) -> dict:
    streams_of = jax.random.split(jax.random.key(seed), 17)
    tokens = noise_with(streams_of[0], (SEQS, SEQ_LEN, D), 1.0, 16.0, ((0, 2), (1, 64)), (1, 2, 64, 4.0))
    block_index = draw_block_index(jax.random.fold_in(streams_of[16], 71), 0)
    positions = draw_positions(jax.random.fold_in(streams_of[16], 71), 0)
    cotangent = gaussian(streams_of[3], (SEQS, SEQ_LEN, D), 1.0, 6.0, ((0, 2), (1, 64)))
    norm_attn = jnp.clip(1.0 + 0.18 * jax.random.normal(streams_of[4], (D,), jnp.float32), 0.099609375, 1.8984375).astype(jnp.bfloat16)
    w_q = gaussian(streams_of[5], (D, QW), D ** -0.5, 0.1875, ((0, 2),))
    b_q = gaussian(streams_of[6], (QW,), 0.5, 3.0)
    w_k = gaussian(streams_of[7], (D, KW), D ** -0.5, 0.1875, ((0, 2),))
    b_k = gaussian(streams_of[8], (KW,), 0.5, 3.0)
    w_v = gaussian(streams_of[9], (D, KW), D ** -0.5, 0.1875, ((0, 2),))
    b_v = gaussian(streams_of[10], (KW,), 0.5, 3.0)
    w_o = gaussian(streams_of[11], (QW, D), ((SEQ_LEN // 32) ** 0.5 * QW ** -0.5), 3.0, ((0, 2),))
    norm_mlp = jnp.clip(1.0 + 0.18 * jax.random.normal(streams_of[12], (D,), jnp.float32), 0.099609375, 1.8984375).astype(jnp.bfloat16)
    w_gate = gaussian(streams_of[13], (D, FF), D ** -0.5, 0.1875, ((0, 2),))
    w_up = gaussian(streams_of[14], (D, FF), D ** -0.5, 0.1875, ((0, 2),))
    w_down = gaussian(streams_of[15], (FF, D), FF ** -0.5, 0.078125, ((0, 2),))
    return dict(tokens=tokens, block_index=block_index, positions=positions, cotangent=cotangent, norm_attn=norm_attn, w_q=w_q, b_q=b_q, w_k=w_k, b_k=b_k, w_v=w_v, b_v=b_v, w_o=w_o, norm_mlp=norm_mlp, w_gate=w_gate, w_up=w_up, w_down=w_down)


@jax.custom_vjp
def low(v):
    return lax.optimization_barrier(v.astype(jnp.bfloat16)).astype(jnp.float32)

@jax.custom_vjp
def low_back(v):
    return v

def low_keep(v):
    return (low(v), None)

def low_pass(kept, grad):
    return (grad,)

def back_keep(v):
    return (v, None)

def back_low(kept, grad):
    return (low(grad),)
low.defvjp(low_keep, low_pass)
low_back.defvjp(back_keep, back_low)
EPSILON = 1e-06
THETA = 1000000.0
MASKED = -1e+30
HIGHEST = lax.Precision.HIGHEST

def rope_tables(positions, width):
    halfway = width // 2
    freq = THETA ** (-(jnp.arange(halfway, dtype=jnp.float32) * 2.0 / width))
    angle = positions.astype(jnp.float32)[:, None] * freq[None, :]
    cosine = jnp.cos(angle)
    sine = jnp.sin(angle)
    return (jnp.concatenate([cosine, cosine], -1), jnp.concatenate([sine, sine], -1))

def rotate(field, cosine, sine):
    halfway = field.shape[-1] // 2
    turned = jnp.concatenate([-field[..., halfway:], field[..., :halfway]], -1)
    return field * cosine[:, None, :] + turned * sine[:, None, :]

def rms_norm(field, gain):
    inverse = lax.rsqrt(lax.optimization_barrier(jnp.mean(field * field, axis=-1, keepdims=True)) + EPSILON)
    return field * inverse * gain

def layer(field, positions, norm_attn, w_q, b_q, w_k, b_k, w_v, b_v, w_o, norm_mlp, w_gate, w_up, w_down):
    length = field.shape[0]
    group = H // KVH
    cosine, sine = rope_tables(positions, HD)
    normed = low(rms_norm(field, norm_attn))
    q_lin = low_back(jnp.dot(normed, w_q, precision=HIGHEST) + b_q)
    k_lin = low_back(jnp.dot(normed, w_k, precision=HIGHEST) + b_k)
    v_lin = low(low_back(jnp.dot(normed, w_v, precision=HIGHEST) + b_v))
    queries = low(rotate(q_lin.reshape(length, H, HD), cosine, sine) * HD ** (-0.5))
    queries = queries.reshape(length, KVH, group, HD)
    keys = low(rotate(k_lin.reshape(length, KVH, HD), cosine, sine))
    values = v_lin.reshape(length, KVH, HD)
    places = jnp.arange(length, dtype=jnp.int32)
    query_block = min(length, 512)

    def attend(start):
        picked = lax.dynamic_slice_in_dim(queries, start, query_block, 0)
        scores = low_back(jnp.einsum('qkgd,skd->kgqs', picked, keys, precision=HIGHEST))
        query_places = start + jnp.arange(query_block, dtype=jnp.int32)
        allowed = places[None, :] <= query_places[:, None]
        scores = jnp.where(allowed, scores, MASKED)
        top = lax.optimization_barrier(jnp.max(scores, axis=-1, keepdims=True))
        lse = top + jnp.log(lax.optimization_barrier(jnp.sum(jnp.exp(scores - top), axis=-1, keepdims=True)))
        probs = low(jnp.exp(scores - lse))
        return jnp.einsum('kgqs,skd->qkgd', probs, values, precision=HIGHEST)
    starts = (jnp.arange(length // query_block, dtype=jnp.int32) * query_block).astype(jnp.int32)
    mixed = lax.map(jax.checkpoint(attend), starts).reshape(length, H * HD)
    merged = low(low_back(mixed))
    attn_out = low_back(jnp.dot(merged, w_o, precision=HIGHEST))
    hidden = field + attn_out
    normed2 = low(rms_norm(hidden, norm_mlp))
    gate = low_back(jnp.dot(normed2, w_gate, precision=HIGHEST))
    up = low_back(jnp.dot(normed2, w_up, precision=HIGHEST))
    inner = low(jax.nn.silu(gate) * up)
    return hidden + low_back(jnp.dot(inner, w_down, precision=HIGHEST))

def reorder(field, order):
    blocks = order.shape[1]

    def one_sequence(row, picks):
        shaped = row.reshape((blocks, row.shape[0] // blocks) + row.shape[1:])
        return shaped[picks].reshape(row.shape)
    return jax.vmap(one_sequence)(field, order)

def reference(tokens, block_index, positions, cotangent, norm_attn, w_q, b_q, w_k, b_k, w_v, b_v, w_o, norm_mlp, w_gate, w_up, w_down):
    inverse = jnp.argsort(block_index, axis=1).astype(jnp.int32)
    weights = tuple((item.astype(jnp.float32) for item in (norm_attn, w_q, b_q, w_k, b_k, w_v, b_v, w_o, norm_mlp, w_gate, w_up, w_down)))
    field_nat = reorder(tokens.astype(jnp.float32), inverse)
    place_nat = reorder(positions, inverse)
    grad_nat = reorder(cotangent.astype(jnp.float32), inverse)

    def one(totals, item):
        field, place, grad = item

        def apply(inputs, *params):
            return layer(inputs, place, *params)
        result, pull = jax.vjp(apply, field, *weights)
        grads = pull(grad)
        totals = tuple((left + right for left, right in zip(totals, grads[1:])))
        return (totals, (result, grads[0]))
    zeros = tuple((jnp.zeros_like(item) for item in weights))
    totals, (results, input_grads) = lax.scan(one, zeros, (field_nat, place_nat, grad_nat))
    mixed_out = reorder(results, block_index).astype(jnp.bfloat16)
    d_tokens = reorder(input_grads, block_index)
    g_norm_attn, g_wq, g_bq, g_wk, g_bk, g_wv, g_bv, g_wo, g_norm_mlp, g_gate, g_up, g_down = totals
    return (mixed_out, d_tokens, g_wq, g_wk, g_wv, g_wo, g_gate, g_up, g_down, g_norm_attn, g_norm_mlp, g_bq, g_bk, g_bv)
```

```python
import functools

import jax
import jax.numpy as jnp
import numpy as np
from jax import lax
from jax.experimental import pallas as pl
from jax.experimental.pallas import tpu as pltpu
from jax.sharding import PartitionSpec as P

D = 896
H = 14
HD = 64
HALF = 448
FF = 4864
SLICE = 608
PADDED = 640
CHUNK = 256
EPSILON = 1e-06
THETA = 1000000.0
MASKED = -1e30
MESH = pl.DeviceIdType.MESH
F32 = jnp.float32
BF16 = jnp.bfloat16
VMEM_LIMIT = 56 * 1024 * 1024


def own_place():
    f, c = lax.axis_index("fsdp"), lax.axis_index("ctx")
    zh = lax.rem(lax.div(c, 2), 2)
    return (lax.div(c, 16), lax.rem(lax.div(c, 4), 4), zh * 2 + f, lax.rem(c, 2))


def device(place):
    x, y, z, core = place
    return (lax.rem(z, 2), (x * 4 + y) * 4 + 2 * lax.div(z, 2) + core)


def turned(value, step):
    return lax.rem(value + (step + 4), 4)


def shifted(place, axis, step):
    moved = list(place)
    moved[axis] = turned(place[axis], step)
    return tuple(moved)


def partner(place):
    return place[:3] + (1 - place[3],)


def greet(places):
    barrier = pltpu.get_barrier_semaphore()
    for place in places:
        pl.semaphore_signal(barrier, inc=1, device_id=device(place), device_id_type=MESH)
    pl.semaphore_wait(barrier, len(places))


class Links:
    def __init__(self, send, recv):
        self.send, self.recv, self.opened = send, recv, []

    def start(self, src, dst, place):
        at = len(self.opened)
        copy = pltpu.make_async_remote_copy(
            src_ref=src,
            dst_ref=dst,
            send_sem=self.send.at[at],
            recv_sem=self.recv.at[at],
            device_id=device(place),
            device_id_type=MESH,
        )
        copy.start()
        self.opened.append(copy)
        return copy

    def close(self):
        for copy in self.opened:
            copy.wait_send()


def ring_gather(links, slot, half, place, axis):
    me = place[axis]
    right, left = shifted(place, axis, 1), shifted(place, axis, -1)
    first = links.start(slot(me), slot(me), right)
    second = links.start(slot(me), slot(me), left)
    yield
    before, after = turned(me, -1), turned(me, 1)
    first.wait_recv()
    third = links.start(half(before, 0), half(before, 0), right)
    yield
    second.wait_recv()
    fourth = links.start(half(after, 1), half(after, 1), left)
    yield
    third.wait_recv()
    fourth.wait_recv()


def ring_reduce(links, part, low, high, place, axis, emit):
    me = place[axis]
    right, left = shifted(place, axis, 1), shifted(place, axis, -1)
    before, after, far = turned(me, -1), turned(me, 1), turned(me, 2)
    first = links.start(part(far, 0), low.at[0], right)
    second = links.start(part(far, 1), high.at[0], left)
    third = links.start(part(after, 1), high.at[1], right)
    fourth = links.start(part(before, 0), low.at[1], left)
    yield
    first.wait_recv()
    low[0] = (low[0].astype(F32) + part(after, 0)[...].astype(F32)).astype(low.dtype)
    fifth = links.start(low.at[0], low.at[2], right)
    second.wait_recv()
    high[0] = (high[0].astype(F32) + part(before, 1)[...].astype(F32)).astype(high.dtype)
    sixth = links.start(high.at[0], high.at[2], left)
    yield
    fourth.wait_recv()
    fifth.wait_recv()
    emit(0, part(me, 0)[...].astype(F32) + low[1].astype(F32) + low[2].astype(F32))
    third.wait_recv()
    sixth.wait_recv()
    emit(1, part(me, 1)[...].astype(F32) + high[1].astype(F32) + high[2].astype(F32))


def in_turn(*streams):
    waiting = list(streams)
    while waiting:
        still = []
        for stream in waiting:
            try:
                next(stream)
            except StopIteration:
                continue
            still.append(stream)
        waiting = still


def local_norm(field, gain):
    inverse = lax.rsqrt(jnp.mean(field * field, axis=-1, keepdims=True) + EPSILON)
    return field * inverse * gain, inverse


def norm_backward(field, inverse, gain, grad):
    scaled = grad * gain
    grad_gain = jnp.sum(grad * field * inverse, axis=0, keepdims=True)
    mean = jnp.mean(scaled * field, axis=-1, keepdims=True)
    return inverse * scaled - field * (inverse * inverse * inverse) * mean, grad_gain


def dot(left, right, contract=((1,), (0,))):
    return lax.dot_general(left, right, (contract, ((), ())), preferred_element_type=F32)


def whole(count):
    return [pl.BlockSpec(memory_space=pltpu.VMEM)] * count


def shape(dims, dtype):
    return jax.ShapeDtypeStruct(dims, dtype)


def remote_call(kernel, collective_id, outs, copies, scratch, *args):
    return pl.pallas_call(
        kernel,
        out_shape=outs,
        in_specs=whole(len(args)),
        out_specs=[pl.BlockSpec(memory_space=pltpu.VMEM)] * len(outs),
        scratch_shapes=list(scratch)
        + [pltpu.SemaphoreType.DMA((copies,)), pltpu.SemaphoreType.DMA((copies,))],
        compiler_params=pltpu.CompilerParams(
            collective_id=collective_id, has_side_effects=True, vmem_limit_bytes=VMEM_LIMIT
        ),
    )(*args)


def enter_kernel(
    tokens, gain, table, weight, bias, cot,
    normed_all, table_all, weight_all, queries, kv_a, kv_b, cot_all,
    send, recv,
):
    place = own_place()
    x, y, z, core = place
    f, zh = lax.rem(z, 2), lax.div(z, 2)
    other, up, down, far = partner(place), shifted(place, 2, 1), shifted(place, 2, -1), shifted(place, 2, 2)
    greet(
        [other, up, down, far]
        + [shifted(place, axis, step) for axis in (0, 1) for step in (1, -1)]
    )
    links = Links(send, recv)
    base = pl.multiple_of(f * HALF, HALF)
    w_down = links.start(weight.at[pl.ds(0, 224)], weight_all.at[pl.ds(base, 224)], down)
    w_up = links.start(weight.at[pl.ds(224, 224)], weight_all.at[pl.ds(base + 224, 224)], up)
    normed, _ = local_norm(tokens[...].astype(F32), gain[...])
    normed_all[core] = normed.astype(BF16)
    n_copy = links.start(normed_all.at[core], normed_all.at[core], other)
    table_all[core] = table[...]
    t_copy = links.start(table_all.at[core], table_all.at[core], other)
    cot_all[z, core] = cot[...]
    c_copy = links.start(cot_all.at[z, core], cot_all.at[z, core], other)
    weight_all[pl.ds(base, HALF)] = weight[...]
    n_copy.wait_recv()
    t_copy.wait_recv()
    w_down.wait_recv()
    w_up.wait_recv()
    lin = dot(normed_all[...].reshape(256, D), weight_all[...]) + bias[...]
    turn = lin[:, :512]
    lane = lax.broadcasted_iota(jnp.int32, (256, 512), 1)
    swapped = jnp.where(lax.rem(lane, 64) < 32, -pltpu.roll(turn, 480, 1), pltpu.roll(turn, 32, 1))
    both = table_all[...].reshape(256, 128)
    cosine = jnp.concatenate([both[:, :64]] * 8, axis=1)
    sine = jnp.concatenate([both[:, 64:]] * 8, axis=1)
    rotated = turn * cosine + swapped * sine
    queries[...] = (rotated[:, :HALF] * HD**-0.5).astype(BF16)
    kv = jnp.concatenate([rotated[:, HALF:512], lin[:, 512:576]], axis=1).astype(BF16)
    kv_a[x, y, zh] = kv[:128]
    kv_b[x, y, zh] = kv[128:]
    a_far = links.start(kv_a.at[x, y, zh], kv_a.at[x, y, zh], far)
    b_far = links.start(kv_b.at[x, y, zh], kv_b.at[x, y, zh], far)

    def stream_a():
        a_far.wait_recv()
        yield from ring_gather(
            links, lambda k: kv_a.at[x, k], lambda k, h: kv_a.at[x, k, h], place, 1
        )
        yield from ring_gather(
            links, lambda k: kv_a.at[k], lambda k, h: kv_a.at[k, pl.ds(2 * h, 2)], place, 0
        )

    def stream_b():
        b_far.wait_recv()
        yield from ring_gather(
            links, lambda k: kv_b.at[k, y], lambda k, h: kv_b.at[k, y, h], place, 0
        )
        yield from ring_gather(
            links,
            lambda k: kv_b.at[pl.ds(0, 4), k],
            lambda k, h: kv_b.at[pl.ds(2 * h, 2), k],
            place,
            1,
        )

    in_turn(stream_a(), stream_b(), shared_gather(links, cot_all, place, c_copy))
    links.close()


def shared_gather(links, blocks, place, own_copy):
    z, core = place[2], place[3]
    other = partner(place)
    copies = [own_copy]
    ring = ring_gather(
        links,
        lambda k: blocks.at[k, core],
        lambda k, h: blocks.at[k, core, pl.ds(64 * h, 64)],
        place,
        2,
    )
    next(ring)
    yield
    next(ring)
    before = turned(z, -1)
    copies.append(links.start(blocks.at[before, core], blocks.at[before, core], other))
    yield
    next(ring)
    after = turned(z, 1)
    copies.append(links.start(blocks.at[after, core], blocks.at[after, core], other))
    yield
    for _ in ring:
        yield
    last = turned(z, 2)
    copies.append(links.start(blocks.at[last, core], blocks.at[last, core], other))
    yield
    for copy in copies:
        copy.wait_recv()


def shared_reduce(links, blocks, arrived, paired, low, high, place, emit):
    z, core = place[2], place[3]
    other = partner(place)
    copy = links.start(blocks.at[pl.ds(0, 4), 1 - core], arrived, other)
    yield
    copy.wait_recv()
    for k in range(4):
        paired[k] = (arrived[k].astype(F32) + blocks[k, core].astype(F32)).astype(BF16)
    yield from ring_reduce(
        links, lambda k, h: paired.at[k, pl.ds(64 * h, 64)], low, high, place, 2, emit
    )


def hidden_kernel(mixed, w_o, tokens, gain, mixed_all, hidden, normed_all, send, recv):
    place = own_place()
    z, core = place[2], place[3]
    other = partner(place)
    greet([other, shifted(place, 2, 1), shifted(place, 2, -1)])
    links = Links(send, recv)
    copy = links.start(mixed, mixed_all.at[core], other)
    mixed_all[core] = mixed[...]
    copy.wait_recv()
    rows = pl.ds(pl.multiple_of(core * 128, 128), 128)
    branch = dot(mixed_all[0, rows], w_o[:HALF]) + dot(mixed_all[1, rows], w_o[HALF:])
    field = tokens[...].astype(F32) + branch
    hidden[...] = field
    normed, _ = local_norm(field, gain[...])
    normed_all[z, core] = normed.astype(BF16)
    own = links.start(normed_all.at[z, core], normed_all.at[z, core], other)
    in_turn(shared_gather(links, normed_all, place, own))
    links.close()


def branch_kernel(
    out_part, grad_part, hidden, cot, gain,
    mixed_out, grad_hidden, branch_all, grad_gain,
    arrived_o, paired_o, low_o, high_o, arrived_g, paired_g, low_g, high_g, grad_sum, send, recv,
):
    place = own_place()
    core = place[3]
    other = partner(place)
    greet([other, shifted(place, 2, 1), shifted(place, 2, -1)])
    links = Links(send, recv)

    def emit_out(h, value):
        rows = pl.ds(64 * h, 64)
        mixed_out[rows] = (hidden[rows] + value).astype(BF16)

    def emit_grad(h, value):
        grad_sum[pl.ds(64 * h, 64)] = value

    in_turn(
        shared_reduce(links, grad_part, arrived_g, paired_g, low_g, high_g, place, emit_grad),
        shared_reduce(links, out_part, arrived_o, paired_o, low_o, high_o, place, emit_out),
    )
    field = hidden[...]
    _, inverse = local_norm(field, gain[...])
    through, gains = norm_backward(field, inverse, gain[...], grad_sum[...])
    grad_gain[...] = gains
    total = cot[...].astype(F32) + through
    grad_hidden[...] = total
    branch_all[core] = total.astype(BF16)
    copy = links.start(branch_all.at[core], branch_all.at[core], other)
    copy.wait_recv()
    links.close()


def kv_reduce_kernel(part_a, part_b, total, mid_a, mid_b, end_a, end_b, *rest):
    slots, (send, recv) = rest[:-2], rest[-2:]
    far_a, far_b = slots[8], slots[9]
    place = own_place()
    x, y, z, core = place
    zh = lax.div(z, 2)
    far = shifted(place, 2, 2)
    greet([far] + [shifted(place, axis, step) for axis in (0, 1) for step in (1, -1)])
    links = Links(send, recv)

    def stream(part, mid, end, order, low1, high1, low2, high2, landing, base):
        def put_mid(h, value):
            mid[pl.ds(2 * h, 2)] = value.astype(BF16)

        def put_end(h, value):
            end[h] = value

        if order == 0:
            first = lambda k, h: part.at[k, pl.ds(2 * h, 2)]
        else:
            first = lambda k, h: part.at[pl.ds(2 * h, 2), k]
        yield from ring_reduce(links, first, low1, high1, place, order, put_mid)
        yield from ring_reduce(
            links, lambda k, h: mid.at[k, h], low2, high2, place, 1 - order, put_end
        )
        copy = links.start(end.at[1 - zh], landing, far)
        yield
        copy.wait_recv()
        total[pl.ds(base, 128)] = end[zh] + landing[...]

    in_turn(
        stream(part_a, mid_a, end_a, 0, *slots[0:4], far_a, 0),
        stream(part_b, mid_b, end_b, 1, *slots[4:8], far_b, 128),
    )
    links.close()


def mlp_grads_kernel(gate, up, down, rows_all, down_out, *rest):
    (
        mid_gate, mid_up, mid_down, end,
        g_low1, g_high1, g_low2, g_high2, u_low1, u_high1, u_low2, u_high2,
        d_low1, d_high1, d_low2, d_high2, send, recv,
    ) = rest
    place = own_place()
    x, y, z, core = place
    mine = z * 2 + core
    others = []
    for step in range(1, 8):
        at = lax.rem(mine + step, 8)
        others.append((x, y, lax.div(at, 2), lax.rem(at, 2)))
    greet(others + [shifted(place, axis, step) for axis in (0, 1) for step in (1, -1)])
    links = Links(send, recv)

    def wide(part, mid, order, low1, high1, low2, high2, column):
        def put_mid(h, value):
            mid[pl.ds(2 * h, 2)] = value.astype(BF16)

        def put_end(h, value):
            end[pl.ds(4 * h, 4), :, pl.ds(column, PADDED)] = value.reshape(4, 8, PADDED)

        if order == 0:
            first = lambda k, h: part.at[k, pl.ds(2 * h, 2)]
        else:
            first = lambda k, h: part.at[pl.ds(2 * h, 2), k]
        yield from ring_reduce(links, first, low1, high1, place, order, put_mid)
        yield from ring_reduce(
            links, lambda k, h: mid.at[k, pl.ds(32 * h, 32)], low2, high2, place, 1 - order, put_end
        )

    def tall():
        def put_mid(h, value):
            mid_down[pl.ds(2 * h, 2)] = value.reshape(2, 40, D)

        def put_end(h, value):
            down_out[pl.ds(24 * h, 24 - 8 * h)] = value

        yield from ring_reduce(
            links, lambda k, h: down.at[k, pl.ds(80 * h, 80)], d_low1, d_high1, place, 0, put_mid
        )
        yield from ring_reduce(
            links,
            lambda k, h: mid_down.at[k, pl.ds(24 * h, 24 - 8 * h)],
            d_low2,
            d_high2,
            place,
            1,
            put_end,
        )

    in_turn(
        wide(gate, mid_gate, 0, g_low1, g_high1, g_low2, g_high2, 0),
        wide(up, mid_up, 1, u_low1, u_high1, u_low2, u_high2, PADDED),
        tall(),
    )
    copies = []
    for to in others:
        copies.append(links.start(end.at[to[2] * 2 + to[3]], rows_all.at[mine], to))
    rows_all[mine] = end[mine]
    for copy in copies:
        copy.wait_recv()
    links.close()


def leave_kernel(
    part_q, part_o, grad_normed, grad_hidden, tokens, gain, vector,
    d_tokens, rows_q, rows_o, vector_out,
    half_sum, mid_q1, mid_q2, end_q, mid_o1, mid_o2, end_o,
    q_low1, q_high1, q_low2, q_high2, q_low3, q_high3,
    o_low1, o_high1, o_low2, o_high2, o_low3, o_high3,
    vec_now, vec_in, send, recv,
):
    place = own_place()
    x, y, z, core = place
    other = partner(place)
    greet([other] + [shifted(place, axis, step) for axis in (0, 1, 2) for step in (1, -1, 2)])
    links = Links(send, recv)
    copy = links.start(grad_normed.at[1 - core], half_sum, other)

    def grads(part, mid1, mid2, end, order, low1, high1, low2, high2, low3, high3, rows):
        def put1(h, value):
            mid1[pl.ds(2 * h, 2)] = value.astype(BF16)

        def put2(h, value):
            mid2[pl.ds(2 * h, 2)] = value

        def put3(h, value):
            end[h] = value

        if order == 0:
            first = lambda k, h: part.at[k, pl.ds(2 * h, 2)]
        else:
            first = lambda k, h: part.at[pl.ds(2 * h, 2), k]
        yield from ring_reduce(links, first, low1, high1, place, order, put1)
        yield from ring_reduce(
            links, lambda k, h: mid1.at[k, pl.ds(2 * h, 2)], low2, high2, place, 1 - order, put2
        )
        yield from ring_reduce(
            links, lambda k, h: mid2.at[k, pl.ds(8 * h, 8)], low3, high3, place, 2, put3
        )
        last = links.start(end.at[1 - core], rows.at[core], other)
        rows[core] = end[core]
        yield
        last.wait_recv()

    def sums():
        copy.wait_recv()
        grad = grad_normed[core] + half_sum[...]
        field = tokens[...].astype(F32)
        _, inverse = local_norm(field, gain[...])
        through, gains = norm_backward(field, inverse, gain[...], grad)
        d_tokens[...] = grad_hidden[...] + through
        vec_now[0] = vector[...]
        vec_now[0, :, pl.ds(0, D)] = gains
        yield
        trip = links.start(vec_now.at[0], vec_in.at[0], other)
        yield
        trip.wait_recv()
        vec_now[1] = vec_now[0] + vec_in[0]
        for stage, axis in enumerate((2, 1, 0)):
            trips = [
                links.start(
                    vec_now.at[1 + stage],
                    vec_in.at[1 + 3 * stage + at],
                    shifted(place, axis, step),
                )
                for at, step in enumerate((1, -1, 2))
            ]
            yield
            for trip in trips:
                trip.wait_recv()
            at = 1 + 3 * stage
            near = vec_in[at] + vec_in[at + 1]
            vec_now[2 + stage] = (vec_now[1 + stage] + vec_in[at + 2]) + near
        vector_out[...] = vec_now[4]

    in_turn(
        grads(
            part_q, mid_q1, mid_q2, end_q, 0, q_low1, q_high1, q_low2, q_high2, q_low3, q_high3,
            rows_q,
        ),
        grads(
            part_o, mid_o1, mid_o2, end_o, 1, o_low1, o_high1, o_low2, o_high2, o_low3, o_high3,
            rows_o,
        ),
        sums(),
    )
    links.close()


def natural_order(order, kv_a, kv_b, kv, kv_t):
    @pl.loop(0, 32)
    def _(chip):
        for t in range(4):
            block = kv_a[chip, pl.ds(64 * t, 64)] if t < 2 else kv_b[chip, pl.ds(64 * (t - 2), 64)]
            at = pl.multiple_of(order[4 * chip + t] * 64, 64)
            kv[pl.ds(at, 64)] = block

    @pl.loop(0, 8192 // CHUNK)
    def _(c):
        kv_t[c] = kv[pl.ds(pl.multiple_of(c * CHUNK, CHUNK), CHUNK)].T


def allowed_at(c, base):
    key = c * CHUNK + lax.broadcasted_iota(jnp.int32, (CHUNK, HALF), 0)
    lane = lax.broadcasted_iota(jnp.int32, (CHUNK, HALF), 1)
    return key <= base + lax.rem(lane, 64)


def attend_kernel(order, owned, kv_a, kv_b, query_t, out_t, lse, kv, kv_t, acc):
    natural_order(order, kv_a, kv_b, kv, kv_t)
    for t in range(4):
        spot = owned[t]
        q_t = query_t[t]
        last = lax.div(spot * 64, CHUNK)
        acc[...] = jnp.zeros_like(acc)

        def step(c, carry, masked):
            top, total = carry
            scores = dot(kv[pl.ds(pl.multiple_of(c * CHUNK, CHUNK), CHUNK)], q_t)
            if masked:
                scores = jnp.where(allowed_at(c, spot * 64), scores, MASKED)
            new_top = jnp.maximum(top, jnp.max(scores, axis=0, keepdims=True))
            probs = jnp.exp(scores - new_top)
            scale = jnp.exp(top - new_top)
            total = total * scale + jnp.sum(probs, axis=0, keepdims=True)
            acc[...] = acc[...] * scale + dot(kv_t[c, pl.ds(64, 64)], probs.astype(BF16))
            return new_top, total

        start = (jnp.full((1, HALF), MASKED, F32), jnp.zeros((1, HALF), F32))
        carry = lax.fori_loop(0, last, lambda c, carry: step(c, carry, False), start)
        top, total = step(last, carry, True)
        out_t[t] = acc[...] / total
        lse[t] = top + jnp.log(total)


def attend_back_kernel(
    order, owned, kv_a, kv_b, query_t, query, grad_t, grad, out_t, lse,
    grad_query_t, grad_a, grad_b, kv, kv_t, acc, acc_q,
):
    natural_order(order, kv_a, kv_b, kv, kv_t)
    acc[...] = jnp.zeros_like(acc)
    for t in range(4):
        spot = owned[t]
        last = lax.div(spot * 64, CHUNK)
        q_t, q, g_t, g = query_t[t], query[t], grad_t[t], grad[t]
        delta = jnp.sum(g_t[64:].astype(F32) * out_t[t], axis=0, keepdims=True)
        norm = lse[t]
        acc_q[...] = jnp.zeros_like(acc_q)

        def step(c, masked):
            rows = pl.ds(pl.multiple_of(c * CHUNK, CHUNK), CHUNK)
            block = kv[rows]
            scores = dot(block, q_t)
            if masked:
                scores = jnp.where(allowed_at(c, spot * 64), scores, MASKED)
            probs = jnp.exp(scores - norm)
            grad_probs = dot(block, g_t)
            grad_scores = (probs * (grad_probs - delta)).astype(BF16)
            acc[rows] += dot(probs.astype(BF16), g) + dot(grad_scores, q)
            acc_q[...] += dot(kv_t[c, pl.ds(0, 64)], grad_scores)

        def body(c, carry):
            step(c, False)
            return carry

        lax.fori_loop(0, last, body, 0)
        step(last, True)
        grad_query_t[t] = acc_q[...]

    @pl.loop(0, 32)
    def _(chip):
        for t in range(4):
            at = pl.multiple_of(order[4 * chip + t] * 64, 64)
            block = acc[pl.ds(at, 64)].astype(BF16)
            if t < 2:
                grad_a[chip, pl.ds(64 * t, 64)] = block
            else:
                grad_b[chip, pl.ds(64 * (t - 2), 64)] = block


def local_call(kernel, outs, scratch, scalars, flops, *args):
    return pl.pallas_call(
        kernel,
        out_shape=outs,
        in_specs=[pl.BlockSpec(memory_space=pltpu.SMEM)] * scalars + whole(len(args) - scalars),
        out_specs=[pl.BlockSpec(memory_space=pltpu.VMEM)] * len(outs),
        scratch_shapes=scratch,
        compiler_params=pltpu.CompilerParams(vmem_limit_bytes=VMEM_LIMIT),
        cost_estimate=pl.CostEstimate(flops=flops, bytes_accessed=8 << 20, transcendentals=1 << 23),
    )(*args)


def padded_columns(offset):
    row = lax.broadcasted_iota(jnp.int32, (768, PADDED), 0)
    col = lax.broadcasted_iota(jnp.int32, (768, PADDED), 1)
    inner = col % 40
    return ((row == offset + (col // 40) * 38 + inner) & (inner < 38)).astype(BF16)


def owner_columns():
    col = np.arange(1024)
    i, core, z, y, x = col % 8, col // 8 % 2, col // 16 % 4, col // 64 % 4, col // 256
    at = 7 * (64 * (z % 2) + 16 * x + 4 * y + 2 * (z // 2) + core) + i
    pick = np.zeros((D, 1024), np.float32)
    keep = i < 7
    pick[at[keep], col[keep]] = 1.0
    return jnp.asarray(pick, BF16)


def index_of(x, y, z, core):
    return (z % 2) * 64 + (x * 4 + y) * 4 + 2 * (z // 2) + core


def permutation(move):
    pairs = []
    for x in range(4):
        for y in range(4):
            for z in range(4):
                for core in range(2):
                    pairs.append((index_of(x, y, z, core), index_of(*move(x, y, z, core))))
    return pairs


BOTH = ("fsdp", "ctx")


def per_device(
    tokens, block_index, positions, cotangent, norm_attn, w_q, b_q, w_k, b_k, w_v, b_v, w_o,
    norm_mlp, w_gate, w_up, w_down,
):
    f, c = lax.axis_index("fsdp"), lax.axis_index("ctx")
    core, zh = c % 2, (c // 2) % 2
    z = 2 * zh + f
    sub = 2 * zh + core
    field, cot = tokens[0], cotangent[0]
    order = block_index[0]
    owned = lax.dynamic_slice_in_dim(order, 4 * (c // 2), 4, 0)
    gain_attn = norm_attn.astype(F32)[None]
    gain_mlp = norm_mlp.astype(F32)[None]

    freq = THETA ** (-(jnp.arange(HD // 2, dtype=F32) * 2.0 / HD))
    angle = positions[0].astype(F32)[:, None] * freq[None, :]
    cosine, sine = jnp.cos(angle), jnp.sin(angle)
    table = jnp.concatenate([cosine, cosine, sine, sine], -1)

    def core_columns(array):
        half = array.shape[-1] // 2
        return jnp.where(core == 0, array[..., :half], array[..., half:])

    zeros = jnp.zeros((HALF, 64), BF16)
    weight = jnp.concatenate(
        [core_columns(w_q), core_columns(w_k), core_columns(w_v), zeros], axis=1
    )
    bias = jnp.concatenate(
        [core_columns(b_q), core_columns(b_k), core_columns(b_v), zeros[0]], axis=0
    ).astype(F32)[None]

    normed_all, table_all, weight_all, queries, kv_a, kv_b, cot_all = remote_call(
        enter_kernel,
        0,
        [
            shape((2, 128, D), BF16),
            shape((2, 128, 128), F32),
            shape((D, PADDED), BF16),
            shape((256, HALF), BF16),
            shape((4, 4, 2, 128, 128), BF16),
            shape((4, 4, 2, 128, 128), BF16),
            shape((4, 2, 128, D), BF16),
        ],
        32,
        [],
        field, gain_attn, table, weight, bias, cot,
    )

    def window(s):
        start = jnp.minimum((19 * s) // 4, 32) * 128
        return start, padded_columns(SLICE * s - start)

    def slice_of(array, s):
        start, pick = window(s)
        part = lax.dynamic_slice(array, (0, start), (array.shape[0], 768))
        return dot(part, pick).astype(BF16)

    z_up, z_down = (z + 1) % 4, (z + 3) % 4
    s_own = 4 * f + sub
    s_up = 4 * (z_up % 2) + 2 * (z_up // 2) + core
    s_down = 4 * (z_down % 2) + 2 * (z_down // 2) + core
    to_up = permutation(lambda x, y, z, core: (x, y, (z + 1) % 4, core))
    to_down = permutation(lambda x, y, z, core: (x, y, (z + 3) % 4, core))

    def from_neighbours(own, for_up, for_down):
        late = lax.ppermute(for_up, BOTH, to_up)
        early = lax.ppermute(for_down, BOTH, to_down)
        theirs = jnp.concatenate([early, late], axis=0)
        return jnp.where(
            f == 0, jnp.concatenate([own, theirs], 0), jnp.concatenate([theirs, own], 0)
        )

    out_weight = from_neighbours(w_o, w_o[224:], w_o[:224])
    gate_up_own = jnp.concatenate([slice_of(w_gate, s_own), slice_of(w_up, s_own)], 1)
    gate_up = from_neighbours(
        gate_up_own,
        jnp.concatenate([slice_of(w_gate[224:], s_up), slice_of(w_up[224:], s_up)], 1),
        jnp.concatenate([slice_of(w_gate[:224], s_down), slice_of(w_up[:224], s_down)], 1),
    )
    down_rows = lax.dynamic_slice_in_dim(w_down, SLICE * sub, SLICE, 0)
    down_weight = dot(padded_columns(0)[:SLICE], down_rows, ((0,), (0,))).astype(BF16)

    per_head = queries.reshape(4, 64, 7, 64)
    zero_t = jnp.zeros((4, 64, HALF), BF16)
    query_t = per_head.transpose(0, 3, 2, 1).reshape(4, 64, HALF)
    query = per_head.transpose(0, 2, 1, 3).reshape(4, HALF, 64)
    query_t = jnp.concatenate([query_t, zero_t], 1)
    zero = jnp.zeros((4, HALF, 64), BF16)
    query = jnp.concatenate([query, zero], 2)
    kv_a, kv_b = kv_a.reshape(32, 128, 128), kv_b.reshape(32, 128, 128)
    natural = [pltpu.VMEM((8192, 128), BF16), pltpu.VMEM((32, 128, CHUNK), BF16)]
    out_t, lse = local_call(
        attend_kernel,
        [shape((4, 64, HALF), F32), shape((4, 1, HALF), F32)],
        natural + [pltpu.VMEM((64, HALF), F32)],
        2,
        8 << 30,
        order, owned, kv_a, kv_b, query_t,
    )
    mixed = out_t.reshape(4, 64, 7, 64).transpose(0, 3, 2, 1).reshape(256, HALF).astype(BF16)

    mixed_all, hidden, normed2 = remote_call(
        hidden_kernel,
        1,
        [shape((2, 256, HALF), BF16), shape((128, D), F32), shape((4, 2, 128, D), BF16)],
        12,
        [],
        mixed, out_weight, field, gain_mlp,
    )

    normed2 = normed2.reshape(1024, D)
    cots = cot_all.reshape(1024, D)
    owners = owner_columns()
    gate = dot(normed2, gate_up[:, :PADDED])
    up = dot(normed2, gate_up[:, PADDED:])
    sigmoid = jax.nn.sigmoid(gate)
    inner = (gate * sigmoid * up).astype(BF16)
    out_part = dot(inner, down_weight).astype(BF16)
    grad_inner = dot(cots, down_weight, ((1,), (1,)))
    grad_gate = (grad_inner * up * sigmoid * (1.0 + gate * (1.0 - sigmoid))).astype(BF16)
    grad_up = (grad_inner * (gate * sigmoid)).astype(BF16)
    grad_part = (
        dot(grad_gate, gate_up[:, :PADDED], ((1,), (1,)))
        + dot(grad_up, gate_up[:, PADDED:], ((1,), (1,)))
    ).astype(BF16)
    spread2 = dot(normed2, owners).astype(BF16)
    rows0 = ((0,), (0,))
    grad_gate_part = dot(spread2, grad_gate, rows0).astype(BF16)
    grad_up_part = dot(spread2, grad_up, rows0).astype(BF16)
    grad_down_part = dot(inner, cots, rows0).astype(BF16)

    def pair(dims, dtype=BF16, other=None):
        return [pltpu.VMEM((3,) + dims, dtype), pltpu.VMEM((3,) + (other or dims), dtype)]

    block = [pltpu.VMEM((4, 128, D), BF16)] * 2 + pair((64, D))
    mixed_out, grad_hidden, branch_all, grad_gain_mlp = remote_call(
        branch_kernel,
        2,
        [shape((128, D), BF16), shape((128, D), F32), shape((2, 128, D), BF16), shape((1, D), F32)],
        16,
        block + block + [pltpu.VMEM((128, D), F32)],
        out_part.reshape(4, 2, 128, D), grad_part.reshape(4, 2, 128, D), hidden, cot, gain_mlp,
    )

    rows_all, down_rows_out = remote_call(
        mlp_grads_kernel,
        3,
        [shape((8, 8, 2 * PADDED), F32), shape((40, D), F32)],
        48,
        [
            pltpu.VMEM((4, 64, PADDED), BF16),
            pltpu.VMEM((4, 64, PADDED), BF16),
            pltpu.VMEM((4, 40, D), F32),
            pltpu.VMEM((8, 8, 2 * PADDED), F32),
        ]
        + pair((2, 64, PADDED)) + pair((32, PADDED))
        + pair((2, 64, PADDED)) + pair((32, PADDED))
        + pair((80, D)) + pair((24, D), F32, (16, D)),
        grad_gate_part.reshape(4, 4, 64, PADDED),
        grad_up_part.reshape(4, 4, 64, PADDED),
        grad_down_part.reshape(4, 160, D),
    )
    down_owner = permutation(
        lambda x, y, z, core: (2 * (z // 2) + core, x, 2 * (y // 2) + z % 2, y % 2)
    )
    grad_w_down = lax.ppermute(down_rows_out, BOTH, down_owner)[:38]

    def unpadded(rows):
        parts = rows.reshape(2, 2, 2, 8, 16, 40)[:, :, :, :7, :, :38]
        return parts.transpose(3, 1, 0, 2, 4, 5).reshape(7, FF)

    grad_w_gate = unpadded(rows_all[:, :, :PADDED])
    grad_w_up = unpadded(rows_all[:, :, PADDED:])

    branch = branch_all.reshape(256, D)
    w_o_core = lax.dynamic_slice_in_dim(out_weight, core * HALF, HALF, 0)
    grad_mixed = dot(branch, w_o_core, ((1,), (1,))).astype(BF16).reshape(4, 64, 7, 64)
    grad_t = grad_mixed.transpose(0, 3, 2, 1).reshape(4, 64, HALF)
    grad = grad_mixed.transpose(0, 2, 1, 3).reshape(4, HALF, 64)
    grad_query_t, part_a, part_b = local_call(
        attend_back_kernel,
        [shape((4, 64, HALF), F32), shape((32, 128, 128), BF16), shape((32, 128, 128), BF16)],
        natural + [pltpu.VMEM((8192, 128), F32), pltpu.VMEM((64, HALF), F32)],
        2,
        24 << 30,
        order, owned, kv_a, kv_b, query_t, query,
        jnp.concatenate([zero_t, grad_t], 1), jnp.concatenate([zero, grad], 2), out_t, lse,
    )
    chips = (4, 4, 2, 128, 128)
    (grad_kv,) = remote_call(
        kv_reduce_kernel,
        4,
        [shape((256, 128), F32)],
        32,
        [pltpu.VMEM((4, 2, 128, 128), BF16)] * 2
        + [pltpu.VMEM((2, 128, 128), F32)] * 2
        + (pair((2, 2, 128, 128)) + pair((128, 128))) * 2
        + [pltpu.VMEM((128, 128), F32)] * 2,
        part_a.reshape(chips), part_b.reshape(chips),
    )

    both = table_all.reshape(256, 128)
    cosine, sine = both[:, None, :64], both[:, None, 64:]
    grad_query = grad_query_t.reshape(4, 64, 7, 64).transpose(0, 3, 2, 1).reshape(256, 7, 64)
    lin_grads = jnp.concatenate([grad_query * HD**-0.5, grad_kv[:, None, :64]], 1)
    scaled = lin_grads * sine
    lin_grads = lin_grads * cosine + jnp.concatenate([scaled[..., 32:], -scaled[..., :32]], -1)
    lin_grads = jnp.concatenate(
        [lin_grads.reshape(256, 512), grad_kv[:, 64:], jnp.zeros((256, 64), F32)], 1
    ).astype(BF16)
    normed = normed_all.reshape(256, D)
    spread1 = dot(normed, owners).astype(BF16)
    part_q = dot(spread1, lin_grads, rows0).astype(BF16)
    merged = jnp.concatenate([mixed_all[0], mixed_all[1]], 1)
    spread_o = dot(merged, owners).astype(BF16)
    part_o = dot(spread_o, core_columns(branch), rows0).astype(BF16)
    grad_normed = dot(lin_grads, weight_all, ((1,), (1,)))
    sums = jnp.sum(lin_grads.astype(F32), axis=0)

    def placed(values):
        empty = jnp.zeros_like(values)
        return jnp.where(
            core == 0, jnp.concatenate([values, empty]), jnp.concatenate([empty, values])
        )

    vector = jnp.concatenate(
        [
            jnp.zeros((D,), F32),
            grad_gain_mlp[0],
            placed(sums[:HALF]),
            placed(sums[HALF:512]),
            placed(sums[512:576]),
            jnp.zeros((128,), F32),
        ]
    )[None]

    def three(columns):
        return (
            pair((2, 4, 16, columns)) + pair((2, 16, columns)) + pair((8, columns), F32)
        )

    d_tokens, rows_q, rows_o, vector = remote_call(
        leave_kernel,
        5,
        [
            shape((128, D), F32),
            shape((2, 8, PADDED), F32),
            shape((2, 8, HALF), F32),
            shape((1, 3072), F32),
        ],
        52,
        [
            pltpu.VMEM((128, D), F32),
            pltpu.VMEM((4, 4, 16, PADDED), BF16),
            pltpu.VMEM((4, 16, PADDED), F32),
            pltpu.VMEM((2, 8, PADDED), F32),
            pltpu.VMEM((4, 4, 16, HALF), BF16),
            pltpu.VMEM((4, 16, HALF), F32),
            pltpu.VMEM((2, 8, HALF), F32),
        ]
        + three(PADDED)
        + three(HALF)
        + [pltpu.VMEM((5, 1, 3072), F32), pltpu.VMEM((10, 1, 3072), F32)],
        part_q.reshape(4, 4, 4, 16, PADDED), part_o.reshape(4, 4, 4, 16, HALF),
        grad_normed.reshape(2, 128, D), grad_hidden, field, gain_attn, vector,
    )

    def both_cores(low, high):
        return jnp.concatenate([rows_q[0, :7, low:high], rows_q[1, :7, low:high]], 1)

    sums = vector[0]
    return (
        mixed_out[None],
        d_tokens[None],
        both_cores(0, HALF),
        both_cores(HALF, 512),
        both_cores(512, 576),
        jnp.concatenate([rows_o[0, :7], rows_o[1, :7]], 1),
        grad_w_gate,
        grad_w_up,
        grad_w_down,
        sums[:D],
        sums[D : 2 * D],
        sums[2 * D : 3 * D],
        sums[3 * D : 3 * D + 128],
        sums[3 * D + 128 : 3 * D + 256],
    )


def solution(mesh):
    rows, flat = P("fsdp", None), P(("fsdp", "ctx"), None)
    field = P("fsdp", "ctx", None)
    return jax.shard_map(
        per_device,
        mesh=mesh,
        in_specs=(
            field, rows, P("fsdp", "ctx"), field, P(), rows, P(), rows, P(), rows, P(), rows, P(),
            rows, rows, rows,
        ),
        out_specs=(field, field) + (flat,) * 7 + (P(),) * 5,
        check_vma=False,
    )
```

```python
import functools

import jax
import jax.numpy as jnp
import numpy as np
from jax import lax
from jax.experimental import pallas as pl
from jax.experimental.pallas import tpu as pltpu
from jax.sharding import PartitionSpec as P

D = 896
H = 14
HD = 64
HALF = 448
FF = 4864
SLICE = 608
PADDED = 640
CHUNK = 256
EPSILON = 1e-06
THETA = 1000000.0
MASKED = -1e30
MESH = pl.DeviceIdType.MESH
F32 = jnp.float32
BF16 = jnp.bfloat16
VMEM_LIMIT = 56 * 1024 * 1024


def own_place():
    f, c = lax.axis_index("fsdp"), lax.axis_index("ctx")
    zh = lax.rem(lax.div(c, 2), 2)
    return (lax.div(c, 16), lax.rem(lax.div(c, 4), 4), zh * 2 + f, lax.rem(c, 2))


def device(place):
    x, y, z, core = place
    return (lax.rem(z, 2), (x * 4 + y) * 4 + 2 * lax.div(z, 2) + core)


def turned(value, step):
    return lax.rem(value + (step + 4), 4)


def shifted(place, axis, step):
    moved = list(place)
    moved[axis] = turned(place[axis], step)
    return tuple(moved)


def partner(place):
    return place[:3] + (1 - place[3],)


def greet(places):
    barrier = pltpu.get_barrier_semaphore()
    for place in places:
        pl.semaphore_signal(barrier, inc=1, device_id=device(place), device_id_type=MESH)
    pl.semaphore_wait(barrier, len(places))


class Links:
    def __init__(self, send, recv):
        self.send, self.recv, self.opened = send, recv, []

    def start(self, src, dst, place):
        at = len(self.opened)
        copy = pltpu.make_async_remote_copy(
            src_ref=src,
            dst_ref=dst,
            send_sem=self.send.at[at],
            recv_sem=self.recv.at[at],
            device_id=device(place),
            device_id_type=MESH,
        )
        copy.start()
        self.opened.append(copy)
        return copy

    def close(self):
        for copy in self.opened:
            copy.wait_send()


def ring_gather(links, slot, half, place, axis):
    me = place[axis]
    right, left = shifted(place, axis, 1), shifted(place, axis, -1)
    first = links.start(slot(me), slot(me), right)
    second = links.start(slot(me), slot(me), left)
    yield
    before, after = turned(me, -1), turned(me, 1)
    first.wait_recv()
    third = links.start(half(before, 0), half(before, 0), right)
    yield
    second.wait_recv()
    fourth = links.start(half(after, 1), half(after, 1), left)
    yield
    third.wait_recv()
    fourth.wait_recv()


def ring_reduce(links, part, low, high, place, axis, emit):
    me = place[axis]
    right, left = shifted(place, axis, 1), shifted(place, axis, -1)
    before, after, far = turned(me, -1), turned(me, 1), turned(me, 2)
    first = links.start(part(far, 0), low.at[0], right)
    second = links.start(part(far, 1), high.at[0], left)
    yield
    third = links.start(part(after, 1), high.at[1], right)
    yield
    fourth = links.start(part(before, 0), low.at[1], left)
    yield
    first.wait_recv()
    low[0] = (low[0].astype(F32) + part(after, 0)[...].astype(F32)).astype(low.dtype)
    fifth = links.start(low.at[0], low.at[2], right)
    second.wait_recv()
    high[0] = (high[0].astype(F32) + part(before, 1)[...].astype(F32)).astype(high.dtype)
    sixth = links.start(high.at[0], high.at[2], left)
    yield
    fourth.wait_recv()
    fifth.wait_recv()
    emit(0, part(me, 0)[...].astype(F32) + low[1].astype(F32) + low[2].astype(F32))
    third.wait_recv()
    sixth.wait_recv()
    emit(1, part(me, 1)[...].astype(F32) + high[1].astype(F32) + high[2].astype(F32))


def in_turn(*streams):
    waiting = list(streams)
    while waiting:
        still = []
        for stream in waiting:
            try:
                next(stream)
            except StopIteration:
                continue
            still.append(stream)
        waiting = still


def local_norm(field, gain):
    inverse = lax.rsqrt(jnp.mean(field * field, axis=-1, keepdims=True) + EPSILON)
    return field * inverse * gain, inverse


def norm_backward(field, inverse, gain, grad):
    scaled = grad * gain
    grad_gain = jnp.sum(grad * field * inverse, axis=0, keepdims=True)
    mean = jnp.mean(scaled * field, axis=-1, keepdims=True)
    return inverse * scaled - field * (inverse * inverse * inverse) * mean, grad_gain


def dot(left, right, contract=((1,), (0,))):
    return lax.dot_general(left, right, (contract, ((), ())), preferred_element_type=F32)


def whole(count):
    return [pl.BlockSpec(memory_space=pltpu.VMEM)] * count


def shape(dims, dtype):
    return jax.ShapeDtypeStruct(dims, dtype)


def remote_call(kernel, collective_id, outs, copies, scratch, *args, far=0):
    return pl.pallas_call(
        kernel,
        out_shape=outs,
        in_specs=whole(len(args) - far) + [pl.BlockSpec(memory_space=pl.ANY)] * far,
        out_specs=whole(len(outs)),
        scratch_shapes=list(scratch)
        + [pltpu.SemaphoreType.DMA((copies,)), pltpu.SemaphoreType.DMA((copies,))],
        compiler_params=pltpu.CompilerParams(
            collective_id=collective_id, has_side_effects=True, vmem_limit_bytes=VMEM_LIMIT
        ),
    )(*args)


def enter_kernel(
    tokens, gain, table, weight, bias, cot, row_pick, col_pick, w_gate, w_up, w_down,
    normed_all, table_all, weight_all, queries, kv_a, kv_b, cot_all, own_units, up_units, down_units, down_rows,
    own_window, up_window, down_window, tall_window, fetched, send, recv,
):
    place = own_place()
    x, y, z, core = place
    f, zh = lax.rem(z, 2), lax.div(z, 2)
    other, up, down, far = partner(place), shifted(place, 2, 1), shifted(place, 2, -1), shifted(place, 2, 2)
    fetches = []

    def fetch(src, dst):
        copy = pltpu.make_async_copy(src, dst, fetched.at[len(fetches)])
        copy.start()
        fetches.append(copy)

    def offset(at):
        part = 4 * lax.rem(at[2], 2) + 2 * lax.div(at[2], 2) + at[3]
        start = jnp.minimum(lax.div(19 * part, 4), 32) * 128
        return start, SLICE * part - start

    windows = ((own_window, place, 0, HALF), (up_window, up, 224, 224), (down_window, down, 0, 224))
    for window, at, row, rows in windows:
        columns = pl.ds(pl.multiple_of(offset(at)[0], 128), 768)
        for which, array in enumerate((w_gate, w_up)):
            fetch(array.at[pl.ds(row, rows), columns], window.at[which])
    sub = 2 * zh + core
    fetch(w_down.at[pl.ds(pl.multiple_of(sub * SLICE, 16), SLICE)], tall_window)
    greet(
        [other, up, down, far]
        + [shifted(place, axis, step) for axis in (0, 1) for step in (1, -1)]
    )
    links = Links(send, recv)
    base = pl.multiple_of(f * HALF, HALF)
    w_down_copy = links.start(weight.at[pl.ds(0, 224)], weight_all.at[pl.ds(base, 224)], down)
    w_up_copy = links.start(weight.at[pl.ds(224, 224)], weight_all.at[pl.ds(base + 224, 224)], up)
    normed, _ = local_norm(tokens[...].astype(F32), gain[...])
    normed_all[core] = normed.astype(BF16)
    n_copy = links.start(normed_all.at[core], normed_all.at[core], other)
    table_all[core] = table[...]
    t_copy = links.start(table_all.at[core], table_all.at[core], other)
    cot_all[z, core] = cot[...]
    c_copy = links.start(cot_all.at[z, core], cot_all.at[z, core], other)
    weight_all[pl.ds(base, HALF)] = weight[...]
    for copy in fetches:
        copy.wait()
    n_copy.wait_recv()
    t_copy.wait_recv()
    w_down_copy.wait_recv()
    w_up_copy.wait_recv()
    lin = dot(normed_all[...].reshape(256, D), weight_all[...]) + bias[...]
    turn = lin[:, :512]
    lane = lax.broadcasted_iota(jnp.int32, (256, 512), 1)
    swapped = jnp.where(lax.rem(lane, 64) < 32, -pltpu.roll(turn, 480, 1), pltpu.roll(turn, 32, 1))
    both = table_all[...].reshape(256, 128)
    cosine = jnp.concatenate([both[:, :64]] * 8, axis=1)
    sine = jnp.concatenate([both[:, 64:]] * 8, axis=1)
    rotated = turn * cosine + swapped * sine
    kv = jnp.concatenate([rotated[:, HALF:512], lin[:, 512:576]], axis=1).astype(BF16)
    kv_a[x, y, zh] = kv[:128]
    kv_b[x, y, zh] = kv[128:]
    a_far = links.start(kv_a.at[x, y, zh], kv_a.at[x, y, zh], far)
    b_far = links.start(kv_b.at[x, y, zh], kv_b.at[x, y, zh], far)
    queries[...] = (rotated[:, :HALF] * HD**-0.5).astype(BF16)

    def stream_a():
        a_far.wait_recv()
        yield from ring_gather(
            links, lambda k: kv_a.at[x, k], lambda k, h: kv_a.at[x, k, h], place, 1
        )
        yield from ring_gather(
            links, lambda k: kv_a.at[k], lambda k, h: kv_a.at[k, pl.ds(2 * h, 2)], place, 0
        )

    def stream_b():
        b_far.wait_recv()
        yield from ring_gather(
            links, lambda k: kv_b.at[k, y], lambda k, h: kv_b.at[k, y, h], place, 0
        )
        yield from ring_gather(
            links,
            lambda k: kv_b.at[pl.ds(0, 4), k],
            lambda k, h: kv_b.at[pl.ds(2 * h, 2), k],
            place,
            1,
        )

    def units():
        for (window, at, _, rows), out in zip(windows, (own_units, up_units, down_units)):
            line = lax.broadcasted_iota(jnp.int32, (768, PADDED), 0) - offset(at)[1]
            pick = (line == row_pick[...]).astype(F32).astype(BF16)
            for which in range(2):
                out[:, PADDED * which : PADDED * (which + 1)] = dot(window[which], pick).astype(BF16)
            yield
        line = lax.broadcasted_iota(jnp.int32, (PADDED, SLICE), 1)
        pick = (line == col_pick[...]).astype(F32).astype(BF16)
        down_rows[...] = dot(pick, tall_window[...]).astype(BF16)

    in_turn(stream_a(), stream_b(), shared_gather(links, cot_all, place, c_copy), units())
    links.close()


def shared_gather(links, blocks, place, own_copy):
    z, core = place[2], place[3]
    other = partner(place)
    copies = [own_copy]
    ring = ring_gather(
        links,
        lambda k: blocks.at[k, core],
        lambda k, h: blocks.at[k, core, pl.ds(64 * h, 64)],
        place,
        2,
    )
    next(ring)
    yield
    next(ring)
    before = turned(z, -1)
    copies.append(links.start(blocks.at[before, core], blocks.at[before, core], other))
    yield
    next(ring)
    after = turned(z, 1)
    copies.append(links.start(blocks.at[after, core], blocks.at[after, core], other))
    yield
    for _ in ring:
        yield
    last = turned(z, 2)
    copies.append(links.start(blocks.at[last, core], blocks.at[last, core], other))
    yield
    for copy in copies:
        copy.wait_recv()


def feed_kernel(
    mixed, o_own, o_early, o_late, u_own, u_early, u_late, w_down, cot_all, tokens, gain, owners, col_pick,
    mixed_all, o_core, mixed_out, grad_hidden, branch_all, grad_gain, gate_out, up_out, down_out,
    w_o, w_units, hidden, normed_all, spread_t, inner_t, grad_gates, grad_ups,
    out_part, out_arrived, out_paired, out_low, out_high,
    grad_part, grad_arrived, grad_paired, grad_low, grad_high, grad_sum,
    gate, up, down, *rest,
):
    (
        mid_gate, mid_up, mid_down, end, rows_all,
        g_low1, g_high1, g_low2, g_high2, u_low1, u_high1, u_low2, u_high2,
        d_low1, d_high1, d_low2, d_high2, send, recv,
    ) = rest
    place = own_place()
    x, y, z, core = place
    f = lax.rem(z, 2)
    other = partner(place)
    mine = z * 2 + core
    others = []
    for step in range(1, 8):
        at = lax.rem(mine + step, 8)
        others.append((x, y, lax.div(at, 2), lax.rem(at, 2)))
    greet(others + [shifted(place, axis, step) for axis in (0, 1) for step in (1, -1)])
    links = Links(send, recv)
    copy = links.start(mixed, mixed_all.at[core], other)
    mixed_all[core] = mixed[...]
    own_base = pl.multiple_of(f * HALF, HALF)
    base = pl.multiple_of((1 - f) * HALF, HALF)
    w_o[pl.ds(own_base, HALF)] = o_own[...]
    w_o[pl.ds(base, 224)] = o_early[...]
    w_o[pl.ds(base + 224, 224)] = o_late[...]
    copy.wait_recv()
    rows = pl.ds(pl.multiple_of(core * 128, 128), 128)
    field = tokens[...].astype(F32) + (
        dot(mixed_all[0, rows], w_o[:HALF]) + dot(mixed_all[1, rows], w_o[HALF:])
    )
    hidden[...] = field
    normed, _ = local_norm(field, gain[...])
    normed_all[z, core] = normed.astype(BF16)
    own = links.start(normed_all.at[z, core], normed_all.at[z, core], other)

    def assemble():
        w_units[pl.ds(own_base, HALF)] = u_own[...]
        yield
        w_units[pl.ds(base, 224)] = u_early[...]
        w_units[pl.ds(base + 224, 224)] = u_late[...]
        o_core[...] = w_o[pl.ds(pl.multiple_of(core * HALF, HALF), HALF)]

    in_turn(shared_gather(links, normed_all, place, own), assemble())

    before, after, far = turned(z, -1), turned(z, 1), turned(z, 2)
    both = (
        (out_part, out_arrived, out_paired), (grad_part, grad_arrived, grad_paired),
    )

    def tile(k):
        n = normed_all[k].reshape(256, D)
        c = cot_all[k].reshape(256, D)
        g = dot(n, w_units[:, :PADDED])
        u = dot(n, w_units[:, PADDED:])
        s = 1.0 / (1.0 + jnp.exp(-g))
        silu = g * s
        inner = silu * u
        low = inner.astype(BF16)
        out_part[k] = dot(low, w_down[...]).astype(BF16).reshape(2, 128, D)
        columns = pl.ds(pl.multiple_of(k * 256, 256), 256)
        inner_t[:, columns] = low.T
        gi = dot(c, w_down[...], ((1,), (1,)))
        gg = (gi * u * s * (1.0 + g * (1.0 - s))).astype(BF16)
        gu = (gi * silu).astype(BF16)
        grad_gates[columns] = gg
        grad_ups[columns] = gu
        grad_part[k] = (
            dot(gg, w_units[:, :PADDED], ((1,), (1,))) + dot(gu, w_units[:, PADDED:], ((1,), (1,)))
        ).astype(BF16).reshape(2, 128, D)
        return [links.start(part.at[k, 1 - core], come.at[k], other) for part, come, _ in both]

    def pair_up(k, copies):
        for trip, (part, come, paired) in zip(copies, both):
            trip.wait_recv()
            paired[k] = (come[k].astype(F32) + part[k, core].astype(F32)).astype(BF16)

    def emit_out(h, value):
        at = pl.ds(64 * h, 64)
        mixed_out[at] = (hidden[at] + value).astype(BF16)

    def emit_grad(h, value):
        grad_sum[pl.ds(64 * h, 64)] = value

    reduces = [
        ring_reduce(
            links, lambda k, h, p=paired: p.at[k, pl.ds(64 * h, 64)], low, high, place, 2, emit
        )
        for paired, low, high, emit in (
            (grad_paired, grad_low, grad_high, emit_grad),
            (out_paired, out_low, out_high, emit_out),
        )
    ]

    def advance():
        for stream in reduces:
            next(stream, None)

    trips = tile(far)
    pair_up(far, trips)
    advance()
    trips = tile(after)
    pair_up(after, trips)
    advance()
    trips = tile(before)
    pair_up(before, trips)
    advance()
    trips = tile(z)
    advance()
    pair_up(z, trips)

    @pl.loop(0, 4)
    def _(k):
        columns = pl.ds(pl.multiple_of(k * 256, 256), 256)
        spread_t[:, columns] = dot(
            owners[...], normed_all[k].reshape(256, D), ((1,), (1,))
        ).astype(BF16)

    @pl.loop(0, 4)
    def _(k):
        lines = spread_t[pl.ds(pl.multiple_of(k * 256, 256), 256)]
        gate[k] = dot(lines, grad_gates[...]).astype(BF16).reshape(4, 64, PADDED)
        up[k] = dot(lines, grad_ups[...]).astype(BF16).reshape(4, 64, PADDED)
        lines = inner_t[pl.ds(pl.multiple_of(k * 160, 160), 160)]
        down[k] = dot(lines, cot_all[...].reshape(1024, D)).astype(BF16)

    def wide(part, mid, order, low1, high1, low2, high2, column):
        def put_mid(h, value):
            mid[pl.ds(2 * h, 2)] = value.astype(BF16)

        def put_end(h, value):
            end[pl.ds(4 * h, 4), :, pl.ds(column, PADDED)] = value.reshape(4, 8, PADDED)

        if order == 0:
            first = lambda k, h: part.at[k, pl.ds(2 * h, 2)]
        else:
            first = lambda k, h: part.at[pl.ds(2 * h, 2), k]
        yield from ring_reduce(links, first, low1, high1, place, order, put_mid)
        yield from ring_reduce(
            links, lambda k, h: mid.at[k, pl.ds(32 * h, 32)], low2, high2, place, 1 - order, put_end
        )

    def tall():
        def put_mid(h, value):
            mid_down[pl.ds(2 * h, 2)] = value.reshape(2, 40, D)

        def put_end(h, value):
            down_out[pl.ds(24 * h, 24 - 8 * h)] = value

        yield from ring_reduce(
            links, lambda k, h: down.at[k, pl.ds(80 * h, 80)], d_low1, d_high1, place, 0, put_mid
        )
        yield from ring_reduce(
            links,
            lambda k, h: mid_down.at[k, pl.ds(24 * h, 24 - 8 * h)],
            d_low2,
            d_high2,
            place,
            1,
            put_end,
        )

    def branch():
        for _ in range(8):
            advance()
        field = hidden[...]
        _, inverse = local_norm(field, gain[...])
        through, gains = norm_backward(field, inverse, gain[...], grad_sum[...])
        grad_gain[...] = gains
        total = cot_all[z, core].astype(F32) + through
        grad_hidden[...] = total
        branch_all[core] = total.astype(BF16)
        trip = links.start(branch_all.at[core], branch_all.at[core], other)
        yield
        trip.wait_recv()

    in_turn(
        wide(gate, mid_gate, 0, g_low1, g_high1, g_low2, g_high2, 0),
        wide(up, mid_up, 1, u_low1, u_high1, u_low2, u_high2, PADDED),
        tall(),
        branch(),
    )
    copies = []
    for to in others:
        copies.append(links.start(end.at[to[2] * 2 + to[3]], rows_all.at[mine], to))
    rows_all[mine] = end[mine]
    line = lax.broadcasted_iota(jnp.int32, (PADDED, SLICE), 1)
    pick = (line == col_pick[...]).astype(F32).astype(BF16)
    for copy in copies:
        copy.wait_recv()
    for which, out in enumerate((gate_out, up_out)):
        values = rows_all[:, :, PADDED * which : PADDED * (which + 1)].reshape(64, PADDED)
        top = values.astype(BF16)
        below = (values - top.astype(F32)).astype(BF16)
        units = dot(top, pick) + dot(below, pick)
        for at in range(8):
            part = 4 * (at // 2 % 2) + 2 * (at // 4) + at % 2
            out[:, SLICE * part : SLICE * (part + 1)] = units[8 * at : 8 * at + 7]
    links.close()


def finish_kernel(
    kv_part_a, kv_part_b, grad_query, table_all, weight_all, normed_all, mixed_all, branch_half,
    owners, owners_half, grad_hidden, tokens, gain, gain_mlp_grad,
    d_tokens, wq_out, wk_out, wv_out, wo_out, vector_out,
    grad_kv, kv_mid_a, kv_mid_b, kv_end_a, kv_end_b, part_q, part_o, grad_normed, *rest,
):
    slots, rest = rest[:10], rest[10:]
    (
        half_sum, mid_q1, mid_q2, end_q, rows_q, mid_o1, mid_o2, end_o, rows_o,
        q_low1, q_high1, q_low2, q_high2, q_low3, q_high3,
        o_low1, o_high1, o_low2, o_high2, o_low3, o_high3,
        vec_now, vec_in, send, recv,
    ) = rest
    place = own_place()
    x, y, z, core = place
    zh = lax.div(z, 2)
    far = shifted(place, 2, 2)
    other = partner(place)
    greet([other] + [shifted(place, axis, step) for axis in (0, 1, 2) for step in (1, -1, 2)])
    links = Links(send, recv)

    def kv_stream(part, mid, end, order, low1, high1, low2, high2, landing, base):
        def put_mid(h, value):
            mid[pl.ds(2 * h, 2)] = value.astype(BF16)

        def put_end(h, value):
            end[h] = value

        if order == 0:
            first = lambda k, h: part.at[k, pl.ds(2 * h, 2)]
        else:
            first = lambda k, h: part.at[pl.ds(2 * h, 2), k]
        yield from ring_reduce(links, first, low1, high1, place, order, put_mid)
        yield from ring_reduce(
            links, lambda k, h: mid.at[k, h], low2, high2, place, 1 - order, put_end
        )
        copy = links.start(end.at[1 - zh], landing, far)
        yield
        copy.wait_recv()
        grad_kv[pl.ds(base, 128)] = end[zh] + landing[...]

    def grads(part, mid1, mid2, end, order, low1, high1, low2, high2, low3, high3, rows):
        def put1(h, value):
            mid1[pl.ds(2 * h, 2)] = value.astype(BF16)

        def put2(h, value):
            mid2[pl.ds(2 * h, 2)] = value

        def put3(h, value):
            end[h] = value

        if order == 0:
            first = lambda k, h: part.at[k, pl.ds(2 * h, 2)]
        else:
            first = lambda k, h: part.at[pl.ds(2 * h, 2), k]
        yield from ring_reduce(links, first, low1, high1, place, order, put1)
        yield from ring_reduce(
            links, lambda k, h: mid1.at[k, pl.ds(2 * h, 2)], low2, high2, place, 1 - order, put2
        )
        yield from ring_reduce(
            links, lambda k, h: mid2.at[k, pl.ds(8 * h, 8)], low3, high3, place, 2, put3
        )
        last = links.start(end.at[1 - core], rows.at[core], other)
        rows[core] = end[core]
        yield
        last.wait_recv()

    kv_streams = [
        kv_stream(kv_part_a, kv_mid_a, kv_end_a, 0, *slots[0:4], slots[8], 0),
        kv_stream(kv_part_b, kv_mid_b, kv_end_b, 1, *slots[4:8], slots[9], 128),
    ]
    for _ in range(3):
        for stream in kv_streams:
            next(stream)
    spread_o = (
        dot(owners_half[0], mixed_all[0], ((1,), (1,))) + dot(owners_half[1], mixed_all[1], ((1,), (1,)))
    ).astype(BF16)
    part_o[...] = dot(spread_o, branch_half[...]).astype(BF16).reshape(4, 4, 4, 16, HALF)
    spread_n = dot(owners[...], normed_all[...].reshape(256, D), ((1,), (1,))).astype(BF16)
    o_stream = grads(
        part_o, mid_o1, mid_o2, end_o, 1, o_low1, o_high1, o_low2, o_high2, o_low3, o_high3, rows_o
    )
    in_turn(*kv_streams)
    for _ in range(3):
        next(o_stream)

    table = table_all[...].reshape(256, 128)
    cosine = jnp.concatenate([table[:, :64]] * 8, axis=1)
    sine = jnp.concatenate([table[:, 64:]] * 8, axis=1)
    turn = jnp.concatenate([grad_query[...] * HD**-0.5, grad_kv[:, :64]], axis=1)
    scaled = turn * sine
    lane = lax.broadcasted_iota(jnp.int32, (256, 512), 1)
    swapped = jnp.where(
        lax.rem(lane, 64) < 32, pltpu.roll(scaled, 480, 1), -pltpu.roll(scaled, 32, 1)
    )
    lin = jnp.concatenate(
        [turn * cosine + swapped, grad_kv[:, 64:], jnp.zeros((256, 64), F32)], axis=1
    ).astype(BF16)
    part_q[...] = dot(spread_n, lin).astype(BF16).reshape(4, 4, 4, 16, PADDED)
    q_stream = grads(
        part_q, mid_q1, mid_q2, end_q, 0, q_low1, q_high1, q_low2, q_high2, q_low3, q_high3, rows_q
    )
    for _ in range(3):
        next(q_stream)

    def sums():
        grad_normed[...] = dot(lin, weight_all[...], ((1,), (1,))).reshape(2, 128, D)
        copy = links.start(grad_normed.at[1 - core], half_sum, other)
        column = jnp.sum(lin.astype(F32), axis=0, keepdims=True)

        def placed(values):
            empty = jnp.zeros_like(values)
            return jnp.where(
                core == 0,
                jnp.concatenate([values, empty], axis=1),
                jnp.concatenate([empty, values], axis=1),
            )

        biases = [placed(column[:, low:high]) for low, high in ((0, HALF), (HALF, 512), (512, 576))]
        yield
        copy.wait_recv()
        grad = grad_normed[core] + half_sum[...]
        field = tokens[...].astype(F32)
        _, inverse = local_norm(field, gain[...])
        through, gains = norm_backward(field, inverse, gain[...], grad)
        d_tokens[...] = grad_hidden[...] + through
        vec_now[0] = jnp.concatenate(
            [gains, gain_mlp_grad[...], *biases, jnp.zeros((1, 128), F32)], axis=1
        )
        trip = links.start(vec_now.at[0], vec_in.at[0], other)
        yield
        trip.wait_recv()
        vec_now[1] = vec_now[0] + vec_in[0]
        for stage, axis in enumerate((2, 1, 0)):
            trips = [
                links.start(
                    vec_now.at[1 + stage],
                    vec_in.at[1 + 3 * stage + at],
                    shifted(place, axis, step),
                )
                for at, step in enumerate((1, -1, 2))
            ]
            yield
            for trip in trips:
                trip.wait_recv()
            at = 1 + 3 * stage
            near = vec_in[at] + vec_in[at + 1]
            vec_now[2 + stage] = (vec_now[1 + stage] + vec_in[at + 2]) + near
        vector_out[...] = vec_now[4]

    in_turn(sums(), o_stream, q_stream)
    for out, rows, low, high in (
        (wq_out, rows_q, 0, HALF), (wk_out, rows_q, HALF, 512), (wv_out, rows_q, 512, 576),
        (wo_out, rows_o, 0, HALF),
    ):
        first, second = rows[0], rows[1]
        out[...] = jnp.concatenate([first[:7, low:high], second[:7, low:high]], axis=1)
    links.close()


def natural_order(order, kv_a, kv_b, kv, kv_t):
    @pl.loop(0, 32)
    def _(chip):
        for t in range(4):
            block = kv_a[chip, pl.ds(64 * t, 64)] if t < 2 else kv_b[chip, pl.ds(64 * (t - 2), 64)]
            at = pl.multiple_of(order[4 * chip + t] * 64, 64)
            kv[pl.ds(at, 64)] = block

    @pl.loop(0, 8192 // CHUNK)
    def _(c):
        kv_t[c] = kv[pl.ds(pl.multiple_of(c * CHUNK, CHUNK), CHUNK)].T


def allowed_at(c, base):
    key = c * CHUNK + lax.broadcasted_iota(jnp.int32, (CHUNK, HALF), 0)
    lane = lax.broadcasted_iota(jnp.int32, (CHUNK, HALF), 1)
    return key <= base + lax.rem(lane, 64)


def by_head(rows):
    return jnp.concatenate([rows[:, 64 * h : 64 * (h + 1)] for h in range(7)], axis=0)


def side_by_side(columns_t):
    stacked = columns_t.T
    return jnp.concatenate([stacked[64 * h : 64 * (h + 1)] for h in range(7)], axis=1)


def attend_kernel(order, owned, kv_a, kv_b, queries, out_t, lse, mixed, kv, kv_t, acc):
    natural_order(order, kv_a, kv_b, kv, kv_t)
    none = jnp.zeros((64, HALF), F32)
    for t in range(4):
        spot = owned[t]
        rows = by_head(queries[64 * t : 64 * (t + 1)].astype(F32))
        q_t = jnp.concatenate([rows.T, none], axis=0).astype(BF16)
        last = lax.div(spot * 64, CHUNK)
        acc[...] = jnp.zeros_like(acc)

        def step(c, carry, masked):
            top, total = carry
            scores = dot(kv[pl.ds(pl.multiple_of(c * CHUNK, CHUNK), CHUNK)], q_t)
            if masked:
                scores = jnp.where(allowed_at(c, spot * 64), scores, MASKED)
            new_top = jnp.maximum(top, jnp.max(scores, axis=0, keepdims=True))
            probs = jnp.exp(scores - new_top)
            scale = jnp.exp(top - new_top)
            total = total * scale + jnp.sum(probs, axis=0, keepdims=True)
            acc[...] = acc[...] * scale + dot(kv_t[c, pl.ds(64, 64)], probs.astype(BF16))
            return new_top, total

        start = (jnp.full((1, HALF), MASKED, F32), jnp.zeros((1, HALF), F32))
        carry = lax.fori_loop(0, last, lambda c, carry: step(c, carry, False), start)
        top, total = step(last, carry, True)
        result = acc[...] / total
        out_t[t] = result
        mixed[64 * t : 64 * (t + 1)] = side_by_side(result).astype(BF16)
        lse[t] = top + jnp.log(total)


def attend_back_kernel(
    order, owned, kv_a, kv_b, queries, branch, w_o, out_t, lse,
    grad_query, grad_a, grad_b, kv, kv_t, acc, acc_q,
):
    natural_order(order, kv_a, kv_b, kv, kv_t)
    acc[...] = jnp.zeros_like(acc)
    grad_mixed = dot(branch[...].reshape(256, D), w_o[...], ((1,), (1,)))
    none_t, none = jnp.zeros((64, HALF), F32), jnp.zeros((HALF, 64), F32)
    for t in range(4):
        spot = owned[t]
        last = lax.div(spot * 64, CHUNK)
        rows = by_head(queries[64 * t : 64 * (t + 1)].astype(F32))
        q = jnp.concatenate([rows, none], axis=1).astype(BF16)
        q_t = jnp.concatenate([rows.T, none_t], axis=0).astype(BF16)
        rows = by_head(grad_mixed[64 * t : 64 * (t + 1)].astype(BF16).astype(F32))
        g = jnp.concatenate([none, rows], axis=1).astype(BF16)
        rows_t = rows.T
        g_t = jnp.concatenate([none_t, rows_t], axis=0).astype(BF16)
        delta = jnp.sum(rows_t * out_t[t], axis=0, keepdims=True)
        norm = lse[t]
        acc_q[...] = jnp.zeros_like(acc_q)

        def step(c, masked):
            rows = pl.ds(pl.multiple_of(c * CHUNK, CHUNK), CHUNK)
            block = kv[rows]
            scores = dot(block, q_t)
            if masked:
                scores = jnp.where(allowed_at(c, spot * 64), scores, MASKED)
            probs = jnp.exp(scores - norm)
            grad_probs = dot(block, g_t)
            grad_scores = (probs * (grad_probs - delta)).astype(BF16)
            acc[rows] += dot(probs.astype(BF16), g) + dot(grad_scores, q)
            acc_q[...] += dot(kv_t[c, pl.ds(0, 64)], grad_scores)

        def body(c, carry):
            step(c, False)
            return carry

        lax.fori_loop(0, last, body, 0)
        step(last, True)
        grad_query[64 * t : 64 * (t + 1)] = side_by_side(acc_q[...])

    @pl.loop(0, 32)
    def _(chip):
        for t in range(4):
            at = pl.multiple_of(order[4 * chip + t] * 64, 64)
            block = acc[pl.ds(at, 64)].astype(BF16)
            if t < 2:
                grad_a[chip, pl.ds(64 * t, 64)] = block
            else:
                grad_b[chip, pl.ds(64 * (t - 2), 64)] = block


def local_call(kernel, outs, scratch, scalars, flops, *args):
    return pl.pallas_call(
        kernel,
        out_shape=outs,
        in_specs=[pl.BlockSpec(memory_space=pltpu.SMEM)] * scalars + whole(len(args) - scalars),
        out_specs=[pl.BlockSpec(memory_space=pltpu.VMEM)] * len(outs),
        scratch_shapes=scratch,
        compiler_params=pltpu.CompilerParams(vmem_limit_bytes=VMEM_LIMIT),
        cost_estimate=pl.CostEstimate(flops=flops, bytes_accessed=8 << 20, transcendentals=1 << 23),
    )(*args)


def padded_columns():
    col = np.arange(PADDED)
    return np.where(col % 40 < 38, col // 40 * 38 + col % 40, -(1 << 20)).astype(np.int32)


def owner_rows():
    row = np.arange(1024)
    i, core, z, y, x = row % 8, row // 8 % 2, row // 16 % 4, row // 64 % 4, row // 256
    at = 7 * (64 * (z % 2) + 16 * x + 4 * y + 2 * (z // 2) + core) + i
    pick = np.zeros((1024, D), np.float32)
    keep = i < 7
    pick[row[keep], at[keep]] = 1.0
    return pick


def index_of(x, y, z, core):
    return (z % 2) * 64 + (x * 4 + y) * 4 + 2 * (z // 2) + core


def permutation(move):
    pairs = []
    for x in range(4):
        for y in range(4):
            for z in range(4):
                for core in range(2):
                    pairs.append((index_of(x, y, z, core), index_of(*move(x, y, z, core))))
    return pairs


BOTH = ("fsdp", "ctx")


def per_device(
    tokens, block_index, positions, cotangent, norm_attn, w_q, b_q, w_k, b_k, w_v, b_v, w_o,
    norm_mlp, w_gate, w_up, w_down,
):
    f, c = lax.axis_index("fsdp"), lax.axis_index("ctx")
    core, zh = c % 2, (c // 2) % 2
    z = 2 * zh + f
    sub = 2 * zh + core
    field, cot = tokens[0], cotangent[0]
    order = block_index[0]
    owned = lax.dynamic_slice_in_dim(order, 4 * (c // 2), 4, 0)
    gain_attn = norm_attn.astype(F32)[None]
    gain_mlp = norm_mlp.astype(F32)[None]

    freq = THETA ** (-(jnp.arange(HD // 2, dtype=F32) * 2.0 / HD))
    angle = positions[0].astype(F32)[:, None] * freq[None, :]
    cosine, sine = jnp.cos(angle), jnp.sin(angle)
    table = jnp.concatenate([cosine, cosine, sine, sine], -1)

    def core_columns(array):
        half = array.shape[-1] // 2
        return jnp.where(core == 0, array[..., :half], array[..., half:])

    zeros = jnp.zeros((HALF, 64), BF16)
    weight = jnp.concatenate(
        [core_columns(w_q), core_columns(w_k), core_columns(w_v), zeros], axis=1
    )
    bias = jnp.concatenate(
        [core_columns(b_q), core_columns(b_k), core_columns(b_v), zeros[0]], axis=0
    ).astype(F32)[None]

    picked = padded_columns()
    row_pick, col_pick = jnp.asarray(picked[None]), jnp.asarray(picked[:, None])
    owners = owner_rows()
    owners_half = jnp.asarray(np.stack([owners[:, :HALF], owners[:, HALF:]]), BF16)
    owners = jnp.asarray(owners, BF16)

    (
        normed_all, table_all, weight_all, queries, kv_a, kv_b, cot_all,
        own_units, up_units, down_units, down_weight,
    ) = remote_call(
        enter_kernel,
        0,
        [
            shape((2, 128, D), BF16),
            shape((2, 128, 128), F32),
            shape((D, PADDED), BF16),
            shape((256, HALF), BF16),
            shape((4, 4, 2, 128, 128), BF16),
            shape((4, 4, 2, 128, 128), BF16),
            shape((4, 2, 128, D), BF16),
            shape((HALF, 2 * PADDED), BF16),
            shape((224, 2 * PADDED), BF16),
            shape((224, 2 * PADDED), BF16),
            shape((PADDED, D), BF16),
        ],
        32,
        [
            pltpu.VMEM((2, HALF, 768), BF16),
            pltpu.VMEM((2, 224, 768), BF16),
            pltpu.VMEM((2, 224, 768), BF16),
            pltpu.VMEM((SLICE, D), BF16),
            pltpu.SemaphoreType.DMA((7,)),
        ],
        field, gain_attn, table, weight, bias, cot, row_pick, col_pick, w_gate, w_up, w_down,
        far=3,
    )

    to_up = permutation(lambda x, y, z, core: (x, y, (z + 1) % 4, core))
    to_down = permutation(lambda x, y, z, core: (x, y, (z + 3) % 4, core))
    o_late, o_early = lax.ppermute(w_o[224:], BOTH, to_up), lax.ppermute(w_o[:224], BOTH, to_down)
    u_late, u_early = lax.ppermute(up_units, BOTH, to_up), lax.ppermute(down_units, BOTH, to_down)

    kv_a, kv_b = kv_a.reshape(32, 128, 128), kv_b.reshape(32, 128, 128)
    natural = [pltpu.VMEM((8192, 128), BF16), pltpu.VMEM((8192 // CHUNK, 128, CHUNK), BF16)]
    out_t, lse, mixed = local_call(
        attend_kernel,
        [shape((4, 64, HALF), F32), shape((4, 1, HALF), F32), shape((256, HALF), BF16)],
        natural + [pltpu.VMEM((64, HALF), F32)],
        2,
        8 << 30,
        order, owned, kv_a, kv_b, queries,
    )

    def pair(dims, dtype=BF16, other=None):
        return [pltpu.VMEM((3,) + dims, dtype), pltpu.VMEM((3,) + (other or dims), dtype)]

    exchange = [pltpu.VMEM((4, 2, 128, D), BF16)] + [pltpu.VMEM((4, 128, D), BF16)] * 2 + pair((64, D))
    (
        mixed_all, o_core, mixed_out, grad_hidden, branch_all, grad_gain_mlp, grad_w_gate, grad_w_up, down_part,
    ) = remote_call(
        feed_kernel,
        1,
        [
            shape((2, 256, HALF), BF16),
            shape((HALF, D), BF16),
            shape((128, D), BF16),
            shape((128, D), F32),
            shape((2, 128, D), BF16),
            shape((1, D), F32),
            shape((7, FF), F32),
            shape((7, FF), F32),
            shape((40, D), F32),
        ],
        80,
        [
            pltpu.VMEM((D, D), BF16),
            pltpu.VMEM((D, 2 * PADDED), BF16),
            pltpu.VMEM((128, D), F32),
            pltpu.VMEM((4, 2, 128, D), BF16),
            pltpu.VMEM((1024, 1024), BF16),
            pltpu.VMEM((PADDED, 1024), BF16),
            pltpu.VMEM((1024, PADDED), BF16),
            pltpu.VMEM((1024, PADDED), BF16),
        ]
        + exchange
        + exchange
        + [
            pltpu.VMEM((128, D), F32),
            pltpu.VMEM((4, 4, 64, PADDED), BF16),
            pltpu.VMEM((4, 4, 64, PADDED), BF16),
            pltpu.VMEM((4, 160, D), BF16),
            pltpu.VMEM((4, 64, PADDED), BF16),
            pltpu.VMEM((4, 64, PADDED), BF16),
            pltpu.VMEM((4, 40, D), F32),
            pltpu.VMEM((8, 8, 2 * PADDED), F32),
            pltpu.VMEM((8, 8, 2 * PADDED), F32),
        ]
        + pair((2, 64, PADDED)) + pair((32, PADDED))
        + pair((2, 64, PADDED)) + pair((32, PADDED))
        + pair((80, D)) + pair((24, D), F32, (16, D)),
        mixed, w_o, o_early, o_late, own_units, u_early, u_late, down_weight, cot_all, field, gain_mlp,
        owners, col_pick,
    )
    down_owner = permutation(
        lambda x, y, z, core: (2 * (z // 2) + core, x, 2 * (y // 2) + z % 2, y % 2)
    )
    grad_w_down = lax.ppermute(down_part, BOTH, down_owner)[:38]

    grad_query, part_a, part_b = local_call(
        attend_back_kernel,
        [shape((256, HALF), F32), shape((32, 128, 128), BF16), shape((32, 128, 128), BF16)],
        natural + [pltpu.VMEM((8192, 128), F32), pltpu.VMEM((64, HALF), F32)],
        2,
        24 << 30,
        order, owned, kv_a, kv_b, queries, branch_all, o_core, out_t, lse,
    )

    def three(columns):
        return pair((2, 4, 16, columns)) + pair((2, 16, columns)) + pair((8, columns), F32)

    def stages(columns):
        return [
            pltpu.VMEM((4, 4, 16, columns), BF16),
            pltpu.VMEM((4, 16, columns), F32),
            pltpu.VMEM((2, 8, columns), F32),
            pltpu.VMEM((2, 8, columns), F32),
        ]

    chips = (4, 4, 2, 128, 128)
    d_tokens, grad_w_q, grad_w_k, grad_w_v, grad_w_o, vector = remote_call(
        finish_kernel,
        2,
        [
            shape((128, D), F32),
            shape((7, D), F32),
            shape((7, 128), F32),
            shape((7, 128), F32),
            shape((7, D), F32),
            shape((1, 3072), F32),
        ],
        80,
        [
            pltpu.VMEM((256, 128), F32),
            pltpu.VMEM((4, 2, 128, 128), BF16),
            pltpu.VMEM((4, 2, 128, 128), BF16),
            pltpu.VMEM((2, 128, 128), F32),
            pltpu.VMEM((2, 128, 128), F32),
            pltpu.VMEM((4, 4, 4, 16, PADDED), BF16),
            pltpu.VMEM((4, 4, 4, 16, HALF), BF16),
            pltpu.VMEM((2, 128, D), F32),
        ]
        + (pair((2, 2, 128, 128)) + pair((128, 128))) * 2
        + [pltpu.VMEM((128, 128), F32)] * 2
        + [pltpu.VMEM((128, D), F32)]
        + stages(PADDED)
        + stages(HALF)
        + three(PADDED)
        + three(HALF)
        + [pltpu.VMEM((5, 1, 3072), F32), pltpu.VMEM((10, 1, 3072), F32)],
        part_a.reshape(chips), part_b.reshape(chips), grad_query, table_all, weight_all, normed_all,
        mixed_all, core_columns(branch_all.reshape(256, D)), owners, owners_half, grad_hidden, field,
        gain_attn, grad_gain_mlp,
    )
    sums = vector[0]
    return (
        mixed_out[None],
        d_tokens[None],
        grad_w_q,
        grad_w_k,
        grad_w_v,
        grad_w_o,
        grad_w_gate,
        grad_w_up,
        grad_w_down,
        sums[:D],
        sums[D : 2 * D],
        sums[2 * D : 3 * D],
        sums[3 * D : 3 * D + 128],
        sums[3 * D + 128 : 3 * D + 256],
    )


def solution(mesh):
    rows, flat = P("fsdp", None), P(("fsdp", "ctx"), None)
    field = P("fsdp", "ctx", None)
    return jax.shard_map(
        per_device,
        mesh=mesh,
        in_specs=(
            field, rows, P("fsdp", "ctx"), field, P(), rows, P(), rows, P(), rows, P(), rows, P(),
            rows, rows, rows,
        ),
        out_specs=(field, field) + (flat,) * 7 + (P(),) * 5,
        check_vma=False,
    )
```

```python
import functools

import jax
import jax.numpy as jnp
import numpy as np
from jax import lax
from jax.experimental import pallas as pl
from jax.experimental.pallas import tpu as pltpu
from jax.sharding import PartitionSpec as P

D = 896
H = 14
HD = 64
HALF = 448
FF = 4864
SLICE = 608
PADDED = 640
CHUNK = 512
EPSILON = 1e-06
THETA = 1000000.0
MASKED = -1e30
MESH = pl.DeviceIdType.MESH
F32 = jnp.float32
BF16 = jnp.bfloat16
VMEM_LIMIT = 56 * 1024 * 1024


def own_place():
    f, c = lax.axis_index("fsdp"), lax.axis_index("ctx")
    zh = lax.rem(lax.div(c, 2), 2)
    return (lax.div(c, 16), lax.rem(lax.div(c, 4), 4), zh * 2 + f, lax.rem(c, 2))


def device(place):
    x, y, z, core = place
    return (lax.rem(z, 2), (x * 4 + y) * 4 + 2 * lax.div(z, 2) + core)


def turned(value, step):
    return lax.rem(value + (step + 4), 4)


def shifted(place, axis, step):
    moved = list(place)
    moved[axis] = turned(place[axis], step)
    return tuple(moved)


def partner(place):
    return place[:3] + (1 - place[3],)


def greet(places):
    barrier = pltpu.get_barrier_semaphore()
    for place in places:
        pl.semaphore_signal(barrier, inc=1, device_id=device(place), device_id_type=MESH)
    pl.semaphore_wait(barrier, len(places))


class Links:
    def __init__(self, send, recv):
        self.send, self.recv, self.opened = send, recv, []

    def made(self, src, dst, place, sent, received):
        return pltpu.make_async_remote_copy(
            src_ref=src,
            dst_ref=dst,
            send_sem=self.send.at[sent],
            recv_sem=self.recv.at[received],
            device_id=device(place),
            device_id_type=MESH,
        )

    def start(self, src, dst, place, received=None):
        at = len(self.opened)
        assert at < self.send.shape[0]
        copy = self.made(src, dst, place, at, at if received is None else received)
        copy.start()
        self.opened.append(copy)
        return copy

    def close(self):
        for copy in self.opened:
            copy.wait_send()


def ring_gather(links, slot, half, place, axis):
    me = place[axis]
    right, left = shifted(place, axis, 1), shifted(place, axis, -1)
    first = links.start(slot(me), slot(me), right)
    second = links.start(slot(me), slot(me), left)
    yield
    before, after = turned(me, -1), turned(me, 1)
    first.wait_recv()
    third = links.start(half(before, 0), half(before, 0), right)
    yield
    second.wait_recv()
    fourth = links.start(half(after, 1), half(after, 1), left)
    yield
    third.wait_recv()
    fourth.wait_recv()


def ring_reduce(links, part, low, high, place, axis, emit):
    me = place[axis]
    right, left = shifted(place, axis, 1), shifted(place, axis, -1)
    before, after, far = turned(me, -1), turned(me, 1), turned(me, 2)
    first = links.start(part(far, 0), low.at[0], right)
    second = links.start(part(far, 1), high.at[0], left)
    yield
    third = links.start(part(after, 1), high.at[1], right)
    yield
    fourth = links.start(part(before, 0), low.at[1], left)
    yield
    first.wait_recv()
    low[0] = (low[0].astype(F32) + part(after, 0)[...].astype(F32)).astype(low.dtype)
    fifth = links.start(low.at[0], low.at[2], right)
    second.wait_recv()
    high[0] = (high[0].astype(F32) + part(before, 1)[...].astype(F32)).astype(high.dtype)
    sixth = links.start(high.at[0], high.at[2], left)
    yield
    fourth.wait_recv()
    fifth.wait_recv()
    emit(0, part(me, 0)[...].astype(F32) + low[1].astype(F32) + low[2].astype(F32))
    third.wait_recv()
    sixth.wait_recv()
    emit(1, part(me, 1)[...].astype(F32) + high[1].astype(F32) + high[2].astype(F32))


def direct_reduce(links, places, part, landing, own, emit):
    copies = [links.start(part(at), landing.at[i], at) for i, at in enumerate(places)]
    yield
    total = own[...].astype(F32)
    for i, copy in enumerate(copies):
        copy.wait_recv()
        total = total + landing[i].astype(F32)
    emit(total)


def around(place, steps):
    places = []
    for step in steps:
        at = place
        for axis, by in enumerate(step):
            if by:
                at = shifted(at, axis, by)
        places.append(at)
    return places


def in_turn(*streams):
    waiting = list(streams)
    while waiting:
        still = []
        for stream in waiting:
            try:
                next(stream)
            except StopIteration:
                continue
            still.append(stream)
        waiting = still


def local_norm(field, gain):
    inverse = lax.rsqrt(jnp.mean(field * field, axis=-1, keepdims=True) + EPSILON)
    return field * inverse * gain, inverse


def norm_backward(field, inverse, gain, grad):
    scaled = grad * gain
    grad_gain = jnp.sum(grad * field * inverse, axis=0, keepdims=True)
    mean = jnp.mean(scaled * field, axis=-1, keepdims=True)
    return inverse * scaled - field * (inverse * inverse * inverse) * mean, grad_gain


def dot(left, right, contract=((1,), (0,))):
    return lax.dot_general(left, right, (contract, ((), ())), preferred_element_type=F32)


def whole(count):
    return [pl.BlockSpec(memory_space=pltpu.VMEM)] * count


def shape(dims, dtype):
    return jax.ShapeDtypeStruct(dims, dtype)


def remote_call(kernel, collective_id, outs, copies, scratch, *args, far=0):
    return pl.pallas_call(
        kernel,
        out_shape=outs,
        in_specs=whole(len(args) - far) + [pl.BlockSpec(memory_space=pl.ANY)] * far,
        out_specs=whole(len(outs)),
        scratch_shapes=list(scratch)
        + [pltpu.SemaphoreType.DMA((copies,)), pltpu.SemaphoreType.DMA((copies,))],
        compiler_params=pltpu.CompilerParams(
            collective_id=collective_id, has_side_effects=True, vmem_limit_bytes=VMEM_LIMIT
        ),
    )(*args)


KV_A_STEPS = [(0, dy, dz) for dz in (0, 2) for dy in (0, 1, -1, 2) if dy or dz]
KV_B_STEPS = [(dx, 0, dz) for dz in (0, 2) for dx in (0, 1, -1, 2) if dx or dz]


def enter_kernel(
    tokens, gain, table, weight, bias, cot, row_pick, col_pick, w_o, w_gate, w_up, w_down,
    normed_all, table_all, weight_all, w_o_all, queries, kv_a, kv_b, cot_all, own_units, up_units, down_units, down_rows,
    own_window, up_window, down_window, tall_window, fetched, send, recv,
):
    place = own_place()
    x, y, z, core = place
    f, zh = lax.rem(z, 2), lax.div(z, 2)
    other, up, down, far = partner(place), shifted(place, 2, 1), shifted(place, 2, -1), shifted(place, 2, 2)
    fetches = []

    def fetch(src, dst):
        copy = pltpu.make_async_copy(src, dst, fetched.at[len(fetches)])
        copy.start()
        fetches.append(copy)

    def offset(at):
        part = 4 * lax.rem(at[2], 2) + 2 * lax.div(at[2], 2) + at[3]
        start = jnp.minimum(lax.div(19 * part, 4), 32) * 128
        return start, SLICE * part - start

    windows = ((own_window, place, 0, HALF), (up_window, up, 224, 224), (down_window, down, 0, 224))
    for window, at, row, rows in windows:
        columns = pl.ds(pl.multiple_of(offset(at)[0], 128), 768)
        for which, array in enumerate((w_gate, w_up)):
            fetch(array.at[pl.ds(row, rows), columns], window.at[which])
    sub = 2 * zh + core
    fetch(w_down.at[pl.ds(pl.multiple_of(sub * SLICE, 16), SLICE)], tall_window)
    a_peers = around(place, KV_A_STEPS)
    b_peers = around(place, KV_B_STEPS)
    greet([other, up, down, far] + [at for at in a_peers + b_peers if at is not far])
    links = Links(send, recv)
    base = pl.multiple_of(f * HALF, HALF)
    w_down_copy = links.start(weight.at[pl.ds(0, 224)], weight_all.at[pl.ds(base, 224)], down)
    w_up_copy = links.start(weight.at[pl.ds(224, 224)], weight_all.at[pl.ds(base + 224, 224)], up)
    normed, _ = local_norm(tokens[...].astype(F32), gain[...])
    normed_all[core] = normed.astype(BF16)
    n_copy = links.start(normed_all.at[core], normed_all.at[core], other)
    table_all[core] = table[...]
    t_copy = links.start(table_all.at[core], table_all.at[core], other)
    cot_all[z, core] = cot[...]
    c_copy = links.start(cot_all.at[z, core], cot_all.at[z, core], other)
    weight_all[pl.ds(base, HALF)] = weight[...]
    for copy in fetches:
        copy.wait()
    n_copy.wait_recv()
    t_copy.wait_recv()
    w_down_copy.wait_recv()
    w_up_copy.wait_recv()
    lin = dot(normed_all[...].reshape(256, D), weight_all[...]) + bias[...]
    turn = lin[:, :512]
    lane = lax.broadcasted_iota(jnp.int32, (256, 512), 1)
    swapped = jnp.where(lax.rem(lane, 64) < 32, -pltpu.roll(turn, 480, 1), pltpu.roll(turn, 32, 1))
    both = table_all[...].reshape(256, 128)
    cosine = jnp.concatenate([both[:, :64]] * 8, axis=1)
    sine = jnp.concatenate([both[:, 64:]] * 8, axis=1)
    rotated = turn * cosine + swapped * sine
    kv = jnp.concatenate([rotated[:, HALF:512], lin[:, 512:576]], axis=1).astype(BF16)
    kv_a[x, y, zh] = kv[:128]
    kv_b[x, y, zh] = kv[128:]
    a_copies = [links.start(kv_a.at[x, y, zh], kv_a.at[x, y, zh], at) for at in a_peers]
    b_copies = [links.start(kv_b.at[x, y, zh], kv_b.at[x, y, zh], at) for at in b_peers]
    o_down = links.start(w_o.at[pl.ds(0, 224)], w_o_all.at[pl.ds(base, 224)], down)
    o_up = links.start(w_o.at[pl.ds(224, 224)], w_o_all.at[pl.ds(base + 224, 224)], up)
    w_o_all[pl.ds(base, HALF)] = w_o[...]
    queries[...] = (rotated[:, :HALF] * HD**-0.5).astype(BF16)

    def stream_a():
        for copy in a_copies:
            copy.wait_recv()
        yield from ring_gather(
            links, lambda k: kv_a.at[k], lambda k, h: kv_a.at[k, pl.ds(2 * h, 2)], place, 0
        )

    def stream_b():
        for copy in b_copies:
            copy.wait_recv()
        yield from ring_gather(
            links,
            lambda k: kv_b.at[pl.ds(0, 4), k],
            lambda k, h: kv_b.at[pl.ds(2 * h, 2), k],
            place,
            1,
        )

    def units():
        for (window, at, _, rows), out in zip(windows, (own_units, up_units, down_units)):
            line = lax.broadcasted_iota(jnp.int32, (768, PADDED), 0) - offset(at)[1]
            pick = (line == row_pick[...]).astype(F32).astype(BF16)
            for which in range(2):
                out[:, PADDED * which : PADDED * (which + 1)] = dot(window[which], pick).astype(BF16)
            yield
        line = lax.broadcasted_iota(jnp.int32, (PADDED, SLICE), 1)
        pick = (line == col_pick[...]).astype(F32).astype(BF16)
        down_rows[...] = dot(pick, tall_window[...]).astype(BF16)

    in_turn(stream_a(), stream_b(), units(), shared_gather(links, cot_all, place, c_copy))
    o_down.wait_recv()
    o_up.wait_recv()
    links.close()


def shared_gather(links, blocks, place, own_copy):
    z, core = place[2], place[3]
    other = partner(place)
    copies = [own_copy]
    ring = ring_gather(
        links,
        lambda k: blocks.at[k, core],
        lambda k, h: blocks.at[k, core, pl.ds(64 * h, 64)],
        place,
        2,
    )
    next(ring)
    yield
    next(ring)
    before = turned(z, -1)
    copies.append(links.start(blocks.at[before, core], blocks.at[before, core], other))
    yield
    next(ring)
    after = turned(z, 1)
    copies.append(links.start(blocks.at[after, core], blocks.at[after, core], other))
    yield
    for _ in ring:
        yield
    last = turned(z, 2)
    copies.append(links.start(blocks.at[last, core], blocks.at[last, core], other))
    yield
    for copy in copies:
        copy.wait_recv()


def down_group(place):
    x, y, z, core = place
    return lax.rem(x + y + 5 - (2 * lax.div(z, 2) + core), 4)


def feed_kernel(
    mixed, w_o, u_own, u_early, u_late, w_down, cot_all, tokens, gain, owners, owners_half,
    mixed_out, grad_hidden, branch_all, grad_gain, *rest,
):
    gate, up, down, part_o = rest[0:4], rest[4:8], rest[8:12], rest[12:16]
    (
        mixed_all, w_units, hidden, normed_all, spread_t, inner_t, grad_gates, grad_ups, up_all, o_all,
        out_part, out_arrived, out_paired, out_low, out_high,
        grad_part, grad_arrived, grad_paired, grad_low, grad_high, grad_sum, send, recv,
    ) = rest[16:]
    place = own_place()
    x, y, z, core = place
    f = lax.rem(z, 2)
    other = partner(place)
    greet([other, shifted(place, 2, 1), shifted(place, 2, -1)])
    links = Links(send, recv)
    copy = links.start(mixed, mixed_all.at[core], other)
    mixed_all[core] = mixed[...]
    own_base = pl.multiple_of(f * HALF, HALF)
    base = pl.multiple_of((1 - f) * HALF, HALF)
    copy.wait_recv()
    rows = pl.ds(pl.multiple_of(core * 128, 128), 128)
    field = tokens[...].astype(F32) + (
        dot(mixed_all[0, rows], w_o[:HALF]) + dot(mixed_all[1, rows], w_o[HALF:])
    )
    hidden[...] = field
    normed, _ = local_norm(field, gain[...])
    normed_all[z, core] = normed.astype(BF16)
    own = links.start(normed_all.at[z, core], normed_all.at[z, core], other)

    def assemble():
        w_units[pl.ds(own_base, HALF)] = u_own[...]
        yield
        w_units[pl.ds(base, 224)] = u_early[...]
        w_units[pl.ds(base + 224, 224)] = u_late[...]

    in_turn(shared_gather(links, normed_all, place, own), assemble())

    before, after, far = turned(z, -1), turned(z, 1), turned(z, 2)
    both = (
        (out_part, out_arrived, out_paired), (grad_part, grad_arrived, grad_paired),
    )

    def tile(k):
        n = normed_all[k].reshape(256, D)
        c = cot_all[k].reshape(256, D)
        g = dot(n, w_units[:, :PADDED])
        u = dot(n, w_units[:, PADDED:])
        s = 1.0 / (1.0 + jnp.exp(-g))
        silu = g * s
        inner = silu * u
        low = inner.astype(BF16)
        out_part[k] = dot(low, w_down[...]).astype(BF16).reshape(2, 128, D)
        columns = pl.ds(pl.multiple_of(k * 256, 256), 256)
        inner_t[:, columns] = low.T
        gi = dot(c, w_down[...], ((1,), (1,)))
        gg = (gi * u * s * (1.0 + g * (1.0 - s))).astype(BF16)
        gu = (gi * silu).astype(BF16)
        grad_gates[columns] = gg
        grad_ups[columns] = gu
        grad_part[k] = (
            dot(gg, w_units[:, :PADDED], ((1,), (1,))) + dot(gu, w_units[:, PADDED:], ((1,), (1,)))
        ).astype(BF16).reshape(2, 128, D)
        return [links.start(part.at[k, 1 - core], come.at[k], other) for part, come, _ in both]

    def pair_up(k, copies):
        for trip, (part, come, paired) in zip(copies, both):
            trip.wait_recv()
            paired[k] = (come[k].astype(F32) + part[k, core].astype(F32)).astype(BF16)

    def emit_out(h, value):
        at = pl.ds(64 * h, 64)
        mixed_out[at] = (hidden[at] + value).astype(BF16)

    def emit_grad(h, value):
        grad_sum[pl.ds(64 * h, 64)] = value

    reduces = [
        ring_reduce(
            links, lambda k, h, p=paired: p.at[k, pl.ds(64 * h, 64)], low, high, place, 2, emit
        )
        for paired, low, high, emit in (
            (grad_paired, grad_low, grad_high, emit_grad),
            (out_paired, out_low, out_high, emit_out),
        )
    ]

    def advance():
        for stream in reduces:
            next(stream, None)

    trips = tile(far)
    pair_up(far, trips)
    advance()
    trips = tile(after)
    pair_up(after, trips)
    advance()
    trips = tile(before)
    pair_up(before, trips)
    advance()
    trips = tile(z)
    advance()
    pair_up(z, trips)

    advance()

    @pl.loop(0, 4)
    def _(k):
        columns = pl.ds(pl.multiple_of(k * 256, 256), 256)
        spread_t[:, columns] = dot(
            owners[...], normed_all[k].reshape(256, D), ((1,), (1,))
        ).astype(BF16)

    for step in range(4):
        lines = spread_t[pl.ds(pl.multiple_of(turned(x, step) * 256, 256), 256)]
        gate[step][...] = dot(lines, grad_gates[...]).astype(BF16).reshape(4, 64, PADDED)
        lines = spread_t[pl.ds(256 * step, 256)]
        up_all[step] = dot(lines, grad_ups[...]).astype(BF16).reshape(4, 64, PADDED)
        if step == 1:
            advance()
        group = down_group(shifted(place, 0, step))
        lines = inner_t[pl.ds(pl.multiple_of(group * 160, 16), 160)]
        down[step][...] = dot(lines, cot_all[...].reshape(1024, D)).astype(BF16)
    for step in range(4):
        at = turned(y, step)
        for k in range(4):
            up[step][k] = up_all[k, at]
    spread_o = (
        dot(owners_half[0], mixed_all[0], ((1,), (1,))) + dot(owners_half[1], mixed_all[1], ((1,), (1,)))
    ).astype(BF16)
    for _ in range(8):
        advance()
    field = hidden[...]
    _, inverse = local_norm(field, gain[...])
    through, gains = norm_backward(field, inverse, gain[...], grad_sum[...])
    grad_gain[...] = gains
    total = cot_all[z, core].astype(F32) + through
    grad_hidden[...] = total
    branch_all[core] = total.astype(BF16)
    trip = links.start(branch_all.at[core], branch_all.at[core], other)
    trip.wait_recv()
    branch = branch_all[...].reshape(256, D).astype(F32)
    half = jnp.where(core == 0, branch[:, :HALF], branch[:, HALF:]).astype(BF16)
    o_all[...] = dot(spread_o, half).astype(BF16).reshape(4, 4, 4, 16, HALF)
    for step in range(4):
        at = turned(z, step)
        for k in range(4):
            part_o[step][k] = o_all[k, pl.ds(0, 4), at]
    links.close()


def finish_kernel(
    kv_part_a, kv_part_b, grad_query, table_all, weight_all, normed_all, owners, grad_hidden, tokens, gain,
    gain_mlp_grad, col_pick, *rest,
):
    gate, up, down, part_o, rest = rest[0:4], rest[4:8], rest[8:12], rest[12:16], rest[16:]
    (
        d_tokens, wq_out, wk_out, wv_out, wo_out, gate_out, up_out, down_out, vector_out,
        grad_kv, kv_mid_a, kv_mid_b, kv_land_a, kv_land_b, part_qa, part_qb, grad_normed, half_sum,
        gate_mid, gate_land, up_mid, up_land, down_mid, down_land, end, rows_all,
        o_mid, o_land, o_end, o_rows, qa_mid, qa_land, qa_end, qa_rows, qb_mid, qb_land, qb_end, qb_rows,
        vec_now, vec_in,
        a_low, a_high, b_low, b_high, qa_low, qa_high, qb_low, qb_high, send, recv,
    ) = rest
    place = own_place()
    x, y, z, core = place
    f, zh = lax.rem(z, 2), lax.div(z, 2)
    sub = 2 * zh + core
    other = partner(place)
    mine = z * 2 + core
    x_peers, y_peers = around(place, X_STEPS), around(place, Y_STEPS)
    xy_peers, xz_peers, yz_peers = (
        around(place, steps) for steps in (XY_STEPS, XZ_STEPS, YZ_STEPS)
    )
    ring = []
    for step in range(1, 8):
        at = lax.rem(mine + step, 8)
        ring.append((x, y, lax.div(at, 2), lax.rem(at, 2)))
    quarter = down_group(place)
    to_owner = [(sub, quarter, 2 * (k // 2) + f, k % 2) for k in range(4)]
    from_group = [
        (lax.rem(y + x + 7 - k, 4), k, 2 * lax.div(x, 2) + f, lax.rem(x, 2)) for k in range(4)
    ]
    greet(ring + xy_peers + xz_peers[3:] + yz_peers[3:] + to_owner + from_group)
    links = Links(send, recv)

    def kv_stream(part, mid, landing, order, low, high, peers, base):
        def put_mid(h, value):
            mid[pl.ds(2 * h, 2)] = value.astype(BF16)

        def put_end(value):
            grad_kv[pl.ds(base, 128)] = value

        if order == 0:
            first = lambda k, h: part.at[k, pl.ds(2 * h, 2)]
        else:
            first = lambda k, h: part.at[pl.ds(2 * h, 2), k]
        yield from ring_reduce(links, first, low, high, place, order, put_mid)
        keep = 1 - order
        yield from direct_reduce(
            links, peers, lambda at: mid.at[at[keep], lax.div(at[2], 2)], landing,
            mid.at[place[keep], zh], put_end,
        )

    def to_rows(end, rows):
        last = links.start(end.at[1 - core], rows.at[core], other)
        rows[core] = end[core]
        yield
        last.wait_recv()

    def q_stream(part, mid, landing, end, rows, order, low, high, peers):
        def put_mid(h, value):
            mid[pl.ds(2 * h, 2)] = value.astype(BF16)

        def put_end(value):
            end[0], end[1] = value[:8], value[8:]

        if order == 0:
            first = lambda k, h: part.at[k, pl.ds(2 * h, 2)]
        else:
            first = lambda k, h: part.at[pl.ds(2 * h, 2), k]
        yield from ring_reduce(links, first, low, high, place, order, put_mid)
        keep = 1 - order
        yield from direct_reduce(
            links, peers, lambda at: mid.at[at[keep], at[2]], landing, mid.at[place[keep], z], put_end
        )
        yield from to_rows(end, rows)

    def o_stream():
        def put_end(value):
            o_end[0], o_end[1] = value[:8], value[8:]

        for k in range(4):
            total = sum(part_o[step][k].astype(F32) for step in range(4))
            o_mid[k] = total.astype(BF16)
        yield from direct_reduce(
            links, xy_peers, lambda at: o_mid.at[at[0], at[1]], o_land, o_mid.at[x, y], put_end
        )
        yield from to_rows(o_end, o_rows)

    def wide(parts, mid, landing, axis, peers, column):
        def put_end(value):
            end[:, :, pl.ds(column, PADDED)] = value.reshape(8, 8, PADDED)

        for k in range(4):
            total = sum(parts[step][k].astype(F32) for step in range(4))
            mid[k] = total.astype(BF16)
        yield
        yield from direct_reduce(
            links, peers, lambda at: mid.at[at[axis]], landing, mid.at[place[axis]], put_end
        )

    def tall():
        for k in range(4):
            down_mid[k] = sum(down[step][...].astype(F32)[40 * k : 40 * (k + 1)] for step in range(4))
        yield
        base = len(links.opened)
        for k, at in enumerate(to_owner):
            links.start(down_mid.at[k], down_land.at[y], at, base + y)
        yield
        for k in range(4):
            links.made(down_mid.at[k], down_land.at[k], to_owner[k], base + k, base + k).wait_recv()
        total = (down_land[0] + down_land[1]) + (down_land[2] + down_land[3])
        down_out[...] = total[:38]

    def hidden_units():
        gates = wide(gate, gate_mid, gate_land, 1, y_peers, 0)
        ups = wide(up, up_mid, up_land, 0, x_peers, PADDED)
        for _ in range(2):
            next(gates)
            next(ups)
            yield
        for stream in (gates, ups):
            for _ in stream:
                pass
        copies = [
            links.start(end.at[to[2] * 2 + to[3]], rows_all.at[mine], to) for to in ring
        ]
        rows_all[mine] = end[mine]
        yield
        line = lax.broadcasted_iota(jnp.int32, (PADDED, SLICE), 1)
        pick = (line == col_pick[...]).astype(F32).astype(BF16)
        for copy in copies:
            copy.wait_recv()
        for which, out in enumerate((gate_out, up_out)):
            values = rows_all[:, :, PADDED * which : PADDED * (which + 1)].reshape(64, PADDED)
            top = values.astype(BF16)
            below = (values - top.astype(F32)).astype(BF16)
            units = dot(top, pick) + dot(below, pick)
            for at in range(8):
                part = 4 * (at // 2 % 2) + 2 * (at // 4) + at % 2
                out[:, SLICE * part : SLICE * (part + 1)] = units[8 * at : 8 * at + 7]

    kv_streams = [
        kv_stream(kv_part_a, kv_mid_a, kv_land_a, 0, a_low, a_high, yz_kv(place), 0),
        kv_stream(kv_part_b, kv_mid_b, kv_land_b, 1, b_low, b_high, xz_kv(place), 128),
    ]
    units, talls, os = hidden_units(), tall(), o_stream()
    for _ in range(3):
        for stream in kv_streams:
            next(stream)
    next(units)
    next(talls)
    spread_n = dot(owners[...], normed_all[...].reshape(256, D), ((1,), (1,))).astype(BF16)
    for stream in kv_streams:
        next(stream)
    next(units)
    next(talls)
    next(os)
    in_turn(*kv_streams)

    table = table_all[...].reshape(256, 128)
    cosine = jnp.concatenate([table[:, :64]] * 8, axis=1)
    sine = jnp.concatenate([table[:, 64:]] * 8, axis=1)
    turn = jnp.concatenate([grad_query[...] * HD**-0.5, grad_kv[:, :64]], axis=1)
    scaled = turn * sine
    lane = lax.broadcasted_iota(jnp.int32, (256, 512), 1)
    swapped = jnp.where(
        lax.rem(lane, 64) < 32, pltpu.roll(scaled, 480, 1), -pltpu.roll(scaled, 32, 1)
    )
    lin = jnp.concatenate(
        [turn * cosine + swapped, grad_kv[:, 64:], jnp.zeros((256, 64), F32)], axis=1
    ).astype(BF16)
    part = dot(spread_n, lin).astype(BF16)
    part_qa[...] = part[:, :384].reshape(4, 4, 4, 16, 384)
    part_qb[...] = part[:, 384:].reshape(4, 4, 4, 16, 256)
    q_streams = [
        q_stream(part_qa, qa_mid, qa_land, qa_end, qa_rows, 0, qa_low, qa_high, yz_peers),
        q_stream(part_qb, qb_mid, qb_land, qb_end, qb_rows, 1, qb_low, qb_high, xz_peers),
    ]
    for _ in range(3):
        for stream in q_streams:
            next(stream)

    def sums():
        grad_normed[...] = dot(lin, weight_all[...], ((1,), (1,))).reshape(2, 128, D)
        copy = links.start(grad_normed.at[1 - core], half_sum, other)
        column = jnp.sum(lin.astype(F32), axis=0, keepdims=True)

        def placed(values):
            empty = jnp.zeros_like(values)
            return jnp.where(
                core == 0,
                jnp.concatenate([values, empty], axis=1),
                jnp.concatenate([empty, values], axis=1),
            )

        biases = [placed(column[:, low:high]) for low, high in ((0, HALF), (HALF, 512), (512, 576))]
        copy.wait_recv()
        grad = grad_normed[core] + half_sum[...]
        field = tokens[...].astype(F32)
        _, inverse = local_norm(field, gain[...])
        through, gains = norm_backward(field, inverse, gain[...], grad)
        d_tokens[...] = grad_hidden[...] + through
        vec_now[0] = jnp.concatenate(
            [gains, gain_mlp_grad[...], *biases, jnp.zeros((1, 128), F32)], axis=1
        )
        trip = links.start(vec_now.at[0], vec_in.at[0], other)
        trip.wait_recv()
        vec_now[1] = vec_now[0] + vec_in[0]
        for stage, axis in enumerate((2, 1, 0)):
            trips = [
                links.start(
                    vec_now.at[1 + stage],
                    vec_in.at[1 + 3 * stage + at],
                    shifted(place, axis, step),
                )
                for at, step in enumerate((1, -1, 2))
            ]
            yield
            for trip in trips:
                trip.wait_recv()
            at = 1 + 3 * stage
            near = vec_in[at] + vec_in[at + 1]
            vec_now[2 + stage] = (vec_now[1 + stage] + vec_in[at + 2]) + near
        vector_out[...] = vec_now[4]

    in_turn(sums(), *q_streams, os, units, talls)

    def row_of(core_at):
        return jnp.concatenate([qa_rows[core_at], qb_rows[core_at]], axis=1)[:7]

    first, second = row_of(0), row_of(1)
    for out, low, high in ((wq_out, 0, HALF), (wk_out, HALF, 512), (wv_out, 512, 576)):
        out[...] = jnp.concatenate([first[:, low:high], second[:, low:high]], axis=1)
    wo_out[...] = jnp.concatenate([o_rows[0][:7], o_rows[1][:7]], axis=1)
    links.close()


AROUND = (0, 1, -1, 2)
X_STEPS = [(d, 0, 0) for d in AROUND[1:]]
Y_STEPS = [(0, d, 0) for d in AROUND[1:]]
XY_STEPS = [(dx, dy, 0) for dy in AROUND for dx in AROUND if dx or dy]
XZ_STEPS = [(dx, 0, dz) for dz in AROUND for dx in AROUND if dx or dz]
YZ_STEPS = [(0, dy, dz) for dz in AROUND for dy in AROUND if dy or dz]


def yz_kv(place):
    return around(place, KV_A_STEPS)


def xz_kv(place):
    return around(place, KV_B_STEPS)


def tidy_kernel(*refs):
    half = len(refs) // 2
    for src, dst in zip(refs[:half], refs[half:]):
        dst[...] = src[...]


def natural_order(order, kv_a, kv_b, kv, kv_t):
    @pl.loop(0, 32)
    def _(chip):
        for t in range(4):
            block = kv_a[chip, pl.ds(64 * t, 64)] if t < 2 else kv_b[chip, pl.ds(64 * (t - 2), 64)]
            at = pl.multiple_of(order[4 * chip + t] * 64, 64)
            kv[pl.ds(at, 64)] = block

    @pl.loop(0, 8192 // CHUNK)
    def _(c):
        kv_t[c] = kv[pl.ds(pl.multiple_of(c * CHUNK, CHUNK), CHUNK)].T


def allowed_at(c, base):
    key = c * CHUNK + lax.broadcasted_iota(jnp.int32, (CHUNK, HALF), 0)
    lane = lax.broadcasted_iota(jnp.int32, (CHUNK, HALF), 1)
    return key <= base + lax.rem(lane, 64)


def by_head(rows):
    return jnp.concatenate([rows[:, 64 * h : 64 * (h + 1)] for h in range(7)], axis=0)


def side_by_side(columns_t):
    stacked = columns_t.T
    return jnp.concatenate([stacked[64 * h : 64 * (h + 1)] for h in range(7)], axis=1)


def attend_kernel(order, owned, kv_a, kv_b, queries, out_t, lse, mixed, kv, kv_t, acc):
    natural_order(order, kv_a, kv_b, kv, kv_t)
    none = jnp.zeros((64, HALF), F32)
    for t in range(4):
        spot = owned[t]
        rows = by_head(queries[64 * t : 64 * (t + 1)].astype(F32))
        q_t = jnp.concatenate([rows.T, none], axis=0).astype(BF16)
        last = lax.div(spot * 64, CHUNK)
        acc[...] = jnp.zeros_like(acc)

        def step(c, carry, masked):
            top, total = carry
            scores = dot(kv[pl.ds(pl.multiple_of(c * CHUNK, CHUNK), CHUNK)], q_t)
            if masked:
                scores = jnp.where(allowed_at(c, spot * 64), scores, MASKED)
            new_top = jnp.maximum(top, jnp.max(scores, axis=0, keepdims=True))
            probs = jnp.exp(scores - new_top)
            scale = jnp.exp(top - new_top)
            total = total * scale + jnp.sum(probs, axis=0, keepdims=True)
            acc[...] = acc[...] * scale + dot(kv_t[c, pl.ds(64, 64)], probs.astype(BF16))
            return new_top, total

        start = (jnp.full((1, HALF), MASKED, F32), jnp.zeros((1, HALF), F32))
        carry = lax.fori_loop(0, last, lambda c, carry: step(c, carry, False), start)
        top, total = step(last, carry, True)
        result = acc[...] / total
        out_t[t] = result
        mixed[64 * t : 64 * (t + 1)] = side_by_side(result).astype(BF16)
        lse[t] = top + jnp.log(total)


def attend_back_kernel(
    order, owned, kv_a, kv_b, queries, branch, w_o, out_t, lse,
    grad_query, grad_a, grad_b, kv, kv_t, acc, acc_q,
):
    natural_order(order, kv_a, kv_b, kv, kv_t)
    acc[...] = jnp.zeros_like(acc)
    grad_mixed = dot(
        branch[...].reshape(256, D), w_o[pl.ds(pl.multiple_of(owned[4] * HALF, HALF), HALF)], ((1,), (1,))
    )
    none_t, none = jnp.zeros((64, HALF), F32), jnp.zeros((HALF, 64), F32)
    for t in range(4):
        spot = owned[t]
        last = lax.div(spot * 64, CHUNK)
        rows = by_head(queries[64 * t : 64 * (t + 1)].astype(F32))
        q = jnp.concatenate([rows, none], axis=1).astype(BF16)
        q_t = jnp.concatenate([rows.T, none_t], axis=0).astype(BF16)
        rows = by_head(grad_mixed[64 * t : 64 * (t + 1)].astype(BF16).astype(F32))
        g = jnp.concatenate([none, rows], axis=1).astype(BF16)
        rows_t = rows.T
        g_t = jnp.concatenate([none_t, rows_t], axis=0).astype(BF16)
        delta = jnp.sum(rows_t * out_t[t], axis=0, keepdims=True)
        norm = lse[t]
        acc_q[...] = jnp.zeros_like(acc_q)

        def step(c, masked):
            rows = pl.ds(pl.multiple_of(c * CHUNK, CHUNK), CHUNK)
            block = kv[rows]
            scores = dot(block, q_t)
            if masked:
                scores = jnp.where(allowed_at(c, spot * 64), scores, MASKED)
            probs = jnp.exp(scores - norm)
            grad_probs = dot(block, g_t)
            grad_scores = (probs * (grad_probs - delta)).astype(BF16)
            acc[rows] += dot(probs.astype(BF16), g) + dot(grad_scores, q)
            acc_q[...] += dot(kv_t[c, pl.ds(0, 64)], grad_scores)

        def body(c, carry):
            step(c, False)
            return carry

        lax.fori_loop(0, last, body, 0)
        step(last, True)
        grad_query[64 * t : 64 * (t + 1)] = side_by_side(acc_q[...])

    @pl.loop(0, 32)
    def _(chip):
        for t in range(4):
            at = pl.multiple_of(order[4 * chip + t] * 64, 64)
            block = acc[pl.ds(at, 64)].astype(BF16)
            if t < 2:
                grad_a[chip, pl.ds(64 * t, 64)] = block
            else:
                grad_b[chip, pl.ds(64 * (t - 2), 64)] = block


def local_call(kernel, outs, scratch, scalars, flops, *args):
    return pl.pallas_call(
        kernel,
        out_shape=outs,
        in_specs=[pl.BlockSpec(memory_space=pltpu.SMEM)] * scalars + whole(len(args) - scalars),
        out_specs=[pl.BlockSpec(memory_space=pltpu.VMEM)] * len(outs),
        scratch_shapes=scratch,
        compiler_params=pltpu.CompilerParams(vmem_limit_bytes=VMEM_LIMIT),
        cost_estimate=pl.CostEstimate(flops=flops, bytes_accessed=8 << 20, transcendentals=1 << 23),
    )(*args)


def padded_columns():
    col = np.arange(PADDED)
    return np.where(col % 40 < 38, col // 40 * 38 + col % 40, -(1 << 20)).astype(np.int32)


def owner_rows():
    row = np.arange(1024)
    i, core, z, y, x = row % 8, row // 8 % 2, row // 16 % 4, row // 64 % 4, row // 256
    at = 7 * (64 * (z % 2) + 16 * x + 4 * y + 2 * (z // 2) + core) + i
    pick = np.zeros((1024, D), np.float32)
    keep = i < 7
    pick[row[keep], at[keep]] = 1.0
    return pick


def index_of(x, y, z, core):
    return (z % 2) * 64 + (x * 4 + y) * 4 + 2 * (z // 2) + core


def permutation(move):
    pairs = []
    for x in range(4):
        for y in range(4):
            for z in range(4):
                for core in range(2):
                    pairs.append((index_of(x, y, z, core), index_of(*move(x, y, z, core))))
    return pairs


BOTH = ("fsdp", "ctx")


def per_device(
    tokens, block_index, positions, cotangent, norm_attn, w_q, b_q, w_k, b_k, w_v, b_v, w_o,
    norm_mlp, w_gate, w_up, w_down,
):
    f, c = lax.axis_index("fsdp"), lax.axis_index("ctx")
    core, zh = c % 2, (c // 2) % 2
    z = 2 * zh + f
    sub = 2 * zh + core
    field, cot = tokens[0], cotangent[0]
    order = block_index[0]
    owned = lax.dynamic_slice_in_dim(order, 4 * (c // 2), 4, 0)
    owned = jnp.concatenate([owned, core[None]])
    gain_attn = norm_attn.astype(F32)[None]
    gain_mlp = norm_mlp.astype(F32)[None]

    freq = THETA ** (-(jnp.arange(HD // 2, dtype=F32) * 2.0 / HD))
    angle = positions[0].astype(F32)[:, None] * freq[None, :]
    cosine, sine = jnp.cos(angle), jnp.sin(angle)
    table = jnp.concatenate([cosine, cosine, sine, sine], -1)

    def core_columns(array):
        half = array.shape[-1] // 2
        return jnp.where(core == 0, array[..., :half], array[..., half:])

    zeros = jnp.zeros((HALF, 64), BF16)
    weight = jnp.concatenate(
        [core_columns(w_q), core_columns(w_k), core_columns(w_v), zeros], axis=1
    )
    bias = jnp.concatenate(
        [core_columns(b_q), core_columns(b_k), core_columns(b_v), zeros[0]], axis=0
    ).astype(F32)[None]

    picked = padded_columns()
    row_pick, col_pick = jnp.asarray(picked[None]), jnp.asarray(picked[:, None])
    owners = owner_rows()
    owners_half = jnp.asarray(np.stack([owners[:, :HALF], owners[:, HALF:]]), BF16)
    owners = jnp.asarray(owners, BF16)

    (
        normed_all, table_all, weight_all, w_o_all, queries, kv_a, kv_b, cot_all,
        own_units, up_units, down_units, down_weight,
    ) = remote_call(
        enter_kernel,
        0,
        [
            shape((2, 128, D), BF16),
            shape((2, 128, 128), F32),
            shape((D, PADDED), BF16),
            shape((D, D), BF16),
            shape((256, HALF), BF16),
            shape((4, 4, 2, 128, 128), BF16),
            shape((4, 4, 2, 128, 128), BF16),
            shape((4, 2, 128, D), BF16),
            shape((HALF, 2 * PADDED), BF16),
            shape((224, 2 * PADDED), BF16),
            shape((224, 2 * PADDED), BF16),
            shape((PADDED, D), BF16),
        ],
        40,
        [
            pltpu.VMEM((2, HALF, 768), BF16),
            pltpu.VMEM((2, 224, 768), BF16),
            pltpu.VMEM((2, 224, 768), BF16),
            pltpu.VMEM((SLICE, D), BF16),
            pltpu.SemaphoreType.DMA((7,)),
        ],
        field, gain_attn, table, weight, bias, cot, row_pick, col_pick, w_o, w_gate, w_up, w_down,
        far=3,
    )

    to_up = permutation(lambda x, y, z, core: (x, y, (z + 1) % 4, core))
    to_down = permutation(lambda x, y, z, core: (x, y, (z + 3) % 4, core))
    u_late, u_early = lax.ppermute(up_units, BOTH, to_up), lax.ppermute(down_units, BOTH, to_down)

    kv_a, kv_b = kv_a.reshape(32, 128, 128), kv_b.reshape(32, 128, 128)
    natural = [pltpu.VMEM((8192, 128), BF16), pltpu.VMEM((8192 // CHUNK, 128, CHUNK), BF16)]
    out_t, lse, mixed = local_call(
        attend_kernel,
        [shape((4, 64, HALF), F32), shape((4, 1, HALF), F32), shape((256, HALF), BF16)],
        natural + [pltpu.VMEM((64, HALF), F32)],
        2,
        8 << 30,
        order, owned, kv_a, kv_b, queries,
    )

    def pair(dims, dtype=BF16, other=None):
        return [pltpu.VMEM((3,) + dims, dtype), pltpu.VMEM((3,) + (other or dims), dtype)]

    exchange = [pltpu.VMEM((4, 2, 128, D), BF16)] + [pltpu.VMEM((4, 128, D), BF16)] * 2 + pair((64, D))
    blocks = (
        [shape((4, 64, PADDED), BF16)] * 8
        + [shape((160, D), BF16)] * 4
        + [shape((4, 4, 16, HALF), BF16)] * 4
    )
    mixed_out, grad_hidden, branch_all, grad_gain_mlp, *parts = remote_call(
        feed_kernel,
        1,
        [shape((128, D), BF16), shape((128, D), F32), shape((2, 128, D), BF16), shape((1, D), F32)] + blocks,
        40,
        [
            pltpu.VMEM((2, 256, HALF), BF16),
            pltpu.VMEM((D, 2 * PADDED), BF16),
            pltpu.VMEM((128, D), F32),
            pltpu.VMEM((4, 2, 128, D), BF16),
            pltpu.VMEM((1024, 1024), BF16),
            pltpu.VMEM((PADDED, 1024), BF16),
            pltpu.VMEM((1024, PADDED), BF16),
            pltpu.VMEM((1024, PADDED), BF16),
            pltpu.VMEM((4, 4, 64, PADDED), BF16),
            pltpu.VMEM((4, 4, 4, 16, HALF), BF16),
        ]
        + exchange
        + exchange
        + [pltpu.VMEM((128, D), F32)],
        mixed, w_o_all, own_units, u_early, u_late, down_weight, cot_all, field, gain_mlp, owners, owners_half,
    )

    def moved(array, axis, step):
        def move(*place):
            at = list(place)
            at[axis] = (at[axis] + step) % 4
            return tuple(at)

        return lax.ppermute(array, BOTH, permutation(move))

    gathered = []
    for first, axis in ((0, 0), (4, 1), (8, 0), (12, 2)):
        gathered.append(parts[first])
        gathered += [moved(parts[first + step], axis, step) for step in (1, 2, 3)]

    grad_query, part_a, part_b = local_call(
        attend_back_kernel,
        [shape((256, HALF), F32), shape((32, 128, 128), BF16), shape((32, 128, 128), BF16)],
        natural + [pltpu.VMEM((8192, 128), F32), pltpu.VMEM((64, HALF), F32)],
        2,
        24 << 30,
        order, owned, kv_a, kv_b, queries, branch_all, w_o_all, out_t, lse,
    )

    def rows_of(columns):
        return [
            pltpu.VMEM((4, 4, 16, columns), BF16),
            pltpu.VMEM((15, 16, columns), BF16),
            pltpu.VMEM((2, 8, columns), F32),
            pltpu.VMEM((2, 8, columns), F32),
        ]

    wide = [pltpu.VMEM((4, 64, PADDED), BF16), pltpu.VMEM((3, 64, PADDED), BF16)]
    chips = (4, 4, 2, 128, 128)
    finals = [
        shape((128, D), F32),
        shape((7, D), F32),
        shape((7, 128), F32),
        shape((7, 128), F32),
        shape((7, D), F32),
        shape((7, FF), F32),
        shape((7, FF), F32),
        shape((38, D), F32),
        shape((1, 3072), F32),
    ]
    *results, vector = remote_call(
        finish_kernel,
        2,
        finals,
        130,
        [
            pltpu.VMEM((256, 128), F32),
            pltpu.VMEM((4, 2, 128, 128), BF16),
            pltpu.VMEM((4, 2, 128, 128), BF16),
            pltpu.VMEM((7, 128, 128), BF16),
            pltpu.VMEM((7, 128, 128), BF16),
            pltpu.VMEM((4, 4, 4, 16, 384), BF16),
            pltpu.VMEM((4, 4, 4, 16, 256), BF16),
            pltpu.VMEM((2, 128, D), F32),
            pltpu.VMEM((128, D), F32),
        ]
        + wide
        + wide
        + [pltpu.VMEM((4, 40, D), F32), pltpu.VMEM((4, 40, D), F32)]
        + [pltpu.VMEM((8, 8, 2 * PADDED), F32)] * 2
        + rows_of(HALF)
        + rows_of(384)
        + rows_of(256)
        + [pltpu.VMEM((5, 1, 3072), F32), pltpu.VMEM((10, 1, 3072), F32)]
        + pair((2, 2, 128, 128)) * 2
        + pair((2, 4, 16, 384))
        + pair((2, 4, 16, 256)),
        part_a.reshape(chips), part_b.reshape(chips), grad_query, table_all, weight_all, normed_all, owners,
        grad_hidden, field, gain_attn, grad_gain_mlp, col_pick, *gathered,
    )
    tidied = pl.pallas_call(
        tidy_kernel,
        out_shape=[shape((128, D), BF16)] + finals[:-1],
        in_specs=whole(len(finals)),
        out_specs=whole(len(finals)),
        compiler_params=pltpu.CompilerParams(vmem_limit_bytes=VMEM_LIMIT),
    )(mixed_out, *results)
    mixed_out, d_tokens, *grads = tidied
    sums = vector[0]
    return (
        mixed_out[None],
        d_tokens[None],
        *grads,
        sums[:D],
        sums[D : 2 * D],
        sums[2 * D : 3 * D],
        sums[3 * D : 3 * D + 128],
        sums[3 * D + 128 : 3 * D + 256],
    )


def solution(mesh):
    rows, flat = P("fsdp", None), P(("fsdp", "ctx"), None)
    field = P("fsdp", "ctx", None)
    return jax.shard_map(
        per_device,
        mesh=mesh,
        in_specs=(
            field, rows, P("fsdp", "ctx"), field, P(), rows, P(), rows, P(), rows, P(), rows, P(),
            rows, rows, rows,
        ),
        out_specs=(field, field) + (flat,) * 7 + (P(),) * 5,
        check_vma=False,
    )
```

```python
import functools

import jax
import jax.numpy as jnp
import numpy as np
from jax import lax
from jax.experimental import pallas as pl
from jax.experimental.pallas import tpu as pltpu
from jax.sharding import PartitionSpec as P

D = 896
H = 14
HD = 64
HALF = 448
FF = 4864
SLICE = 608
PADDED = 640
CHUNK = 512
EPSILON = 1e-06
THETA = 1000000.0
MASKED = -1e30
MESH = pl.DeviceIdType.MESH
F32 = jnp.float32
BF16 = jnp.bfloat16
VMEM_LIMIT = 56 * 1024 * 1024


def own_place():
    f, c = lax.axis_index("fsdp"), lax.axis_index("ctx")
    zh = lax.rem(lax.div(c, 2), 2)
    return (lax.div(c, 16), lax.rem(lax.div(c, 4), 4), zh * 2 + f, lax.rem(c, 2))


def device(place):
    x, y, z, core = place
    return (lax.rem(z, 2), (x * 4 + y) * 4 + 2 * lax.div(z, 2) + core)


def turned(value, step):
    return lax.rem(value + (step + 4), 4)


def shifted(place, axis, step):
    moved = list(place)
    moved[axis] = turned(place[axis], step)
    return tuple(moved)


def partner(place):
    return place[:3] + (1 - place[3],)


def greet(places):
    barrier = pltpu.get_barrier_semaphore()
    for place in places:
        pl.semaphore_signal(barrier, inc=1, device_id=device(place), device_id_type=MESH)
    pl.semaphore_wait(barrier, len(places))


class Links:
    def __init__(self, send, recv):
        self.send, self.recv, self.opened = send, recv, []

    def start(self, src, dst, place):
        at = len(self.opened)
        assert at < self.send.shape[0]
        copy = pltpu.make_async_remote_copy(
            src_ref=src,
            dst_ref=dst,
            send_sem=self.send.at[at],
            recv_sem=self.recv.at[at],
            device_id=device(place),
            device_id_type=MESH,
        )
        copy.start()
        self.opened.append(copy)
        return copy

    def close(self):
        for copy in self.opened:
            copy.wait_send()


def ring_gather(links, slot, half, place, axis):
    me = place[axis]
    right, left = shifted(place, axis, 1), shifted(place, axis, -1)
    first = links.start(slot(me), slot(me), right)
    second = links.start(slot(me), slot(me), left)
    yield
    before, after = turned(me, -1), turned(me, 1)
    first.wait_recv()
    third = links.start(half(before, 0), half(before, 0), right)
    yield
    second.wait_recv()
    fourth = links.start(half(after, 1), half(after, 1), left)
    yield
    third.wait_recv()
    fourth.wait_recv()


def ring_reduce(links, part, low, high, place, axis, emit):
    me = place[axis]
    right, left = shifted(place, axis, 1), shifted(place, axis, -1)
    before, after, far = turned(me, -1), turned(me, 1), turned(me, 2)
    first = links.start(part(far, 0), low.at[0], right)
    second = links.start(part(far, 1), high.at[0], left)
    yield
    third = links.start(part(after, 1), high.at[1], right)
    yield
    fourth = links.start(part(before, 0), low.at[1], left)
    yield
    first.wait_recv()
    low[0] = (low[0].astype(F32) + part(after, 0)[...].astype(F32)).astype(low.dtype)
    fifth = links.start(low.at[0], low.at[2], right)
    second.wait_recv()
    high[0] = (high[0].astype(F32) + part(before, 1)[...].astype(F32)).astype(high.dtype)
    sixth = links.start(high.at[0], high.at[2], left)
    yield
    fourth.wait_recv()
    fifth.wait_recv()
    emit(0, part(me, 0)[...].astype(F32) + low[1].astype(F32) + low[2].astype(F32))
    third.wait_recv()
    sixth.wait_recv()
    emit(1, part(me, 1)[...].astype(F32) + high[1].astype(F32) + high[2].astype(F32))


def direct_reduce(links, places, part, landing, own, emit):
    copies = [links.start(part(at), landing.at[i], at) for i, at in enumerate(places)]
    yield
    total = own[...].astype(F32)
    for i, copy in enumerate(copies):
        copy.wait_recv()
        total = total + landing[i].astype(F32)
    emit(total)


def around(place, steps):
    places = []
    for step in steps:
        at = place
        for axis, by in enumerate(step):
            if by:
                at = shifted(at, axis, by)
        places.append(at)
    return places


def in_turn(*streams):
    waiting = list(streams)
    while waiting:
        still = []
        for stream in waiting:
            try:
                next(stream)
            except StopIteration:
                continue
            still.append(stream)
        waiting = still


def local_norm(field, gain):
    inverse = lax.rsqrt(jnp.mean(field * field, axis=-1, keepdims=True) + EPSILON)
    return field * inverse * gain, inverse


def norm_backward(field, inverse, gain, grad):
    scaled = grad * gain
    grad_gain = jnp.sum(grad * field * inverse, axis=0, keepdims=True)
    mean = jnp.mean(scaled * field, axis=-1, keepdims=True)
    return inverse * scaled - field * (inverse * inverse * inverse) * mean, grad_gain


def dot(left, right, contract=((1,), (0,))):
    return lax.dot_general(left, right, (contract, ((), ())), preferred_element_type=F32)


def whole(count):
    return [pl.BlockSpec(memory_space=pltpu.VMEM)] * count


def shape(dims, dtype):
    return jax.ShapeDtypeStruct(dims, dtype)


def remote_call(kernel, collective_id, outs, copies, scratch, *args, far=0):
    return pl.pallas_call(
        kernel,
        out_shape=outs,
        in_specs=whole(len(args) - far) + [pl.BlockSpec(memory_space=pl.ANY)] * far,
        out_specs=whole(len(outs)),
        scratch_shapes=list(scratch)
        + [pltpu.SemaphoreType.DMA((copies,)), pltpu.SemaphoreType.DMA((copies,))],
        compiler_params=pltpu.CompilerParams(
            collective_id=collective_id, has_side_effects=True, vmem_limit_bytes=VMEM_LIMIT
        ),
    )(*args)


KV_A_STEPS = [(0, dy, dz) for dz in (0, 2) for dy in (0, 1, -1, 2) if dy or dz]
KV_B_STEPS = [(dx, 0, dz) for dz in (0, 2) for dx in (0, 1, -1, 2) if dx or dz]


def enter_kernel(
    tokens, gain, table, w_q, w_k, w_v, bias, cot, row_pick, col_pick, w_o, w_gate, w_up, w_down,
    normed_all, table_all, weight_all, w_o_all, queries, kv_a, kv_b, cot_all, own_units, up_units, down_units, down_rows,
    weight, own_window, up_window, down_window, tall_window, fetched, send, recv,
):
    place = own_place()
    x, y, z, core = place
    f, zh = lax.rem(z, 2), lax.div(z, 2)
    other, up, down, far = partner(place), shifted(place, 2, 1), shifted(place, 2, -1), shifted(place, 2, 2)
    fetches = []

    def fetch(src, dst):
        copy = pltpu.make_async_copy(src, dst, fetched.at[len(fetches)])
        copy.start()
        fetches.append(copy)

    def offset(at):
        part = 4 * lax.rem(at[2], 2) + 2 * lax.div(at[2], 2) + at[3]
        start = jnp.minimum(lax.div(19 * part, 4), 32) * 128
        return start, SLICE * part - start

    windows = ((own_window, place, 0, HALF), (up_window, up, 224, 224), (down_window, down, 0, 224))
    for window, at, row, rows in windows:
        columns = pl.ds(pl.multiple_of(offset(at)[0], 128), 768)
        for which, array in enumerate((w_gate, w_up)):
            fetch(array.at[pl.ds(row, rows), columns], window.at[which])
    sub = 2 * zh + core
    fetch(w_down.at[pl.ds(pl.multiple_of(sub * SLICE, 16), SLICE)], tall_window)
    a_peers = around(place, KV_A_STEPS)
    b_peers = around(place, KV_B_STEPS)
    greet([other, up, down, far] + [at for at in a_peers + b_peers if at is not far])
    links = Links(send, recv)
    base = pl.multiple_of(f * HALF, HALF)

    def core_half(array):
        half = array.shape[1] // 2
        wide = array[...].astype(F32)
        return jnp.where(core == 0, wide[:, :half], wide[:, half:])

    weight[...] = jnp.concatenate(
        [core_half(w_q), core_half(w_k), core_half(w_v), jnp.zeros((HALF, 64), F32)], axis=1
    ).astype(BF16)
    w_down_copy = links.start(weight.at[pl.ds(0, 224)], weight_all.at[pl.ds(base, 224)], down)
    w_up_copy = links.start(weight.at[pl.ds(224, 224)], weight_all.at[pl.ds(base + 224, 224)], up)
    normed, _ = local_norm(tokens[...].astype(F32), gain[...])
    normed_all[core] = normed.astype(BF16)
    n_copy = links.start(normed_all.at[core], normed_all.at[core], other)
    table_all[core] = table[...]
    t_copy = links.start(table_all.at[core], table_all.at[core], other)
    cot_all[z, core] = cot[...]
    c_copy = links.start(cot_all.at[z, core], cot_all.at[z, core], other)
    weight_all[pl.ds(base, HALF)] = weight[...]
    for copy in fetches:
        copy.wait()
    for (window, at, _, rows), out in zip(windows, (own_units, up_units, down_units)):
        line = lax.broadcasted_iota(jnp.int32, (768, PADDED), 0) - offset(at)[1]
        pick = (line == row_pick[...]).astype(F32).astype(BF16)
        for which in range(2):
            out[:, PADDED * which : PADDED * (which + 1)] = dot(window[which], pick).astype(BF16)
    line = lax.broadcasted_iota(jnp.int32, (PADDED, SLICE), 1)
    pick = (line == col_pick[...]).astype(F32).astype(BF16)
    down_rows[...] = dot(pick, tall_window[...]).astype(BF16)
    n_copy.wait_recv()
    t_copy.wait_recv()
    w_down_copy.wait_recv()
    w_up_copy.wait_recv()
    lin = dot(normed_all[...].reshape(256, D), weight_all[...]) + bias[...]
    turn = lin[:, :512]
    lane = lax.broadcasted_iota(jnp.int32, (256, 512), 1)
    swapped = jnp.where(lax.rem(lane, 64) < 32, -pltpu.roll(turn, 480, 1), pltpu.roll(turn, 32, 1))
    both = table_all[...].reshape(256, 128)
    cosine = jnp.concatenate([both[:, :64]] * 8, axis=1)
    sine = jnp.concatenate([both[:, 64:]] * 8, axis=1)
    rotated = turn * cosine + swapped * sine
    kv = jnp.concatenate([rotated[:, HALF:512], lin[:, 512:576]], axis=1).astype(BF16)
    kv_a[x, y, zh] = kv[:128]
    kv_b[x, y, zh] = kv[128:]
    a_copies = [links.start(kv_a.at[x, y, zh], kv_a.at[x, y, zh], at) for at in a_peers]
    b_copies = [links.start(kv_b.at[x, y, zh], kv_b.at[x, y, zh], at) for at in b_peers]
    w_o_all[pl.ds(base, HALF)] = w_o[...]
    queries[...] = (rotated[:, :HALF] * HD**-0.5).astype(BF16)

    def stream_a():
        for copy in a_copies:
            copy.wait_recv()
        yield from ring_gather(
            links, lambda k: kv_a.at[k], lambda k, h: kv_a.at[k, pl.ds(2 * h, 2)], place, 0
        )

    def stream_b():
        for copy in b_copies:
            copy.wait_recv()
        yield from ring_gather(
            links,
            lambda k: kv_b.at[pl.ds(0, 4), k],
            lambda k, h: kv_b.at[pl.ds(2 * h, 2), k],
            place,
            1,
        )

    def stream_o():
        down_copy = links.start(w_o.at[pl.ds(0, 224)], w_o_all.at[pl.ds(base, 224)], down)
        up_copy = links.start(w_o.at[pl.ds(224, 224)], w_o_all.at[pl.ds(base + 224, 224)], up)
        for _ in range(6):
            yield
        down_copy.wait_recv()
        up_copy.wait_recv()

    in_turn(stream_a(), stream_b(), shared_gather(links, cot_all, place, c_copy), stream_o())
    links.close()


def shared_gather(links, blocks, place, own_copy):
    z, core = place[2], place[3]
    other = partner(place)
    copies = [own_copy]
    ring = ring_gather(
        links,
        lambda k: blocks.at[k, core],
        lambda k, h: blocks.at[k, core, pl.ds(64 * h, 64)],
        place,
        2,
    )
    next(ring)
    yield
    next(ring)
    before = turned(z, -1)
    copies.append(links.start(blocks.at[before, core], blocks.at[before, core], other))
    yield
    next(ring)
    after = turned(z, 1)
    copies.append(links.start(blocks.at[after, core], blocks.at[after, core], other))
    yield
    for _ in ring:
        yield
    last = turned(z, 2)
    copies.append(links.start(blocks.at[last, core], blocks.at[last, core], other))
    yield
    for copy in copies:
        copy.wait_recv()


def down_group(place):
    x, y, z, core = place
    sub = 2 * lax.div(z, 2) + core
    return lax.rem(x + 5 - sub, 4), lax.rem(y + sub, 4)


def feed_kernel(
    mixed, w_o, u_own, u_early, u_late, w_down, cot_all, tokens, gain, owners, owners_half,
    mixed_out, grad_hidden, branch_all, grad_gain, gate_mid, up_mid, down_mid, part_o, *rest,
):
    (
        mixed_all, w_units, hidden, normed_all, spread_t, inner_t, grad_gates, grad_ups, up_all, along_x,
        x_low, x_high, y_low, y_high,
        out_part, out_arrived, out_paired, out_low, out_high,
        grad_part, grad_arrived, grad_paired, grad_low, grad_high, grad_sum, send, recv,
    ) = rest
    place = own_place()
    x, y, z, core = place
    f = lax.rem(z, 2)
    other = partner(place)
    greet([other] + [shifted(place, axis, step) for axis in (0, 1, 2) for step in (1, -1)])
    links = Links(send, recv)
    copy = links.start(mixed, mixed_all.at[core], other)
    mixed_all[core] = mixed[...]
    own_base = pl.multiple_of(f * HALF, HALF)
    base = pl.multiple_of((1 - f) * HALF, HALF)
    copy.wait_recv()
    rows = pl.ds(pl.multiple_of(core * 128, 128), 128)
    field = tokens[...].astype(F32) + (
        dot(mixed_all[0, rows], w_o[:HALF]) + dot(mixed_all[1, rows], w_o[HALF:])
    )
    hidden[...] = field
    normed, _ = local_norm(field, gain[...])
    normed_all[z, core] = normed.astype(BF16)
    own = links.start(normed_all.at[z, core], normed_all.at[z, core], other)

    def assemble():
        w_units[pl.ds(own_base, HALF)] = u_own[...]
        yield
        w_units[pl.ds(base, 224)] = u_early[...]
        w_units[pl.ds(base + 224, 224)] = u_late[...]

    in_turn(shared_gather(links, normed_all, place, own), assemble())

    before, after, far = turned(z, -1), turned(z, 1), turned(z, 2)
    both = (
        (out_part, out_arrived, out_paired), (grad_part, grad_arrived, grad_paired),
    )

    def tile(k):
        n = normed_all[k].reshape(256, D)
        c = cot_all[k].reshape(256, D)
        g = dot(n, w_units[:, :PADDED])
        u = dot(n, w_units[:, PADDED:])
        s = 1.0 / (1.0 + jnp.exp(-g))
        silu = g * s
        inner = silu * u
        low = inner.astype(BF16)
        out_part[k] = dot(low, w_down[...]).astype(BF16).reshape(2, 128, D)
        columns = pl.ds(pl.multiple_of(k * 256, 256), 256)
        inner_t[:, columns] = low.T
        gi = dot(c, w_down[...], ((1,), (1,)))
        gg = (gi * u * s * (1.0 + g * (1.0 - s))).astype(BF16)
        gu = (gi * silu).astype(BF16)
        grad_gates[columns] = gg
        grad_ups[columns] = gu
        grad_part[k] = (
            dot(gg, w_units[:, :PADDED], ((1,), (1,))) + dot(gu, w_units[:, PADDED:], ((1,), (1,)))
        ).astype(BF16).reshape(2, 128, D)
        return [links.start(part.at[k, 1 - core], come.at[k], other) for part, come, _ in both]

    def pair_up(k, copies):
        for trip, (part, come, paired) in zip(copies, both):
            trip.wait_recv()
            paired[k] = (come[k].astype(F32) + part[k, core].astype(F32)).astype(BF16)

    def emit_out(h, value):
        at = pl.ds(64 * h, 64)
        mixed_out[at] = (hidden[at] + value).astype(BF16)

    def emit_grad(h, value):
        grad_sum[pl.ds(64 * h, 64)] = value

    reduces = [
        ring_reduce(
            links, lambda k, h, p=paired: p.at[k, pl.ds(64 * h, 64)], low, high, place, 2, emit
        )
        for paired, low, high, emit in (
            (grad_paired, grad_low, grad_high, emit_grad),
            (out_paired, out_low, out_high, emit_out),
        )
    ]

    def advance():
        for stream in reduces:
            next(stream, None)

    trips = tile(far)
    pair_up(far, trips)
    advance()
    trips = tile(after)
    pair_up(after, trips)
    advance()
    trips = tile(before)
    pair_up(before, trips)
    advance()
    trips = tile(z)
    advance()
    pair_up(z, trips)

    advance()

    @pl.loop(0, 4)
    def _(k):
        columns = pl.ds(pl.multiple_of(k * 256, 256), 256)
        spread_t[:, columns] = dot(
            owners[...], normed_all[k].reshape(256, D), ((1,), (1,))
        ).astype(BF16)

    @pl.loop(0, 4)
    def _(k):
        lines = spread_t[pl.ds(pl.multiple_of(k * 256, 256), 256)]
        along_x[k, :256] = dot(lines, grad_gates[...]).astype(BF16)
        group, _ = down_group((k, y, z, core))
        lines = inner_t[pl.ds(pl.multiple_of(group * 160, 16), 160)]
        tall = dot(lines, cot_all[...].reshape(1024, D)).astype(BF16)
        along_x[k, 256:416] = tall[:, :PADDED]
        along_x[k, 416:496, :256] = tall[:80, PADDED:]
        along_x[k, 416:496, 256:512] = tall[80:, PADDED:]
        along_x[k, 416:496, 512:] = jnp.zeros((80, 128), BF16)

    def put_x(h, value):
        if h == 0:
            gate_mid[...] = value.astype(BF16).reshape(4, 64, PADDED)
            return
        for k in range(4):
            row, lane = 160 + 40 * (k % 2), 256 * (k // 2)
            down_mid[k, :40, :PADDED] = value[40 * k : 40 * (k + 1)].astype(BF16)
            down_mid[k, :40, PADDED:] = value[row : row + 40, lane : lane + 256].astype(BF16)
            down_mid[k, 40:] = jnp.zeros((8, D), BF16)

    def put_y(h, value):
        up_mid[pl.ds(2 * h, 2)] = value.astype(BF16)

    stream_x = ring_reduce(
        links, lambda k, h: along_x.at[k, pl.ds(256 * h, 256 - 16 * h)], x_low, x_high, place, 0, put_x
    )
    stream_y = ring_reduce(
        links, lambda k, h: up_all.at[pl.ds(2 * h, 2), k], y_low, y_high, place, 1, put_y
    )
    for _ in range(3):
        next(stream_x)
    advance()

    @pl.loop(0, 4)
    def _(k):
        lines = spread_t[pl.ds(pl.multiple_of(k * 256, 256), 256)]
        up_all[k] = dot(lines, grad_ups[...]).astype(BF16).reshape(4, 64, PADDED)

    for _ in range(3):
        next(stream_y)
    spread_o = (
        dot(owners_half[0], mixed_all[0], ((1,), (1,))) + dot(owners_half[1], mixed_all[1], ((1,), (1,)))
    ).astype(BF16)
    for _ in range(8):
        advance()
    field = hidden[...]
    _, inverse = local_norm(field, gain[...])
    through, gains = norm_backward(field, inverse, gain[...], grad_sum[...])
    grad_gain[...] = gains
    total = cot_all[z, core].astype(F32) + through
    grad_hidden[...] = total
    branch_all[core] = total.astype(BF16)
    trip = links.start(branch_all.at[core], branch_all.at[core], other)
    next(stream_x)
    next(stream_y)
    trip.wait_recv()
    branch = branch_all[...].reshape(256, D).astype(F32)
    half = jnp.where(core == 0, branch[:, :HALF], branch[:, HALF:]).astype(BF16)
    part_o[...] = dot(spread_o, half).astype(BF16).reshape(4, 4, 4, 16, HALF)
    in_turn(stream_y, stream_x)
    links.close()


def finish_kernel(
    kv_part_a, kv_part_b, grad_query, table_all, weight_all, normed_all, owners, grad_hidden, tokens, gain,
    gain_mlp_grad, col_pick, gate_mid, up_mid, down_mid, part_o, *rest,
):
    (
        d_tokens, wq_out, wk_out, wv_out, wo_out, gate_out, up_out, down_out, vector_out,
        grad_kv, kv_mid_a, kv_mid_b, kv_land_a, kv_land_b, part_qa, part_qb, grad_normed, half_sum,
        gate_land, up_land, down_land, down_end, down_own, end, rows_all,
        o_first, o_mid, o_land, o_end, o_rows, qa_mid, qa_land, qa_end, qa_rows, qb_mid, qb_land, qb_end, qb_rows,
        vec_now, vec_in,
        a_low, a_high, b_low, b_high, qa_low, qa_high, qb_low, qb_high, send, recv,
    ) = rest
    place = own_place()
    x, y, z, core = place
    f, zh = lax.rem(z, 2), lax.div(z, 2)
    sub = 2 * zh + core
    other = partner(place)
    mine = z * 2 + core
    x_peers, y_peers = around(place, X_STEPS), around(place, Y_STEPS)
    xy_peers, xz_peers, yz_peers = (
        around(place, steps) for steps in (XY_STEPS, XZ_STEPS, YZ_STEPS)
    )
    z_peers = around(place, Z_STEPS)
    ring = []
    for step in range(1, 8):
        at = lax.rem(mine + step, 8)
        ring.append((x, y, lax.div(at, 2), lax.rem(at, 2)))
    first, second = down_group(place)
    to_owner = (sub, first, 2 * lax.div(second, 2) + f, lax.rem(second, 2))
    from_group = (lax.rem(x + y + 3, 4), lax.rem(sub + 4 - x, 4), 2 * lax.div(x, 2) + f, lax.rem(x, 2))
    greet(ring + xy_peers + xz_peers[3:] + yz_peers[3:] + [to_owner, from_group])
    links = Links(send, recv)

    def kv_stream(part, mid, landing, order, low, high, peers, base):
        def put_mid(h, value):
            mid[pl.ds(2 * h, 2)] = value.astype(BF16)

        def put_end(value):
            grad_kv[pl.ds(base, 128)] = value

        if order == 0:
            first = lambda k, h: part.at[k, pl.ds(2 * h, 2)]
        else:
            first = lambda k, h: part.at[pl.ds(2 * h, 2), k]
        yield from ring_reduce(links, first, low, high, place, order, put_mid)
        keep = 1 - order
        yield from direct_reduce(
            links, peers, lambda at: mid.at[at[keep], lax.div(at[2], 2)], landing,
            mid.at[place[keep], zh], put_end,
        )

    def to_rows(end, rows):
        last = links.start(end.at[1 - core], rows.at[core], other)
        rows[core] = end[core]
        yield
        last.wait_recv()

    def q_stream(part, mid, landing, end, rows, order, low, high, peers):
        def put_mid(h, value):
            mid[pl.ds(2 * h, 2)] = value.astype(BF16)

        def put_end(value):
            end[0], end[1] = value[:8], value[8:]

        if order == 0:
            first = lambda k, h: part.at[k, pl.ds(2 * h, 2)]
        else:
            first = lambda k, h: part.at[pl.ds(2 * h, 2), k]
        yield from ring_reduce(links, first, low, high, place, order, put_mid)
        keep = 1 - order
        yield from direct_reduce(
            links, peers, lambda at: mid.at[at[keep], at[2]], landing, mid.at[place[keep], z], put_end
        )
        yield from to_rows(end, rows)

    def o_stream():
        def put_end(value):
            o_end[0], o_end[1] = value[:8], value[8:]

        def put_mid(value):
            o_mid[...] = value.astype(BF16)

        def part(at):
            return part_o.at[pl.ds(0, 4), pl.ds(0, 4), at[2]]

        yield from direct_reduce(links, z_peers, part, o_first, part(place), put_mid)
        yield from direct_reduce(
            links, xy_peers, lambda at: o_mid.at[at[0], at[1]], o_land, o_mid.at[x, y], put_end
        )
        yield from to_rows(o_end, o_rows)

    def wide(mid, landing, axis, peers, column):
        def put_end(value):
            end[:, :, pl.ds(column, PADDED)] = value.reshape(8, 8, PADDED)

        yield from direct_reduce(
            links, peers, lambda at: mid.at[at[axis]], landing, mid.at[place[axis]], put_end
        )

    def tall():
        def put_end(value):
            down_end[...] = value[:40]

        yield from direct_reduce(
            links, y_peers, lambda at: down_mid.at[down_group(at)[1]], down_land, down_mid.at[second], put_end
        )
        copy = links.start(down_end, down_own, to_owner)
        yield
        copy.wait_recv()
        down_out[...] = down_own[:38]

    def hidden_units():
        gates = wide(gate_mid, gate_land, 1, y_peers, 0)
        ups = wide(up_mid, up_land, 0, x_peers, PADDED)
        next(gates)
        next(ups)
        yield
        for stream in (gates, ups):
            for _ in stream:
                pass
        copies = [
            links.start(end.at[to[2] * 2 + to[3]], rows_all.at[mine], to) for to in ring
        ]
        rows_all[mine] = end[mine]
        yield
        line = lax.broadcasted_iota(jnp.int32, (PADDED, SLICE), 1)
        pick = (line == col_pick[...]).astype(F32).astype(BF16)
        for copy in copies:
            copy.wait_recv()
        for which, out in enumerate((gate_out, up_out)):
            values = rows_all[:, :, PADDED * which : PADDED * (which + 1)].reshape(64, PADDED)
            top = values.astype(BF16)
            below = (values - top.astype(F32)).astype(BF16)
            units = dot(top, pick) + dot(below, pick)
            for at in range(8):
                part = 4 * (at // 2 % 2) + 2 * (at // 4) + at % 2
                out[:, SLICE * part : SLICE * (part + 1)] = units[8 * at : 8 * at + 7]

    kv_streams = [
        kv_stream(kv_part_a, kv_mid_a, kv_land_a, 0, a_low, a_high, yz_kv(place), 0),
        kv_stream(kv_part_b, kv_mid_b, kv_land_b, 1, b_low, b_high, xz_kv(place), 128),
    ]
    units, talls, os = hidden_units(), tall(), o_stream()
    for _ in range(3):
        for stream in kv_streams:
            next(stream)
    next(os)
    spread_n = dot(owners[...], normed_all[...].reshape(256, D), ((1,), (1,))).astype(BF16)
    for stream in kv_streams:
        next(stream)
    in_turn(*kv_streams)

    table = table_all[...].reshape(256, 128)
    cosine = jnp.concatenate([table[:, :64]] * 8, axis=1)
    sine = jnp.concatenate([table[:, 64:]] * 8, axis=1)
    turn = jnp.concatenate([grad_query[...] * HD**-0.5, grad_kv[:, :64]], axis=1)
    scaled = turn * sine
    lane = lax.broadcasted_iota(jnp.int32, (256, 512), 1)
    swapped = jnp.where(
        lax.rem(lane, 64) < 32, pltpu.roll(scaled, 480, 1), -pltpu.roll(scaled, 32, 1)
    )
    lin = jnp.concatenate(
        [turn * cosine + swapped, grad_kv[:, 64:], jnp.zeros((256, 64), F32)], axis=1
    ).astype(BF16)
    part = dot(spread_n, lin).astype(BF16)
    part_qa[...] = part[:, :384].reshape(4, 4, 4, 16, 384)
    part_qb[...] = part[:, 384:].reshape(4, 4, 4, 16, 256)
    q_streams = [
        q_stream(part_qa, qa_mid, qa_land, qa_end, qa_rows, 0, qa_low, qa_high, yz_peers),
        q_stream(part_qb, qb_mid, qb_land, qb_end, qb_rows, 1, qb_low, qb_high, xz_peers),
    ]
    for _ in range(3):
        for stream in q_streams:
            next(stream)

    next(units)
    next(talls)

    def sums():
        grad_normed[...] = dot(lin, weight_all[...], ((1,), (1,))).reshape(2, 128, D)
        copy = links.start(grad_normed.at[1 - core], half_sum, other)
        column = jnp.sum(lin.astype(F32), axis=0, keepdims=True)

        def placed(values):
            empty = jnp.zeros_like(values)
            return jnp.where(
                core == 0,
                jnp.concatenate([values, empty], axis=1),
                jnp.concatenate([empty, values], axis=1),
            )

        biases = [placed(column[:, low:high]) for low, high in ((0, HALF), (HALF, 512), (512, 576))]
        copy.wait_recv()
        grad = grad_normed[core] + half_sum[...]
        field = tokens[...].astype(F32)
        _, inverse = local_norm(field, gain[...])
        through, gains = norm_backward(field, inverse, gain[...], grad)
        d_tokens[...] = grad_hidden[...] + through
        vec_now[0] = jnp.concatenate(
            [gains, gain_mlp_grad[...], *biases, jnp.zeros((1, 128), F32)], axis=1
        )
        trip = links.start(vec_now.at[0], vec_in.at[0], other)
        trip.wait_recv()
        vec_now[1] = vec_now[0] + vec_in[0]
        for stage, axis in enumerate((2, 1, 0)):
            trips = [
                links.start(
                    vec_now.at[1 + stage],
                    vec_in.at[1 + 3 * stage + at],
                    shifted(place, axis, step),
                )
                for at, step in enumerate((1, -1, 2))
            ]
            yield
            for trip in trips:
                trip.wait_recv()
            at = 1 + 3 * stage
            near = vec_in[at] + vec_in[at + 1]
            vec_now[2 + stage] = (vec_now[1 + stage] + vec_in[at + 2]) + near
        vector_out[...] = vec_now[4]

    in_turn(sums(), *q_streams, os, units, talls)

    def row_of(core_at):
        return jnp.concatenate([qa_rows[core_at], qb_rows[core_at]], axis=1)[:7]

    first, second = row_of(0), row_of(1)
    for out, low, high in ((wq_out, 0, HALF), (wk_out, HALF, 512), (wv_out, 512, 576)):
        out[...] = jnp.concatenate([first[:, low:high], second[:, low:high]], axis=1)
    wo_out[...] = jnp.concatenate([o_rows[0][:7], o_rows[1][:7]], axis=1)
    links.close()


AROUND = (0, 1, -1, 2)
X_STEPS = [(d, 0, 0) for d in AROUND[1:]]
Y_STEPS = [(0, d, 0) for d in AROUND[1:]]
Z_STEPS = [(0, 0, d) for d in AROUND[1:]]
XY_STEPS = [(dx, dy, 0) for dy in AROUND for dx in AROUND if dx or dy]
XZ_STEPS = [(dx, 0, dz) for dz in AROUND for dx in AROUND if dx or dz]
YZ_STEPS = [(0, dy, dz) for dz in AROUND for dy in AROUND if dy or dz]


def yz_kv(place):
    return around(place, KV_A_STEPS)


def xz_kv(place):
    return around(place, KV_B_STEPS)


def tidy_kernel(*refs):
    half = len(refs) // 2
    for src, dst in zip(refs[:half], refs[half:]):
        dst[...] = src[...]


def natural_order(order, kv_a, kv_b, kv, kv_t):
    @pl.loop(0, 32)
    def _(chip):
        for t in range(4):
            block = kv_a[chip, pl.ds(64 * t, 64)] if t < 2 else kv_b[chip, pl.ds(64 * (t - 2), 64)]
            at = pl.multiple_of(order[4 * chip + t] * 64, 64)
            kv[pl.ds(at, 64)] = block

    @pl.loop(0, 8192 // CHUNK)
    def _(c):
        kv_t[c] = kv[pl.ds(pl.multiple_of(c * CHUNK, CHUNK), CHUNK)].T


def allowed_at(c, base):
    key = c * CHUNK + lax.broadcasted_iota(jnp.int32, (CHUNK, HALF), 0)
    lane = lax.broadcasted_iota(jnp.int32, (CHUNK, HALF), 1)
    return key <= base + lax.rem(lane, 64)


def by_head(rows):
    return jnp.concatenate([rows[:, 64 * h : 64 * (h + 1)] for h in range(7)], axis=0)


def side_by_side(columns_t):
    stacked = columns_t.T
    return jnp.concatenate([stacked[64 * h : 64 * (h + 1)] for h in range(7)], axis=1)


def attend_kernel(order, owned, kv_a, kv_b, queries, out_t, lse, mixed, kv, kv_t, acc):
    natural_order(order, kv_a, kv_b, kv, kv_t)
    none = jnp.zeros((64, HALF), F32)
    for t in range(4):
        spot = owned[t]
        rows = by_head(queries[64 * t : 64 * (t + 1)].astype(F32))
        q_t = jnp.concatenate([rows.T, none], axis=0).astype(BF16)
        last = lax.div(spot * 64, CHUNK)
        acc[...] = jnp.zeros_like(acc)

        def step(c, carry, masked):
            top, total = carry
            scores = dot(kv[pl.ds(pl.multiple_of(c * CHUNK, CHUNK), CHUNK)], q_t)
            if masked:
                scores = jnp.where(allowed_at(c, spot * 64), scores, MASKED)
            new_top = jnp.maximum(top, jnp.max(scores, axis=0, keepdims=True))
            probs = jnp.exp(scores - new_top)
            scale = jnp.exp(top - new_top)
            total = total * scale + jnp.sum(probs, axis=0, keepdims=True)
            acc[...] = acc[...] * scale + dot(kv_t[c, pl.ds(64, 64)], probs.astype(BF16))
            return new_top, total

        start = (jnp.full((1, HALF), MASKED, F32), jnp.zeros((1, HALF), F32))
        carry = lax.fori_loop(0, last, lambda c, carry: step(c, carry, False), start)
        top, total = step(last, carry, True)
        result = acc[...] / total
        out_t[t] = result
        mixed[64 * t : 64 * (t + 1)] = side_by_side(result).astype(BF16)
        lse[t] = top + jnp.log(total)


def attend_back_kernel(
    order, owned, kv_a, kv_b, queries, branch, w_o, out_t, lse,
    grad_query, grad_a, grad_b, kv, kv_t, acc, acc_q,
):
    natural_order(order, kv_a, kv_b, kv, kv_t)
    acc[...] = jnp.zeros_like(acc)
    grad_mixed = dot(
        branch[...].reshape(256, D), w_o[pl.ds(pl.multiple_of(owned[4] * HALF, HALF), HALF)], ((1,), (1,))
    )
    none_t, none = jnp.zeros((64, HALF), F32), jnp.zeros((HALF, 64), F32)
    for t in range(4):
        spot = owned[t]
        last = lax.div(spot * 64, CHUNK)
        rows = by_head(queries[64 * t : 64 * (t + 1)].astype(F32))
        q = jnp.concatenate([rows, none], axis=1).astype(BF16)
        q_t = jnp.concatenate([rows.T, none_t], axis=0).astype(BF16)
        rows = by_head(grad_mixed[64 * t : 64 * (t + 1)].astype(BF16).astype(F32))
        g = jnp.concatenate([none, rows], axis=1).astype(BF16)
        rows_t = rows.T
        g_t = jnp.concatenate([none_t, rows_t], axis=0).astype(BF16)
        delta = jnp.sum(rows_t * out_t[t], axis=0, keepdims=True)
        norm = lse[t]
        acc_q[...] = jnp.zeros_like(acc_q)

        def step(c, masked):
            rows = pl.ds(pl.multiple_of(c * CHUNK, CHUNK), CHUNK)
            block = kv[rows]
            scores = dot(block, q_t)
            if masked:
                scores = jnp.where(allowed_at(c, spot * 64), scores, MASKED)
            probs = jnp.exp(scores - norm)
            grad_probs = dot(block, g_t)
            grad_scores = (probs * (grad_probs - delta)).astype(BF16)
            acc[rows] += dot(probs.astype(BF16), g) + dot(grad_scores, q)
            acc_q[...] += dot(kv_t[c, pl.ds(0, 64)], grad_scores)

        def body(c, carry):
            step(c, False)
            return carry

        lax.fori_loop(0, last, body, 0)
        step(last, True)
        grad_query[64 * t : 64 * (t + 1)] = side_by_side(acc_q[...])

    @pl.loop(0, 32)
    def _(chip):
        for t in range(4):
            at = pl.multiple_of(order[4 * chip + t] * 64, 64)
            block = acc[pl.ds(at, 64)].astype(BF16)
            if t < 2:
                grad_a[chip, pl.ds(64 * t, 64)] = block
            else:
                grad_b[chip, pl.ds(64 * (t - 2), 64)] = block


def local_call(kernel, outs, scratch, scalars, flops, *args):
    return pl.pallas_call(
        kernel,
        out_shape=outs,
        in_specs=[pl.BlockSpec(memory_space=pltpu.SMEM)] * scalars + whole(len(args) - scalars),
        out_specs=[pl.BlockSpec(memory_space=pltpu.VMEM)] * len(outs),
        scratch_shapes=scratch,
        compiler_params=pltpu.CompilerParams(vmem_limit_bytes=VMEM_LIMIT),
        cost_estimate=pl.CostEstimate(flops=flops, bytes_accessed=8 << 20, transcendentals=1 << 23),
    )(*args)


def padded_columns():
    col = np.arange(PADDED)
    return np.where(col % 40 < 38, col // 40 * 38 + col % 40, -(1 << 20)).astype(np.int32)


def owner_rows():
    row = np.arange(1024)
    i, core, z, y, x = row % 8, row // 8 % 2, row // 16 % 4, row // 64 % 4, row // 256
    at = 7 * (64 * (z % 2) + 16 * x + 4 * y + 2 * (z // 2) + core) + i
    pick = np.zeros((1024, D), np.float32)
    keep = i < 7
    pick[row[keep], at[keep]] = 1.0
    return pick


def index_of(x, y, z, core):
    return (z % 2) * 64 + (x * 4 + y) * 4 + 2 * (z // 2) + core


def permutation(move):
    pairs = []
    for x in range(4):
        for y in range(4):
            for z in range(4):
                for core in range(2):
                    pairs.append((index_of(x, y, z, core), index_of(*move(x, y, z, core))))
    return pairs


BOTH = ("fsdp", "ctx")


def per_device(
    tokens, block_index, positions, cotangent, norm_attn, w_q, b_q, w_k, b_k, w_v, b_v, w_o,
    norm_mlp, w_gate, w_up, w_down,
):
    f, c = lax.axis_index("fsdp"), lax.axis_index("ctx")
    core, zh = c % 2, (c // 2) % 2
    z = 2 * zh + f
    sub = 2 * zh + core
    field, cot = tokens[0], cotangent[0]
    order = block_index[0]
    owned = lax.dynamic_slice_in_dim(order, 4 * (c // 2), 4, 0)
    owned = jnp.concatenate([owned, core[None]])
    gain_attn = norm_attn.astype(F32)[None]
    gain_mlp = norm_mlp.astype(F32)[None]

    freq = THETA ** (-(jnp.arange(HD // 2, dtype=F32) * 2.0 / HD))
    angle = positions[0].astype(F32)[:, None] * freq[None, :]
    cosine, sine = jnp.cos(angle), jnp.sin(angle)
    table = jnp.concatenate([cosine, cosine, sine, sine], -1)

    def core_columns(array):
        half = array.shape[-1] // 2
        return jnp.where(core == 0, array[..., :half], array[..., half:])

    bias = jnp.concatenate(
        [core_columns(b_q), core_columns(b_k), core_columns(b_v), jnp.zeros((64,), BF16)], axis=0
    ).astype(F32)[None]

    picked = padded_columns()
    row_pick, col_pick = jnp.asarray(picked[None]), jnp.asarray(picked[:, None])
    owners = owner_rows()
    owners_half = jnp.asarray(np.stack([owners[:, :HALF], owners[:, HALF:]]), BF16)
    owners = jnp.asarray(owners, BF16)

    (
        normed_all, table_all, weight_all, w_o_all, queries, kv_a, kv_b, cot_all,
        own_units, up_units, down_units, down_weight,
    ) = remote_call(
        enter_kernel,
        0,
        [
            shape((2, 128, D), BF16),
            shape((2, 128, 128), F32),
            shape((D, PADDED), BF16),
            shape((D, D), BF16),
            shape((256, HALF), BF16),
            shape((4, 4, 2, 128, 128), BF16),
            shape((4, 4, 2, 128, 128), BF16),
            shape((4, 2, 128, D), BF16),
            shape((HALF, 2 * PADDED), BF16),
            shape((224, 2 * PADDED), BF16),
            shape((224, 2 * PADDED), BF16),
            shape((PADDED, D), BF16),
        ],
        40,
        [
            pltpu.VMEM((HALF, PADDED), BF16),
            pltpu.VMEM((2, HALF, 768), BF16),
            pltpu.VMEM((2, 224, 768), BF16),
            pltpu.VMEM((2, 224, 768), BF16),
            pltpu.VMEM((SLICE, D), BF16),
            pltpu.SemaphoreType.DMA((7,)),
        ],
        field, gain_attn, table, w_q, w_k, w_v, bias, cot, row_pick, col_pick, w_o, w_gate, w_up, w_down,
        far=3,
    )

    to_up = permutation(lambda x, y, z, core: (x, y, (z + 1) % 4, core))
    to_down = permutation(lambda x, y, z, core: (x, y, (z + 3) % 4, core))
    u_late, u_early = lax.ppermute(up_units, BOTH, to_up), lax.ppermute(down_units, BOTH, to_down)

    kv_a, kv_b = kv_a.reshape(32, 128, 128), kv_b.reshape(32, 128, 128)
    natural = [pltpu.VMEM((8192, 128), BF16), pltpu.VMEM((8192 // CHUNK, 128, CHUNK), BF16)]
    out_t, lse, mixed = local_call(
        attend_kernel,
        [shape((4, 64, HALF), F32), shape((4, 1, HALF), F32), shape((256, HALF), BF16)],
        natural + [pltpu.VMEM((64, HALF), F32)],
        2,
        8 << 30,
        order, owned, kv_a, kv_b, queries,
    )

    def pair(dims, dtype=BF16, other=None):
        return [pltpu.VMEM((3,) + dims, dtype), pltpu.VMEM((3,) + (other or dims), dtype)]

    exchange = [pltpu.VMEM((4, 2, 128, D), BF16)] + [pltpu.VMEM((4, 128, D), BF16)] * 2 + pair((64, D))
    blocks = [
        shape((4, 64, PADDED), BF16),
        shape((4, 64, PADDED), BF16),
        shape((4, 48, D), BF16),
        shape((4, 4, 4, 16, HALF), BF16),
    ]
    mixed_out, grad_hidden, branch_all, grad_gain_mlp, *parts = remote_call(
        feed_kernel,
        1,
        [shape((128, D), BF16), shape((128, D), F32), shape((2, 128, D), BF16), shape((1, D), F32)] + blocks,
        48,
        [
            pltpu.VMEM((2, 256, HALF), BF16),
            pltpu.VMEM((D, 2 * PADDED), BF16),
            pltpu.VMEM((128, D), F32),
            pltpu.VMEM((4, 2, 128, D), BF16),
            pltpu.VMEM((1024, 1024), BF16),
            pltpu.VMEM((PADDED, 1024), BF16),
            pltpu.VMEM((1024, PADDED), BF16),
            pltpu.VMEM((1024, PADDED), BF16),
            pltpu.VMEM((4, 4, 64, PADDED), BF16),
            pltpu.VMEM((4, 496, PADDED), BF16),
        ]
        + pair((256, PADDED), BF16, (240, PADDED))
        + pair((2, 64, PADDED))
        + exchange
        + exchange
        + [pltpu.VMEM((128, D), F32)],
        mixed, w_o_all, own_units, u_early, u_late, down_weight, cot_all, field, gain_mlp, owners, owners_half,
    )

    grad_query, part_a, part_b = local_call(
        attend_back_kernel,
        [shape((256, HALF), F32), shape((32, 128, 128), BF16), shape((32, 128, 128), BF16)],
        natural + [pltpu.VMEM((8192, 128), F32), pltpu.VMEM((64, HALF), F32)],
        2,
        24 << 30,
        order, owned, kv_a, kv_b, queries, branch_all, w_o_all, out_t, lse,
    )

    def rows_of(columns):
        return [
            pltpu.VMEM((4, 4, 16, columns), BF16),
            pltpu.VMEM((15, 16, columns), BF16),
            pltpu.VMEM((2, 8, columns), F32),
            pltpu.VMEM((2, 8, columns), F32),
        ]

    chips = (4, 4, 2, 128, 128)
    finals = [
        shape((128, D), F32),
        shape((7, D), F32),
        shape((7, 128), F32),
        shape((7, 128), F32),
        shape((7, D), F32),
        shape((7, FF), F32),
        shape((7, FF), F32),
        shape((38, D), F32),
        shape((1, 3072), F32),
    ]
    *results, vector = remote_call(
        finish_kernel,
        2,
        finals,
        130,
        [
            pltpu.VMEM((256, 128), F32),
            pltpu.VMEM((4, 2, 128, 128), BF16),
            pltpu.VMEM((4, 2, 128, 128), BF16),
            pltpu.VMEM((7, 128, 128), BF16),
            pltpu.VMEM((7, 128, 128), BF16),
            pltpu.VMEM((4, 4, 4, 16, 384), BF16),
            pltpu.VMEM((4, 4, 4, 16, 256), BF16),
            pltpu.VMEM((2, 128, D), F32),
            pltpu.VMEM((128, D), F32),
        ]
        + [pltpu.VMEM((3, 64, PADDED), BF16)] * 2
        + [pltpu.VMEM((3, 48, D), BF16), pltpu.VMEM((40, D), F32), pltpu.VMEM((40, D), F32)]
        + [pltpu.VMEM((8, 8, 2 * PADDED), F32)] * 2
        + [pltpu.VMEM((3, 4, 4, 16, HALF), BF16)]
        + rows_of(HALF)
        + rows_of(384)
        + rows_of(256)
        + [pltpu.VMEM((5, 1, 3072), F32), pltpu.VMEM((10, 1, 3072), F32)]
        + pair((2, 2, 128, 128)) * 2
        + pair((2, 4, 16, 384))
        + pair((2, 4, 16, 256)),
        part_a.reshape(chips), part_b.reshape(chips), grad_query, table_all, weight_all, normed_all, owners,
        grad_hidden, field, gain_attn, grad_gain_mlp, col_pick, *parts,
    )
    tidied = pl.pallas_call(
        tidy_kernel,
        out_shape=[shape((128, D), BF16)] + finals[:-1],
        in_specs=whole(len(finals)),
        out_specs=whole(len(finals)),
        compiler_params=pltpu.CompilerParams(vmem_limit_bytes=VMEM_LIMIT),
    )(mixed_out, *results)
    mixed_out, d_tokens, *grads = tidied
    sums = vector[0]
    return (
        mixed_out[None],
        d_tokens[None],
        *grads,
        sums[:D],
        sums[D : 2 * D],
        sums[2 * D : 3 * D],
        sums[3 * D : 3 * D + 128],
        sums[3 * D + 128 : 3 * D + 256],
    )


def solution(mesh):
    rows, flat = P("fsdp", None), P(("fsdp", "ctx"), None)
    field = P("fsdp", "ctx", None)
    return jax.shard_map(
        per_device,
        mesh=mesh,
        in_specs=(
            field, rows, P("fsdp", "ctx"), field, P(), rows, P(), rows, P(), rows, P(), rows, P(),
            rows, rows, rows,
        ),
        out_specs=(field, field) + (flat,) * 7 + (P(),) * 5,
        check_vma=False,
    )
```

```python
import functools

import jax
import jax.numpy as jnp
import numpy as np
from jax import lax
from jax.experimental import pallas as pl
from jax.experimental.pallas import tpu as pltpu
from jax.sharding import PartitionSpec as P

D = 896
H = 14
HD = 64
HALF = 448
FF = 4864
SLICE = 608
PADDED = 640
CHUNK = 512
EPSILON = 1e-06
THETA = 1000000.0
MASKED = -1e30
MESH = pl.DeviceIdType.MESH
F32 = jnp.float32
BF16 = jnp.bfloat16
VMEM_LIMIT = 56 * 1024 * 1024


def own_place():
    f, c = lax.axis_index("fsdp"), lax.axis_index("ctx")
    zh = lax.rem(lax.div(c, 2), 2)
    return (lax.div(c, 16), lax.rem(lax.div(c, 4), 4), zh * 2 + f, lax.rem(c, 2))


def device(place):
    x, y, z, core = place
    return (lax.rem(z, 2), (x * 4 + y) * 4 + 2 * lax.div(z, 2) + core)


def turned(value, step):
    return lax.rem(value + (step + 4), 4)


def shifted(place, axis, step):
    moved = list(place)
    moved[axis] = turned(place[axis], step)
    return tuple(moved)


def partner(place):
    return place[:3] + (1 - place[3],)


def greet(places):
    barrier = pltpu.get_barrier_semaphore()
    for place in places:
        pl.semaphore_signal(barrier, inc=1, device_id=device(place), device_id_type=MESH)
    pl.semaphore_wait(barrier, len(places))


class Links:
    def __init__(self, send, recv):
        self.send, self.recv, self.opened = send, recv, []

    def start(self, src, dst, place):
        at = len(self.opened)
        assert at < self.send.shape[0]
        copy = pltpu.make_async_remote_copy(
            src_ref=src,
            dst_ref=dst,
            send_sem=self.send.at[at],
            recv_sem=self.recv.at[at],
            device_id=device(place),
            device_id_type=MESH,
        )
        copy.start()
        self.opened.append(copy)
        return copy

    def close(self):
        for copy in self.opened:
            copy.wait_send()


def ring_gather(links, slot, half, place, axis):
    me = place[axis]
    right, left = shifted(place, axis, 1), shifted(place, axis, -1)
    first = links.start(slot(me), slot(me), right)
    second = links.start(slot(me), slot(me), left)
    yield
    before, after = turned(me, -1), turned(me, 1)
    first.wait_recv()
    third = links.start(half(before, 0), half(before, 0), right)
    yield
    second.wait_recv()
    fourth = links.start(half(after, 1), half(after, 1), left)
    yield
    third.wait_recv()
    fourth.wait_recv()


def ring_reduce(links, part, low, high, place, axis, emit):
    me = place[axis]
    right, left = shifted(place, axis, 1), shifted(place, axis, -1)
    before, after, far = turned(me, -1), turned(me, 1), turned(me, 2)
    first = links.start(part(far, 0), low.at[0], right)
    second = links.start(part(far, 1), high.at[0], left)
    yield
    third = links.start(part(after, 1), high.at[1], right)
    yield
    fourth = links.start(part(before, 0), low.at[1], left)
    yield
    first.wait_recv()
    low[0] = (low[0].astype(F32) + part(after, 0)[...].astype(F32)).astype(low.dtype)
    fifth = links.start(low.at[0], low.at[2], right)
    second.wait_recv()
    high[0] = (high[0].astype(F32) + part(before, 1)[...].astype(F32)).astype(high.dtype)
    sixth = links.start(high.at[0], high.at[2], left)
    yield
    fourth.wait_recv()
    fifth.wait_recv()
    emit(0, part(me, 0)[...].astype(F32) + low[1].astype(F32) + low[2].astype(F32))
    third.wait_recv()
    sixth.wait_recv()
    emit(1, part(me, 1)[...].astype(F32) + high[1].astype(F32) + high[2].astype(F32))


def direct_reduce(links, places, part, landing, own, emit):
    copies = [links.start(part(at), landing.at[i], at) for i, at in enumerate(places)]
    yield
    total = own[...].astype(F32)
    for i, copy in enumerate(copies):
        copy.wait_recv()
        total = total + landing[i].astype(F32)
    emit(total)


def around(place, steps):
    places = []
    for step in steps:
        at = place
        for axis, by in enumerate(step):
            if by:
                at = shifted(at, axis, by)
        places.append(at)
    return places


def in_turn(*streams):
    waiting = list(streams)
    while waiting:
        still = []
        for stream in waiting:
            try:
                next(stream)
            except StopIteration:
                continue
            still.append(stream)
        waiting = still


def local_norm(field, gain):
    inverse = lax.rsqrt(jnp.mean(field * field, axis=-1, keepdims=True) + EPSILON)
    return field * inverse * gain, inverse


def norm_backward(field, inverse, gain, grad):
    scaled = grad * gain
    grad_gain = jnp.sum(grad * field * inverse, axis=0, keepdims=True)
    mean = jnp.mean(scaled * field, axis=-1, keepdims=True)
    return inverse * scaled - field * (inverse * inverse * inverse) * mean, grad_gain


def dot(left, right, contract=((1,), (0,))):
    return lax.dot_general(left, right, (contract, ((), ())), preferred_element_type=F32)


def whole(count):
    return [pl.BlockSpec(memory_space=pltpu.VMEM)] * count


def shape(dims, dtype):
    return jax.ShapeDtypeStruct(dims, dtype)


def remote_call(kernel, collective_id, outs, copies, scratch, *args, far=0):
    return pl.pallas_call(
        kernel,
        out_shape=outs,
        in_specs=whole(len(args) - far) + [pl.BlockSpec(memory_space=pl.ANY)] * far,
        out_specs=whole(len(outs)),
        scratch_shapes=list(scratch)
        + [pltpu.SemaphoreType.DMA((copies,)), pltpu.SemaphoreType.DMA((copies,))],
        compiler_params=pltpu.CompilerParams(
            collective_id=collective_id, has_side_effects=True, vmem_limit_bytes=VMEM_LIMIT
        ),
    )(*args)


KV_A_STEPS = [(0, dy, dz) for dz in (0, 2) for dy in (0, 1, -1, 2) if dy or dz]
KV_B_STEPS = [(dx, 0, dz) for dz in (0, 2) for dx in (0, 1, -1, 2) if dx or dz]


def enter_kernel(
    tokens, gain, table, w_q, w_k, w_v, bias, cot, row_pick, col_pick, w_o, w_gate, w_up, w_down,
    normed_all, table_all, weight_all, w_o_all, queries, kv_a, kv_b, cot_all, own_units, up_units, down_units, down_rows,
    weight, own_window, up_window, down_window, tall_window, fetched, send, recv,
):
    place = own_place()
    x, y, z, core = place
    f, zh = lax.rem(z, 2), lax.div(z, 2)
    other, up, down, far = partner(place), shifted(place, 2, 1), shifted(place, 2, -1), shifted(place, 2, 2)
    fetches = []

    def fetch(src, dst):
        copy = pltpu.make_async_copy(src, dst, fetched.at[len(fetches)])
        copy.start()
        fetches.append(copy)

    def offset(at):
        part = 4 * lax.rem(at[2], 2) + 2 * lax.div(at[2], 2) + at[3]
        start = jnp.minimum(lax.div(19 * part, 4), 32) * 128
        return start, SLICE * part - start

    windows = ((own_window, place, 0, HALF), (up_window, up, 224, 224), (down_window, down, 0, 224))
    for window, at, row, rows in windows:
        columns = pl.ds(pl.multiple_of(offset(at)[0], 128), 768)
        for which, array in enumerate((w_gate, w_up)):
            fetch(array.at[pl.ds(row, rows), columns], window.at[which])
    sub = 2 * zh + core
    fetch(w_down.at[pl.ds(pl.multiple_of(sub * SLICE, 16), SLICE)], tall_window)
    a_peers = around(place, KV_A_STEPS)
    b_peers = around(place, KV_B_STEPS)
    greet([other, up, down, far] + [at for at in a_peers + b_peers if at is not far])
    links = Links(send, recv)
    base = pl.multiple_of(f * HALF, HALF)

    def core_half(array):
        half = array.shape[1] // 2
        wide = array[...].astype(F32)
        return jnp.where(core == 0, wide[:, :half], wide[:, half:])

    weight[...] = jnp.concatenate(
        [core_half(w_q), core_half(w_k), core_half(w_v), jnp.zeros((HALF, 64), F32)], axis=1
    ).astype(BF16)
    w_down_copy = links.start(weight.at[pl.ds(0, 224)], weight_all.at[pl.ds(base, 224)], down)
    w_up_copy = links.start(weight.at[pl.ds(224, 224)], weight_all.at[pl.ds(base + 224, 224)], up)
    normed, _ = local_norm(tokens[...].astype(F32), gain[...])
    normed_all[core] = normed.astype(BF16)
    n_copy = links.start(normed_all.at[core], normed_all.at[core], other)
    table_all[core] = table[...]
    t_copy = links.start(table_all.at[core], table_all.at[core], other)
    cot_all[z, core] = cot[...]
    c_copy = links.start(cot_all.at[z, core], cot_all.at[z, core], other)
    weight_all[pl.ds(base, HALF)] = weight[...]
    for copy in fetches:
        copy.wait()
    for (window, at, _, rows), out in zip(windows, (own_units, up_units, down_units)):
        line = lax.broadcasted_iota(jnp.int32, (768, PADDED), 0) - offset(at)[1]
        pick = (line == row_pick[...]).astype(F32).astype(BF16)
        for which in range(2):
            out[:, PADDED * which : PADDED * (which + 1)] = dot(window[which], pick).astype(BF16)
    line = lax.broadcasted_iota(jnp.int32, (PADDED, SLICE), 1)
    pick = (line == col_pick[...]).astype(F32).astype(BF16)
    down_rows[...] = dot(pick, tall_window[...]).astype(BF16)
    n_copy.wait_recv()
    t_copy.wait_recv()
    w_down_copy.wait_recv()
    w_up_copy.wait_recv()
    lin = dot(normed_all[...].reshape(256, D), weight_all[...]) + bias[...]
    turn = lin[:, :512]
    lane = lax.broadcasted_iota(jnp.int32, (256, 512), 1)
    swapped = jnp.where(lax.rem(lane, 64) < 32, -pltpu.roll(turn, 480, 1), pltpu.roll(turn, 32, 1))
    both = table_all[...].reshape(256, 128)
    cosine = jnp.concatenate([both[:, :64]] * 8, axis=1)
    sine = jnp.concatenate([both[:, 64:]] * 8, axis=1)
    rotated = turn * cosine + swapped * sine
    kv = jnp.concatenate([rotated[:, HALF:512], lin[:, 512:576]], axis=1).astype(BF16)
    kv_a[x, y, zh] = kv[:128]
    kv_b[x, y, zh] = kv[128:]
    a_copies = [links.start(kv_a.at[x, y, zh], kv_a.at[x, y, zh], at) for at in a_peers]
    b_copies = [links.start(kv_b.at[x, y, zh], kv_b.at[x, y, zh], at) for at in b_peers]
    w_o_all[pl.ds(base, HALF)] = w_o[...]
    queries[...] = (rotated[:, :HALF] * HD**-0.5).astype(BF16)

    def stream_a():
        for copy in a_copies:
            copy.wait_recv()
        yield from ring_gather(
            links, lambda k: kv_a.at[k], lambda k, h: kv_a.at[k, pl.ds(2 * h, 2)], place, 0
        )

    def stream_b():
        for copy in b_copies:
            copy.wait_recv()
        yield from ring_gather(
            links,
            lambda k: kv_b.at[pl.ds(0, 4), k],
            lambda k, h: kv_b.at[pl.ds(2 * h, 2), k],
            place,
            1,
        )

    def stream_o():
        down_copy = links.start(w_o.at[pl.ds(0, 224)], w_o_all.at[pl.ds(base, 224)], down)
        up_copy = links.start(w_o.at[pl.ds(224, 224)], w_o_all.at[pl.ds(base + 224, 224)], up)
        for _ in range(6):
            yield
        down_copy.wait_recv()
        up_copy.wait_recv()

    c_copies = [c_copy]
    in_turn(stream_a(), stream_b(), shared_gather(links, cot_all, place, c_copies), stream_o())
    for copy in c_copies:
        copy.wait_recv()
    links.close()


def shared_gather(links, blocks, place, copies):
    z, core = place[2], place[3]
    other = partner(place)
    ring = ring_gather(
        links,
        lambda k: blocks.at[k, core],
        lambda k, h: blocks.at[k, core, pl.ds(64 * h, 64)],
        place,
        2,
    )
    next(ring)
    yield
    next(ring)
    before = turned(z, -1)
    copies.append(links.start(blocks.at[before, core], blocks.at[before, core], other))
    yield
    next(ring)
    after = turned(z, 1)
    copies.append(links.start(blocks.at[after, core], blocks.at[after, core], other))
    yield
    for _ in ring:
        yield
    last = turned(z, 2)
    copies.append(links.start(blocks.at[last, core], blocks.at[last, core], other))


def down_group(place):
    x, y, z, core = place
    sub = 2 * lax.div(z, 2) + core
    return lax.rem(x + 5 - sub, 4), lax.rem(y + sub, 4)


def feed_kernel(
    mixed, w_o, u_own, u_early, u_late, w_down, cot_all, tokens, gain, owners, owners_half,
    mixed_out, grad_hidden, branch_all, grad_gain, gate_mid, up_mid, down_mid, part_o, *rest,
):
    (
        mixed_all, w_units, hidden, normed_all, spread_t, inner_t, grad_gates, grad_ups, up_all, along_x,
        x_low, x_high, y_low, y_high,
        out_part, out_arrived, out_paired, out_low, out_high,
        grad_part, grad_arrived, grad_paired, grad_low, grad_high, grad_sum, send, recv,
    ) = rest
    place = own_place()
    x, y, z, core = place
    f = lax.rem(z, 2)
    other = partner(place)
    greet([other] + [shifted(place, axis, step) for axis in (0, 1, 2) for step in (1, -1)])
    links = Links(send, recv)
    copy = links.start(mixed, mixed_all.at[core], other)
    mixed_all[core] = mixed[...]
    own_base = pl.multiple_of(f * HALF, HALF)
    base = pl.multiple_of((1 - f) * HALF, HALF)
    copy.wait_recv()
    rows = pl.ds(pl.multiple_of(core * 128, 128), 128)
    field = tokens[...].astype(F32) + (
        dot(mixed_all[0, rows], w_o[:HALF]) + dot(mixed_all[1, rows], w_o[HALF:])
    )
    hidden[...] = field
    normed, _ = local_norm(field, gain[...])
    normed_all[z, core] = normed.astype(BF16)
    own = links.start(normed_all.at[z, core], normed_all.at[z, core], other)

    copies = [own]
    gather = shared_gather(links, normed_all, place, copies)
    next(gather)
    w_units[pl.ds(own_base, HALF)] = u_own[...]
    w_units[pl.ds(base, 224)] = u_early[...]
    w_units[pl.ds(base + 224, 224)] = u_late[...]

    before, after, far = turned(z, -1), turned(z, 1), turned(z, 2)
    both = (
        (out_part, out_arrived, out_paired), (grad_part, grad_arrived, grad_paired),
    )

    def tile(k):
        n = normed_all[k].reshape(256, D)
        c = cot_all[k].reshape(256, D)
        g = dot(n, w_units[:, :PADDED])
        u = dot(n, w_units[:, PADDED:])
        s = 1.0 / (1.0 + jnp.exp(-g))
        silu = g * s
        inner = silu * u
        low = inner.astype(BF16)
        out_part[k] = dot(low, w_down[...]).astype(BF16).reshape(2, 128, D)
        columns = pl.ds(pl.multiple_of(k * 256, 256), 256)
        inner_t[:, columns] = low.T
        gi = dot(c, w_down[...], ((1,), (1,)))
        gg = (gi * u * s * (1.0 + g * (1.0 - s))).astype(BF16)
        gu = (gi * silu).astype(BF16)
        grad_gates[columns] = gg
        grad_ups[columns] = gu
        grad_part[k] = (
            dot(gg, w_units[:, :PADDED], ((1,), (1,))) + dot(gu, w_units[:, PADDED:], ((1,), (1,)))
        ).astype(BF16).reshape(2, 128, D)
        return [links.start(part.at[k, 1 - core], come.at[k], other) for part, come, _ in both]

    def pair_up(k, copies):
        for trip, (part, come, paired) in zip(copies, both):
            trip.wait_recv()
            paired[k] = (come[k].astype(F32) + part[k, core].astype(F32)).astype(BF16)

    def emit_out(h, value):
        at = pl.ds(64 * h, 64)
        mixed_out[at] = (hidden[at] + value).astype(BF16)

    def emit_grad(h, value):
        grad_sum[pl.ds(64 * h, 64)] = value

    reduces = [
        ring_reduce(
            links, lambda k, h, p=paired: p.at[k, pl.ds(64 * h, 64)], low, high, place, 2, emit
        )
        for paired, low, high, emit in (
            (grad_paired, grad_low, grad_high, emit_grad),
            (out_paired, out_low, out_high, emit_out),
        )
    ]

    def advance():
        for stream in reduces:
            next(stream, None)

    copies[0].wait_recv()
    trips_own = tile(z)
    next(gather)
    next(gather)
    copies[2].wait_recv()
    trips_after = tile(after)
    in_turn(gather)
    copies[3].wait_recv()
    trips_far = tile(far)
    pair_up(far, trips_far)
    advance()
    pair_up(after, trips_after)
    advance()
    copies[1].wait_recv()
    trips_before = tile(before)
    pair_up(before, trips_before)
    advance()
    pair_up(z, trips_own)

    @pl.loop(0, 4)
    def _(k):
        columns = pl.ds(pl.multiple_of(k * 256, 256), 256)
        spread_t[:, columns] = dot(
            owners[...], normed_all[k].reshape(256, D), ((1,), (1,))
        ).astype(BF16)

    @pl.loop(0, 4)
    def _(k):
        lines = spread_t[pl.ds(pl.multiple_of(k * 256, 256), 256)]
        along_x[k, :256] = dot(lines, grad_gates[...]).astype(BF16)
        group, _ = down_group((k, y, z, core))
        lines = inner_t[pl.ds(pl.multiple_of(group * 160, 16), 160)]
        tall = dot(lines, cot_all[...].reshape(1024, D)).astype(BF16)
        along_x[k, 256:416] = tall[:, :PADDED]
        along_x[k, 416:496, :256] = tall[:80, PADDED:]
        along_x[k, 416:496, 256:512] = tall[80:, PADDED:]
        along_x[k, 416:496, 512:] = jnp.zeros((80, 128), BF16)

    def put_x(h, value):
        if h == 0:
            gate_mid[...] = value.astype(BF16).reshape(4, 64, PADDED)
            return
        for k in range(4):
            row, lane = 160 + 40 * (k % 2), 256 * (k // 2)
            down_mid[k, :40, :PADDED] = value[40 * k : 40 * (k + 1)].astype(BF16)
            down_mid[k, :40, PADDED:] = value[row : row + 40, lane : lane + 256].astype(BF16)
            down_mid[k, 40:] = jnp.zeros((8, D), BF16)

    def put_y(h, value):
        up_mid[pl.ds(2 * h, 2)] = value.astype(BF16)

    stream_x = ring_reduce(
        links, lambda k, h: along_x.at[k, pl.ds(256 * h, 256 - 16 * h)], x_low, x_high, place, 0, put_x
    )
    stream_y = ring_reduce(
        links, lambda k, h: up_all.at[pl.ds(2 * h, 2), k], y_low, y_high, place, 1, put_y
    )
    for _ in range(3):
        next(stream_x)
    advance()

    @pl.loop(0, 4)
    def _(k):
        lines = spread_t[pl.ds(pl.multiple_of(k * 256, 256), 256)]
        up_all[k] = dot(lines, grad_ups[...]).astype(BF16).reshape(4, 64, PADDED)

    for _ in range(3):
        next(stream_y)
    spread_o = (
        dot(owners_half[0], mixed_all[0], ((1,), (1,))) + dot(owners_half[1], mixed_all[1], ((1,), (1,)))
    ).astype(BF16)
    for _ in range(8):
        advance()
    field = hidden[...]
    _, inverse = local_norm(field, gain[...])
    through, gains = norm_backward(field, inverse, gain[...], grad_sum[...])
    grad_gain[...] = gains
    total = cot_all[z, core].astype(F32) + through
    grad_hidden[...] = total
    branch_all[core] = total.astype(BF16)
    trip = links.start(branch_all.at[core], branch_all.at[core], other)
    next(stream_x)
    next(stream_y)
    trip.wait_recv()
    branch = branch_all[...].reshape(256, D).astype(F32)
    half = jnp.where(core == 0, branch[:, :HALF], branch[:, HALF:]).astype(BF16)
    part_o[...] = dot(spread_o, half).astype(BF16).reshape(4, 4, 4, 16, HALF)
    in_turn(stream_y, stream_x)
    links.close()


def finish_kernel(
    kv_part_a, kv_part_b, grad_query, table_all, weight_all, normed_all, owners, grad_hidden, tokens, gain,
    gain_mlp_grad, col_pick, gate_mid, up_mid, down_mid, part_o, *rest,
):
    (
        d_tokens, wq_out, wk_out, wv_out, wo_out, gate_out, up_out, down_out, vector_out,
        grad_kv, kv_mid_a, kv_mid_b, kv_land_a, kv_land_b, part_qa, part_qb, grad_normed, half_sum,
        gate_land, up_land, down_land, down_end, down_own, end, rows_all,
        o_first, o_mid, o_land, o_end, o_rows, qa_mid, qa_land, qa_end, qa_rows, qb_mid, qb_land, qb_end, qb_rows,
        vec_now, vec_in,
        a_low, a_high, b_low, b_high, qa_low, qa_high, qb_low, qb_high, send, recv,
    ) = rest
    place = own_place()
    x, y, z, core = place
    f, zh = lax.rem(z, 2), lax.div(z, 2)
    sub = 2 * zh + core
    other = partner(place)
    mine = z * 2 + core
    x_peers, y_peers = around(place, X_STEPS), around(place, Y_STEPS)
    xy_peers, xz_peers, yz_peers = (
        around(place, steps) for steps in (XY_STEPS, XZ_STEPS, YZ_STEPS)
    )
    z_peers = around(place, Z_STEPS)
    ring = []
    for step in range(1, 8):
        at = lax.rem(mine + step, 8)
        ring.append((x, y, lax.div(at, 2), lax.rem(at, 2)))
    first, second = down_group(place)
    to_owner = (sub, first, 2 * lax.div(second, 2) + f, lax.rem(second, 2))
    from_group = (lax.rem(x + y + 3, 4), lax.rem(sub + 4 - x, 4), 2 * lax.div(x, 2) + f, lax.rem(x, 2))
    greet(ring + xy_peers + xz_peers[3:] + yz_peers[3:] + [to_owner, from_group])
    links = Links(send, recv)

    def kv_stream(part, mid, landing, order, low, high, peers, base):
        def put_mid(h, value):
            mid[pl.ds(2 * h, 2)] = value.astype(BF16)

        def put_end(value):
            grad_kv[pl.ds(base, 128)] = value

        if order == 0:
            first = lambda k, h: part.at[k, pl.ds(2 * h, 2)]
        else:
            first = lambda k, h: part.at[pl.ds(2 * h, 2), k]
        yield from ring_reduce(links, first, low, high, place, order, put_mid)
        keep = 1 - order
        yield from direct_reduce(
            links, peers, lambda at: mid.at[at[keep], lax.div(at[2], 2)], landing,
            mid.at[place[keep], zh], put_end,
        )

    def to_rows(end, rows):
        last = links.start(end.at[1 - core], rows.at[core], other)
        rows[core] = end[core]
        yield
        last.wait_recv()

    def q_stream(part, mid, landing, end, rows, order, low, high, peers):
        def put_mid(h, value):
            mid[pl.ds(2 * h, 2)] = value.astype(BF16)

        def put_end(value):
            end[0], end[1] = value[:8], value[8:]

        if order == 0:
            first = lambda k, h: part.at[k, pl.ds(2 * h, 2)]
        else:
            first = lambda k, h: part.at[pl.ds(2 * h, 2), k]
        yield from ring_reduce(links, first, low, high, place, order, put_mid)
        keep = 1 - order
        yield from direct_reduce(
            links, peers, lambda at: mid.at[at[keep], at[2]], landing, mid.at[place[keep], z], put_end
        )
        yield from to_rows(end, rows)

    def o_stream():
        def put_end(value):
            o_end[0], o_end[1] = value[:8], value[8:]

        def put_mid(value):
            o_mid[...] = value.astype(BF16)

        def part(at):
            return part_o.at[pl.ds(0, 4), pl.ds(0, 4), at[2]]

        yield from direct_reduce(links, z_peers, part, o_first, part(place), put_mid)
        yield from direct_reduce(
            links, xy_peers, lambda at: o_mid.at[at[0], at[1]], o_land, o_mid.at[x, y], put_end
        )
        yield from to_rows(o_end, o_rows)

    def wide(mid, landing, axis, peers, column):
        def put_end(value):
            end[:, :, pl.ds(column, PADDED)] = value.reshape(8, 8, PADDED)

        yield from direct_reduce(
            links, peers, lambda at: mid.at[at[axis]], landing, mid.at[place[axis]], put_end
        )

    def tall():
        def put_end(value):
            down_end[...] = value[:40]

        yield from direct_reduce(
            links, y_peers, lambda at: down_mid.at[down_group(at)[1]], down_land, down_mid.at[second], put_end
        )
        copy = links.start(down_end, down_own, to_owner)
        yield
        copy.wait_recv()
        down_out[...] = down_own[:38]

    def hidden_units():
        gates = wide(gate_mid, gate_land, 1, y_peers, 0)
        ups = wide(up_mid, up_land, 0, x_peers, PADDED)
        next(gates)
        next(ups)
        yield
        for stream in (gates, ups):
            for _ in stream:
                pass
        copies = [
            links.start(end.at[to[2] * 2 + to[3]], rows_all.at[mine], to) for to in ring
        ]
        rows_all[mine] = end[mine]
        yield
        line = lax.broadcasted_iota(jnp.int32, (PADDED, SLICE), 1)
        pick = (line == col_pick[...]).astype(F32).astype(BF16)
        for copy in copies:
            copy.wait_recv()
        for which, out in enumerate((gate_out, up_out)):
            values = rows_all[:, :, PADDED * which : PADDED * (which + 1)].reshape(64, PADDED)
            top = values.astype(BF16)
            below = (values - top.astype(F32)).astype(BF16)
            units = dot(top, pick) + dot(below, pick)
            for at in range(8):
                part = 4 * (at // 2 % 2) + 2 * (at // 4) + at % 2
                out[:, SLICE * part : SLICE * (part + 1)] = units[8 * at : 8 * at + 7]

    kv_streams = [
        kv_stream(kv_part_a, kv_mid_a, kv_land_a, 0, a_low, a_high, yz_kv(place), 0),
        kv_stream(kv_part_b, kv_mid_b, kv_land_b, 1, b_low, b_high, xz_kv(place), 128),
    ]
    units, talls, os = hidden_units(), tall(), o_stream()
    for _ in range(3):
        for stream in kv_streams:
            next(stream)
    next(os)
    spread_n = dot(owners[...], normed_all[...].reshape(256, D), ((1,), (1,))).astype(BF16)
    for stream in kv_streams:
        next(stream)
    in_turn(*kv_streams)

    table = table_all[...].reshape(256, 128)
    cosine = jnp.concatenate([table[:, :64]] * 8, axis=1)
    sine = jnp.concatenate([table[:, 64:]] * 8, axis=1)
    turn = jnp.concatenate([grad_query[...] * HD**-0.5, grad_kv[:, :64]], axis=1)
    scaled = turn * sine
    lane = lax.broadcasted_iota(jnp.int32, (256, 512), 1)
    swapped = jnp.where(
        lax.rem(lane, 64) < 32, pltpu.roll(scaled, 480, 1), -pltpu.roll(scaled, 32, 1)
    )
    lin = jnp.concatenate(
        [turn * cosine + swapped, grad_kv[:, 64:], jnp.zeros((256, 64), F32)], axis=1
    ).astype(BF16)
    part = dot(spread_n, lin).astype(BF16)
    part_qa[...] = part[:, :384].reshape(4, 4, 4, 16, 384)
    part_qb[...] = part[:, 384:].reshape(4, 4, 4, 16, 256)
    q_streams = [
        q_stream(part_qa, qa_mid, qa_land, qa_end, qa_rows, 0, qa_low, qa_high, yz_peers),
        q_stream(part_qb, qb_mid, qb_land, qb_end, qb_rows, 1, qb_low, qb_high, xz_peers),
    ]
    for _ in range(3):
        for stream in q_streams:
            next(stream)

    next(units)
    next(talls)

    def sums():
        grad_normed[...] = dot(lin, weight_all[...], ((1,), (1,))).reshape(2, 128, D)
        copy = links.start(grad_normed.at[1 - core], half_sum, other)
        column = jnp.sum(lin.astype(F32), axis=0, keepdims=True)

        def placed(values):
            empty = jnp.zeros_like(values)
            return jnp.where(
                core == 0,
                jnp.concatenate([values, empty], axis=1),
                jnp.concatenate([empty, values], axis=1),
            )

        biases = [placed(column[:, low:high]) for low, high in ((0, HALF), (HALF, 512), (512, 576))]
        copy.wait_recv()
        grad = grad_normed[core] + half_sum[...]
        field = tokens[...].astype(F32)
        _, inverse = local_norm(field, gain[...])
        through, gains = norm_backward(field, inverse, gain[...], grad)
        d_tokens[...] = grad_hidden[...] + through
        vec_now[0] = jnp.concatenate(
            [gains, gain_mlp_grad[...], *biases, jnp.zeros((1, 128), F32)], axis=1
        )
        trip = links.start(vec_now.at[0], vec_in.at[0], other)
        trip.wait_recv()
        vec_now[1] = vec_now[0] + vec_in[0]
        for stage, axis in enumerate((2, 1, 0)):
            trips = [
                links.start(
                    vec_now.at[1 + stage],
                    vec_in.at[1 + 3 * stage + at],
                    shifted(place, axis, step),
                )
                for at, step in enumerate((1, -1, 2))
            ]
            yield
            for trip in trips:
                trip.wait_recv()
            at = 1 + 3 * stage
            near = vec_in[at] + vec_in[at + 1]
            vec_now[2 + stage] = (vec_now[1 + stage] + vec_in[at + 2]) + near
        vector_out[...] = vec_now[4]

    in_turn(sums(), *q_streams, os, units, talls)

    def row_of(core_at):
        return jnp.concatenate([qa_rows[core_at], qb_rows[core_at]], axis=1)[:7]

    first, second = row_of(0), row_of(1)
    for out, low, high in ((wq_out, 0, HALF), (wk_out, HALF, 512), (wv_out, 512, 576)):
        out[...] = jnp.concatenate([first[:, low:high], second[:, low:high]], axis=1)
    wo_out[...] = jnp.concatenate([o_rows[0][:7], o_rows[1][:7]], axis=1)
    links.close()


AROUND = (0, 1, -1, 2)
X_STEPS = [(d, 0, 0) for d in AROUND[1:]]
Y_STEPS = [(0, d, 0) for d in AROUND[1:]]
Z_STEPS = [(0, 0, d) for d in AROUND[1:]]
XY_STEPS = [(dx, dy, 0) for dy in AROUND for dx in AROUND if dx or dy]
XZ_STEPS = [(dx, 0, dz) for dz in AROUND for dx in AROUND if dx or dz]
YZ_STEPS = [(0, dy, dz) for dz in AROUND for dy in AROUND if dy or dz]


def yz_kv(place):
    return around(place, KV_A_STEPS)


def xz_kv(place):
    return around(place, KV_B_STEPS)


def tidy_kernel(*refs):
    half = len(refs) // 2
    for src, dst in zip(refs[:half], refs[half:]):
        dst[...] = src[...]


def natural_order(order, kv_a, kv_b, kv, kv_t):
    @pl.loop(0, 32)
    def _(chip):
        for t in range(4):
            block = kv_a[chip, pl.ds(64 * t, 64)] if t < 2 else kv_b[chip, pl.ds(64 * (t - 2), 64)]
            at = pl.multiple_of(order[4 * chip + t] * 64, 64)
            kv[pl.ds(at, 64)] = block

    @pl.loop(0, 8192 // CHUNK)
    def _(c):
        kv_t[c] = kv[pl.ds(pl.multiple_of(c * CHUNK, CHUNK), CHUNK)].T


def allowed_at(c, base):
    key = c * CHUNK + lax.broadcasted_iota(jnp.int32, (CHUNK, HALF), 0)
    lane = lax.broadcasted_iota(jnp.int32, (CHUNK, HALF), 1)
    return key <= base + lax.rem(lane, 64)


def by_head(rows):
    return jnp.concatenate([rows[:, 64 * h : 64 * (h + 1)] for h in range(7)], axis=0)


def side_by_side(columns_t):
    stacked = columns_t.T
    return jnp.concatenate([stacked[64 * h : 64 * (h + 1)] for h in range(7)], axis=1)


def attend_kernel(order, owned, kv_a, kv_b, queries, out_t, lse, mixed, kv, kv_t, acc):
    natural_order(order, kv_a, kv_b, kv, kv_t)
    none = jnp.zeros((64, HALF), F32)
    for t in range(4):
        spot = owned[t]
        rows = by_head(queries[64 * t : 64 * (t + 1)].astype(F32))
        q_t = jnp.concatenate([rows.T, none], axis=0).astype(BF16)
        last = lax.div(spot * 64, CHUNK)
        acc[...] = jnp.zeros_like(acc)

        def step(c, carry, masked):
            top, total = carry
            scores = dot(kv[pl.ds(pl.multiple_of(c * CHUNK, CHUNK), CHUNK)], q_t)
            if masked:
                scores = jnp.where(allowed_at(c, spot * 64), scores, MASKED)
            new_top = jnp.maximum(top, jnp.max(scores, axis=0, keepdims=True))
            probs = jnp.exp(scores - new_top)
            scale = jnp.exp(top - new_top)
            total = total * scale + jnp.sum(probs, axis=0, keepdims=True)
            acc[...] = acc[...] * scale + dot(kv_t[c, pl.ds(64, 64)], probs.astype(BF16))
            return new_top, total

        start = (jnp.full((1, HALF), MASKED, F32), jnp.zeros((1, HALF), F32))
        carry = lax.fori_loop(0, last, lambda c, carry: step(c, carry, False), start)
        top, total = step(last, carry, True)
        result = acc[...] / total
        out_t[t] = result
        mixed[64 * t : 64 * (t + 1)] = side_by_side(result).astype(BF16)
        lse[t] = top + jnp.log(total)


def attend_back_kernel(
    order, owned, kv_a, kv_b, queries, branch, w_o, out_t, lse,
    grad_query, grad_a, grad_b, kv, kv_t, acc, acc_q,
):
    natural_order(order, kv_a, kv_b, kv, kv_t)
    acc[...] = jnp.zeros_like(acc)
    grad_mixed = dot(
        branch[...].reshape(256, D), w_o[pl.ds(pl.multiple_of(owned[4] * HALF, HALF), HALF)], ((1,), (1,))
    )
    none_t, none = jnp.zeros((64, HALF), F32), jnp.zeros((HALF, 64), F32)
    for t in range(4):
        spot = owned[t]
        last = lax.div(spot * 64, CHUNK)
        rows = by_head(queries[64 * t : 64 * (t + 1)].astype(F32))
        q = jnp.concatenate([rows, none], axis=1).astype(BF16)
        q_t = jnp.concatenate([rows.T, none_t], axis=0).astype(BF16)
        rows = by_head(grad_mixed[64 * t : 64 * (t + 1)].astype(BF16).astype(F32))
        g = jnp.concatenate([none, rows], axis=1).astype(BF16)
        rows_t = rows.T
        g_t = jnp.concatenate([none_t, rows_t], axis=0).astype(BF16)
        delta = jnp.sum(rows_t * out_t[t], axis=0, keepdims=True)
        norm = lse[t]
        acc_q[...] = jnp.zeros_like(acc_q)

        def step(c, masked):
            rows = pl.ds(pl.multiple_of(c * CHUNK, CHUNK), CHUNK)
            block = kv[rows]
            scores = dot(block, q_t)
            if masked:
                scores = jnp.where(allowed_at(c, spot * 64), scores, MASKED)
            probs = jnp.exp(scores - norm)
            grad_probs = dot(block, g_t)
            grad_scores = (probs * (grad_probs - delta)).astype(BF16)
            acc[rows] += dot(probs.astype(BF16), g) + dot(grad_scores, q)
            acc_q[...] += dot(kv_t[c, pl.ds(0, 64)], grad_scores)

        def body(c, carry):
            step(c, False)
            return carry

        lax.fori_loop(0, last, body, 0)
        step(last, True)
        grad_query[64 * t : 64 * (t + 1)] = side_by_side(acc_q[...])

    @pl.loop(0, 32)
    def _(chip):
        for t in range(4):
            at = pl.multiple_of(order[4 * chip + t] * 64, 64)
            block = acc[pl.ds(at, 64)].astype(BF16)
            if t < 2:
                grad_a[chip, pl.ds(64 * t, 64)] = block
            else:
                grad_b[chip, pl.ds(64 * (t - 2), 64)] = block


def local_call(kernel, outs, scratch, scalars, flops, *args):
    return pl.pallas_call(
        kernel,
        out_shape=outs,
        in_specs=[pl.BlockSpec(memory_space=pltpu.SMEM)] * scalars + whole(len(args) - scalars),
        out_specs=[pl.BlockSpec(memory_space=pltpu.VMEM)] * len(outs),
        scratch_shapes=scratch,
        compiler_params=pltpu.CompilerParams(vmem_limit_bytes=VMEM_LIMIT),
        cost_estimate=pl.CostEstimate(flops=flops, bytes_accessed=8 << 20, transcendentals=1 << 23),
    )(*args)


def padded_columns():
    col = np.arange(PADDED)
    return np.where(col % 40 < 38, col // 40 * 38 + col % 40, -(1 << 20)).astype(np.int32)


def owner_rows():
    row = np.arange(1024)
    i, core, z, y, x = row % 8, row // 8 % 2, row // 16 % 4, row // 64 % 4, row // 256
    at = 7 * (64 * (z % 2) + 16 * x + 4 * y + 2 * (z // 2) + core) + i
    pick = np.zeros((1024, D), np.float32)
    keep = i < 7
    pick[row[keep], at[keep]] = 1.0
    return pick


def index_of(x, y, z, core):
    return (z % 2) * 64 + (x * 4 + y) * 4 + 2 * (z // 2) + core


def permutation(move):
    pairs = []
    for x in range(4):
        for y in range(4):
            for z in range(4):
                for core in range(2):
                    pairs.append((index_of(x, y, z, core), index_of(*move(x, y, z, core))))
    return pairs


BOTH = ("fsdp", "ctx")


def per_device(
    tokens, block_index, positions, cotangent, norm_attn, w_q, b_q, w_k, b_k, w_v, b_v, w_o,
    norm_mlp, w_gate, w_up, w_down,
):
    f, c = lax.axis_index("fsdp"), lax.axis_index("ctx")
    core, zh = c % 2, (c // 2) % 2
    z = 2 * zh + f
    sub = 2 * zh + core
    field, cot = tokens[0], cotangent[0]
    order = block_index[0]
    owned = lax.dynamic_slice_in_dim(order, 4 * (c // 2), 4, 0)
    owned = jnp.concatenate([owned, core[None]])
    gain_attn = norm_attn.astype(F32)[None]
    gain_mlp = norm_mlp.astype(F32)[None]

    freq = THETA ** (-(jnp.arange(HD // 2, dtype=F32) * 2.0 / HD))
    angle = positions[0].astype(F32)[:, None] * freq[None, :]
    cosine, sine = jnp.cos(angle), jnp.sin(angle)
    table = jnp.concatenate([cosine, cosine, sine, sine], -1)

    def core_columns(array):
        half = array.shape[-1] // 2
        return jnp.where(core == 0, array[..., :half], array[..., half:])

    bias = jnp.concatenate(
        [core_columns(b_q), core_columns(b_k), core_columns(b_v), jnp.zeros((64,), BF16)], axis=0
    ).astype(F32)[None]

    picked = padded_columns()
    row_pick, col_pick = jnp.asarray(picked[None]), jnp.asarray(picked[:, None])
    owners = owner_rows()
    owners_half = jnp.asarray(np.stack([owners[:, :HALF], owners[:, HALF:]]), BF16)
    owners = jnp.asarray(owners, BF16)

    (
        normed_all, table_all, weight_all, w_o_all, queries, kv_a, kv_b, cot_all,
        own_units, up_units, down_units, down_weight,
    ) = remote_call(
        enter_kernel,
        0,
        [
            shape((2, 128, D), BF16),
            shape((2, 128, 128), F32),
            shape((D, PADDED), BF16),
            shape((D, D), BF16),
            shape((256, HALF), BF16),
            shape((4, 4, 2, 128, 128), BF16),
            shape((4, 4, 2, 128, 128), BF16),
            shape((4, 2, 128, D), BF16),
            shape((HALF, 2 * PADDED), BF16),
            shape((224, 2 * PADDED), BF16),
            shape((224, 2 * PADDED), BF16),
            shape((PADDED, D), BF16),
        ],
        40,
        [
            pltpu.VMEM((HALF, PADDED), BF16),
            pltpu.VMEM((2, HALF, 768), BF16),
            pltpu.VMEM((2, 224, 768), BF16),
            pltpu.VMEM((2, 224, 768), BF16),
            pltpu.VMEM((SLICE, D), BF16),
            pltpu.SemaphoreType.DMA((7,)),
        ],
        field, gain_attn, table, w_q, w_k, w_v, bias, cot, row_pick, col_pick, w_o, w_gate, w_up, w_down,
        far=3,
    )

    to_up = permutation(lambda x, y, z, core: (x, y, (z + 1) % 4, core))
    to_down = permutation(lambda x, y, z, core: (x, y, (z + 3) % 4, core))
    u_late, u_early = lax.ppermute(up_units, BOTH, to_up), lax.ppermute(down_units, BOTH, to_down)

    kv_a, kv_b = kv_a.reshape(32, 128, 128), kv_b.reshape(32, 128, 128)
    natural = [pltpu.VMEM((8192, 128), BF16), pltpu.VMEM((8192 // CHUNK, 128, CHUNK), BF16)]
    out_t, lse, mixed = local_call(
        attend_kernel,
        [shape((4, 64, HALF), F32), shape((4, 1, HALF), F32), shape((256, HALF), BF16)],
        natural + [pltpu.VMEM((64, HALF), F32)],
        2,
        8 << 30,
        order, owned, kv_a, kv_b, queries,
    )

    def pair(dims, dtype=BF16, other=None):
        return [pltpu.VMEM((3,) + dims, dtype), pltpu.VMEM((3,) + (other or dims), dtype)]

    exchange = [pltpu.VMEM((4, 2, 128, D), BF16)] + [pltpu.VMEM((4, 128, D), BF16)] * 2 + pair((64, D))
    blocks = [
        shape((4, 64, PADDED), BF16),
        shape((4, 64, PADDED), BF16),
        shape((4, 48, D), BF16),
        shape((4, 4, 4, 16, HALF), BF16),
    ]
    mixed_out, grad_hidden, branch_all, grad_gain_mlp, *parts = remote_call(
        feed_kernel,
        1,
        [shape((128, D), BF16), shape((128, D), F32), shape((2, 128, D), BF16), shape((1, D), F32)] + blocks,
        48,
        [
            pltpu.VMEM((2, 256, HALF), BF16),
            pltpu.VMEM((D, 2 * PADDED), BF16),
            pltpu.VMEM((128, D), F32),
            pltpu.VMEM((4, 2, 128, D), BF16),
            pltpu.VMEM((1024, 1024), BF16),
            pltpu.VMEM((PADDED, 1024), BF16),
            pltpu.VMEM((1024, PADDED), BF16),
            pltpu.VMEM((1024, PADDED), BF16),
            pltpu.VMEM((4, 4, 64, PADDED), BF16),
            pltpu.VMEM((4, 496, PADDED), BF16),
        ]
        + pair((256, PADDED), BF16, (240, PADDED))
        + pair((2, 64, PADDED))
        + exchange
        + exchange
        + [pltpu.VMEM((128, D), F32)],
        mixed, w_o_all, own_units, u_early, u_late, down_weight, cot_all, field, gain_mlp, owners, owners_half,
    )

    grad_query, part_a, part_b = local_call(
        attend_back_kernel,
        [shape((256, HALF), F32), shape((32, 128, 128), BF16), shape((32, 128, 128), BF16)],
        natural + [pltpu.VMEM((8192, 128), F32), pltpu.VMEM((64, HALF), F32)],
        2,
        24 << 30,
        order, owned, kv_a, kv_b, queries, branch_all, w_o_all, out_t, lse,
    )

    def rows_of(columns):
        return [
            pltpu.VMEM((4, 4, 16, columns), BF16),
            pltpu.VMEM((15, 16, columns), BF16),
            pltpu.VMEM((2, 8, columns), F32),
            pltpu.VMEM((2, 8, columns), F32),
        ]

    chips = (4, 4, 2, 128, 128)
    finals = [
        shape((128, D), F32),
        shape((7, D), F32),
        shape((7, 128), F32),
        shape((7, 128), F32),
        shape((7, D), F32),
        shape((7, FF), F32),
        shape((7, FF), F32),
        shape((38, D), F32),
        shape((1, 3072), F32),
    ]
    *results, vector = remote_call(
        finish_kernel,
        2,
        finals,
        130,
        [
            pltpu.VMEM((256, 128), F32),
            pltpu.VMEM((4, 2, 128, 128), BF16),
            pltpu.VMEM((4, 2, 128, 128), BF16),
            pltpu.VMEM((7, 128, 128), BF16),
            pltpu.VMEM((7, 128, 128), BF16),
            pltpu.VMEM((4, 4, 4, 16, 384), BF16),
            pltpu.VMEM((4, 4, 4, 16, 256), BF16),
            pltpu.VMEM((2, 128, D), F32),
            pltpu.VMEM((128, D), F32),
        ]
        + [pltpu.VMEM((3, 64, PADDED), BF16)] * 2
        + [pltpu.VMEM((3, 48, D), BF16), pltpu.VMEM((40, D), F32), pltpu.VMEM((40, D), F32)]
        + [pltpu.VMEM((8, 8, 2 * PADDED), F32)] * 2
        + [pltpu.VMEM((3, 4, 4, 16, HALF), BF16)]
        + rows_of(HALF)
        + rows_of(384)
        + rows_of(256)
        + [pltpu.VMEM((5, 1, 3072), F32), pltpu.VMEM((10, 1, 3072), F32)]
        + pair((2, 2, 128, 128)) * 2
        + pair((2, 4, 16, 384))
        + pair((2, 4, 16, 256)),
        part_a.reshape(chips), part_b.reshape(chips), grad_query, table_all, weight_all, normed_all, owners,
        grad_hidden, field, gain_attn, grad_gain_mlp, col_pick, *parts,
    )
    tidied = pl.pallas_call(
        tidy_kernel,
        out_shape=[shape((128, D), BF16)] + finals[:-1],
        in_specs=whole(len(finals)),
        out_specs=whole(len(finals)),
        compiler_params=pltpu.CompilerParams(vmem_limit_bytes=VMEM_LIMIT),
    )(mixed_out, *results)
    mixed_out, d_tokens, *grads = tidied
    sums = vector[0]
    return (
        mixed_out[None],
        d_tokens[None],
        *grads,
        sums[:D],
        sums[D : 2 * D],
        sums[2 * D : 3 * D],
        sums[3 * D : 3 * D + 128],
        sums[3 * D + 128 : 3 * D + 256],
    )


def solution(mesh):
    rows, flat = P("fsdp", None), P(("fsdp", "ctx"), None)
    field = P("fsdp", "ctx", None)
    return jax.shard_map(
        per_device,
        mesh=mesh,
        in_specs=(
            field, rows, P("fsdp", "ctx"), field, P(), rows, P(), rows, P(), rows, P(), rows, P(),
            rows, rows, rows,
        ),
        out_specs=(field, field) + (flat,) * 7 + (P(),) * 5,
        check_vma=False,
    )
```

```python
import functools

import jax
import jax.numpy as jnp
import numpy as np
from jax import lax
from jax.experimental import pallas as pl
from jax.experimental.pallas import tpu as pltpu
from jax.sharding import PartitionSpec as P

D = 896
H = 14
HD = 64
HALF = 448
FF = 4864
SLICE = 608
PADDED = 640
CHUNK = 512
EPSILON = 1e-06
THETA = 1000000.0
MASKED = -1e30
MESH = pl.DeviceIdType.MESH
F32 = jnp.float32
BF16 = jnp.bfloat16
VMEM_LIMIT = 56 * 1024 * 1024


def own_place():
    f, c = lax.axis_index("fsdp"), lax.axis_index("ctx")
    zh = lax.rem(lax.div(c, 2), 2)
    return (lax.div(c, 16), lax.rem(lax.div(c, 4), 4), zh * 2 + f, lax.rem(c, 2))


def device(place):
    x, y, z, core = place
    return (lax.rem(z, 2), (x * 4 + y) * 4 + 2 * lax.div(z, 2) + core)


def turned(value, step):
    return lax.rem(value + (step + 4), 4)


def shifted(place, axis, step):
    moved = list(place)
    moved[axis] = turned(place[axis], step)
    return tuple(moved)


def partner(place):
    return place[:3] + (1 - place[3],)


def greet(places):
    barrier = pltpu.get_barrier_semaphore()
    for place in places:
        pl.semaphore_signal(barrier, inc=1, device_id=device(place), device_id_type=MESH)
    pl.semaphore_wait(barrier, len(places))


class Links:
    def __init__(self, send, recv):
        self.send, self.recv, self.opened = send, recv, []

    def start(self, src, dst, place):
        at = len(self.opened)
        assert at < self.send.shape[0]
        copy = pltpu.make_async_remote_copy(
            src_ref=src,
            dst_ref=dst,
            send_sem=self.send.at[at],
            recv_sem=self.recv.at[at],
            device_id=device(place),
            device_id_type=MESH,
        )
        copy.start()
        self.opened.append(copy)
        return copy

    def close(self):
        for copy in self.opened:
            copy.wait_send()


def ring_gather(links, slot, half, place, axis):
    me = place[axis]
    right, left = shifted(place, axis, 1), shifted(place, axis, -1)
    first = links.start(slot(me), slot(me), right)
    second = links.start(slot(me), slot(me), left)
    yield
    before, after = turned(me, -1), turned(me, 1)
    first.wait_recv()
    third = links.start(half(before, 0), half(before, 0), right)
    yield
    second.wait_recv()
    fourth = links.start(half(after, 1), half(after, 1), left)
    yield
    third.wait_recv()
    fourth.wait_recv()


def ring_reduce(links, part, low, high, place, axis, emit):
    me = place[axis]
    right, left = shifted(place, axis, 1), shifted(place, axis, -1)
    before, after, far = turned(me, -1), turned(me, 1), turned(me, 2)
    first = links.start(part(far, 0), low.at[0], right)
    second = links.start(part(far, 1), high.at[0], left)
    yield
    third = links.start(part(after, 1), high.at[1], right)
    yield
    fourth = links.start(part(before, 0), low.at[1], left)
    yield
    first.wait_recv()
    low[0] = (low[0].astype(F32) + part(after, 0)[...].astype(F32)).astype(low.dtype)
    fifth = links.start(low.at[0], low.at[2], right)
    second.wait_recv()
    high[0] = (high[0].astype(F32) + part(before, 1)[...].astype(F32)).astype(high.dtype)
    sixth = links.start(high.at[0], high.at[2], left)
    yield
    fourth.wait_recv()
    fifth.wait_recv()
    emit(0, part(me, 0)[...].astype(F32) + low[1].astype(F32) + low[2].astype(F32))
    third.wait_recv()
    sixth.wait_recv()
    emit(1, part(me, 1)[...].astype(F32) + high[1].astype(F32) + high[2].astype(F32))


def direct_reduce(links, places, part, landing, own, emit):
    copies = [links.start(part(at), landing.at[i], at) for i, at in enumerate(places)]
    yield
    total = own[...].astype(F32)
    for i, copy in enumerate(copies):
        copy.wait_recv()
        total = total + landing[i].astype(F32)
    emit(total)


def around(place, steps):
    places = []
    for step in steps:
        at = place
        for axis, by in enumerate(step):
            if by:
                at = shifted(at, axis, by)
        places.append(at)
    return places


def in_turn(*streams):
    waiting = list(streams)
    while waiting:
        still = []
        for stream in waiting:
            try:
                next(stream)
            except StopIteration:
                continue
            still.append(stream)
        waiting = still


def local_norm(field, gain):
    inverse = lax.rsqrt(jnp.mean(field * field, axis=-1, keepdims=True) + EPSILON)
    return field * inverse * gain, inverse


def norm_backward(field, inverse, gain, grad):
    scaled = grad * gain
    grad_gain = jnp.sum(grad * field * inverse, axis=0, keepdims=True)
    mean = jnp.mean(scaled * field, axis=-1, keepdims=True)
    return inverse * scaled - field * (inverse * inverse * inverse) * mean, grad_gain


def dot(left, right, contract=((1,), (0,))):
    return lax.dot_general(left, right, (contract, ((), ())), preferred_element_type=F32)


def whole(count):
    return [pl.BlockSpec(memory_space=pltpu.VMEM)] * count


def shape(dims, dtype):
    return jax.ShapeDtypeStruct(dims, dtype)


def remote_call(kernel, collective_id, outs, copies, scratch, *args, far=0):
    return pl.pallas_call(
        kernel,
        out_shape=outs,
        in_specs=whole(len(args) - far) + [pl.BlockSpec(memory_space=pl.ANY)] * far,
        out_specs=whole(len(outs)),
        scratch_shapes=list(scratch)
        + [pltpu.SemaphoreType.DMA((copies,)), pltpu.SemaphoreType.DMA((copies,))],
        compiler_params=pltpu.CompilerParams(
            collective_id=collective_id, has_side_effects=True, vmem_limit_bytes=VMEM_LIMIT
        ),
    )(*args)


KV_A_STEPS = [(0, dy, dz) for dz in (0, 2) for dy in (0, 1, -1, 2) if dy or dz]
KV_B_STEPS = [(dx, 0, dz) for dz in (0, 2) for dx in (0, 1, -1, 2) if dx or dz]


def enter_kernel(
    tokens, gain, table, w_q, w_k, w_v, bias, cot, row_pick, col_pick, w_o, w_gate, w_up, w_down,
    normed_all, table_all, weight_all, w_o_all, queries, kv_a, kv_b, cot_all, own_units, up_units, down_units, down_rows,
    weight, own_window, up_window, down_window, tall_window, fetched, send, recv,
):
    place = own_place()
    x, y, z, core = place
    f, zh = lax.rem(z, 2), lax.div(z, 2)
    other, up, down, far = partner(place), shifted(place, 2, 1), shifted(place, 2, -1), shifted(place, 2, 2)
    fetches = []

    def fetch(src, dst):
        copy = pltpu.make_async_copy(src, dst, fetched.at[len(fetches)])
        copy.start()
        fetches.append(copy)

    def offset(at):
        part = 4 * lax.rem(at[2], 2) + 2 * lax.div(at[2], 2) + at[3]
        start = jnp.minimum(lax.div(19 * part, 4), 32) * 128
        return start, SLICE * part - start

    windows = ((own_window, place, 0, HALF), (up_window, up, 224, 224), (down_window, down, 0, 224))
    for window, at, row, rows in windows:
        columns = pl.ds(pl.multiple_of(offset(at)[0], 128), 768)
        for which, array in enumerate((w_gate, w_up)):
            fetch(array.at[pl.ds(row, rows), columns], window.at[which])
    sub = 2 * zh + core
    fetch(w_down.at[pl.ds(pl.multiple_of(sub * SLICE, 16), SLICE)], tall_window)
    a_peers = around(place, KV_A_STEPS)
    b_peers = around(place, KV_B_STEPS)
    greet([other, up, down, far] + [at for at in a_peers + b_peers if at is not far])
    links = Links(send, recv)
    base = pl.multiple_of(f * HALF, HALF)

    def core_half(array):
        half = array.shape[1] // 2
        wide = array[...].astype(F32)
        return jnp.where(core == 0, wide[:, :half], wide[:, half:])

    weight[...] = jnp.concatenate(
        [core_half(w_q), core_half(w_k), core_half(w_v), jnp.zeros((HALF, 64), F32)], axis=1
    ).astype(BF16)
    w_down_copy = links.start(weight.at[pl.ds(0, 224)], weight_all.at[pl.ds(base, 224)], down)
    w_up_copy = links.start(weight.at[pl.ds(224, 224)], weight_all.at[pl.ds(base + 224, 224)], up)
    normed, _ = local_norm(tokens[...].astype(F32), gain[...])
    normed_all[core] = normed.astype(BF16)
    n_copy = links.start(normed_all.at[core], normed_all.at[core], other)
    table_all[core] = table[...]
    t_copy = links.start(table_all.at[core], table_all.at[core], other)
    cot_all[z, core] = cot[...]
    c_copy = links.start(cot_all.at[z, core], cot_all.at[z, core], other)
    weight_all[pl.ds(base, HALF)] = weight[...]
    for copy in fetches:
        copy.wait()
    for (window, at, _, rows), out in zip(windows, (own_units, up_units, down_units)):
        line = lax.broadcasted_iota(jnp.int32, (768, PADDED), 0) - offset(at)[1]
        pick = (line == row_pick[...]).astype(F32).astype(BF16)
        for which in range(2):
            out[:, PADDED * which : PADDED * (which + 1)] = dot(window[which], pick).astype(BF16)
    line = lax.broadcasted_iota(jnp.int32, (PADDED, SLICE), 1)
    pick = (line == col_pick[...]).astype(F32).astype(BF16)
    down_rows[...] = dot(pick, tall_window[...]).astype(BF16)
    n_copy.wait_recv()
    t_copy.wait_recv()
    w_down_copy.wait_recv()
    w_up_copy.wait_recv()
    lin = dot(normed_all[...].reshape(256, D), weight_all[...]) + bias[...]
    turn = lin[:, :512]
    lane = lax.broadcasted_iota(jnp.int32, (256, 512), 1)
    swapped = jnp.where(lax.rem(lane, 64) < 32, -pltpu.roll(turn, 480, 1), pltpu.roll(turn, 32, 1))
    both = table_all[...].reshape(256, 128)
    cosine = jnp.concatenate([both[:, :64]] * 8, axis=1)
    sine = jnp.concatenate([both[:, 64:]] * 8, axis=1)
    rotated = turn * cosine + swapped * sine
    kv = jnp.concatenate([rotated[:, HALF:512], lin[:, 512:576]], axis=1).astype(BF16)
    kv_a[x, y, zh] = kv[:128]
    kv_b[x, y, zh] = kv[128:]
    a_copies = [links.start(kv_a.at[x, y, zh], kv_a.at[x, y, zh], at) for at in a_peers]
    b_copies = [links.start(kv_b.at[x, y, zh], kv_b.at[x, y, zh], at) for at in b_peers]
    w_o_all[pl.ds(base, HALF)] = w_o[...]
    queries[...] = (rotated[:, :HALF] * HD**-0.5).astype(BF16)

    def stream_a():
        for copy in a_copies:
            copy.wait_recv()
        yield from ring_gather(
            links, lambda k: kv_a.at[k], lambda k, h: kv_a.at[k, pl.ds(2 * h, 2)], place, 0
        )

    def stream_b():
        for copy in b_copies:
            copy.wait_recv()
        yield from ring_gather(
            links,
            lambda k: kv_b.at[pl.ds(0, 4), k],
            lambda k, h: kv_b.at[pl.ds(2 * h, 2), k],
            place,
            1,
        )

    def stream_o():
        down_copy = links.start(w_o.at[pl.ds(0, 224)], w_o_all.at[pl.ds(base, 224)], down)
        up_copy = links.start(w_o.at[pl.ds(224, 224)], w_o_all.at[pl.ds(base + 224, 224)], up)
        for _ in range(6):
            yield
        down_copy.wait_recv()
        up_copy.wait_recv()

    c_copies = [c_copy]
    in_turn(stream_a(), stream_b(), shared_gather(links, cot_all, place, c_copies), stream_o())
    for copy in c_copies:
        copy.wait_recv()
    links.close()


def shared_gather(links, blocks, place, copies):
    z, core = place[2], place[3]
    other = partner(place)
    ring = ring_gather(
        links,
        lambda k: blocks.at[k, core],
        lambda k, h: blocks.at[k, core, pl.ds(64 * h, 64)],
        place,
        2,
    )
    next(ring)
    yield
    next(ring)
    before = turned(z, -1)
    copies.append(links.start(blocks.at[before, core], blocks.at[before, core], other))
    yield
    next(ring)
    after = turned(z, 1)
    copies.append(links.start(blocks.at[after, core], blocks.at[after, core], other))
    yield
    for _ in ring:
        yield
    last = turned(z, 2)
    copies.append(links.start(blocks.at[last, core], blocks.at[last, core], other))


def down_group(place):
    x, y, z, core = place
    sub = 2 * lax.div(z, 2) + core
    return lax.rem(x + 5 - sub, 4), lax.rem(y + sub, 4)


def feed_kernel(
    mixed, w_o, u_own, u_early, u_late, w_down, cot_all, tokens, gain, owners, owners_half,
    mixed_out, grad_hidden, branch_all, grad_gain, gate_mid, up_mid, down_mid, part_o, *rest,
):
    (
        mixed_all, w_units, hidden, normed_all, spread_t, inner_t, grad_gates, grad_ups, up_all, along_x,
        x_low, x_high, y_low, y_high,
        out_part, out_arrived, out_paired, out_low, out_high,
        grad_part, grad_arrived, grad_paired, grad_low, grad_high, grad_sum, send, recv,
    ) = rest
    place = own_place()
    x, y, z, core = place
    f = lax.rem(z, 2)
    other = partner(place)
    greet([other] + [shifted(place, axis, step) for axis in (0, 1, 2) for step in (1, -1)])
    links = Links(send, recv)
    copy = links.start(mixed, mixed_all.at[core], other)
    mixed_all[core] = mixed[...]
    own_base = pl.multiple_of(f * HALF, HALF)
    base = pl.multiple_of((1 - f) * HALF, HALF)
    copy.wait_recv()
    rows = pl.ds(pl.multiple_of(core * 128, 128), 128)
    field = tokens[...].astype(F32) + (
        dot(mixed_all[0, rows], w_o[:HALF]) + dot(mixed_all[1, rows], w_o[HALF:])
    )
    hidden[...] = field
    normed, _ = local_norm(field, gain[...])
    normed_all[z, core] = normed.astype(BF16)
    own = links.start(normed_all.at[z, core], normed_all.at[z, core], other)

    copies = [own]
    gather = shared_gather(links, normed_all, place, copies)
    next(gather)
    w_units[pl.ds(own_base, HALF)] = u_own[...]
    w_units[pl.ds(base, 224)] = u_early[...]
    w_units[pl.ds(base + 224, 224)] = u_late[...]

    before, after, far = turned(z, -1), turned(z, 1), turned(z, 2)
    both = (
        (out_part, out_arrived, out_paired), (grad_part, grad_arrived, grad_paired),
    )

    def tile(k):
        n = normed_all[k].reshape(256, D)
        c = cot_all[k].reshape(256, D)
        g = dot(n, w_units[:, :PADDED])
        u = dot(n, w_units[:, PADDED:])
        s = 1.0 / (1.0 + jnp.exp(-g))
        silu = g * s
        inner = silu * u
        low = inner.astype(BF16)
        out_part[k] = dot(low, w_down[...]).astype(BF16).reshape(2, 128, D)
        columns = pl.ds(pl.multiple_of(k * 256, 256), 256)
        inner_t[:, columns] = low.T
        gi = dot(c, w_down[...], ((1,), (1,)))
        gg = (gi * u * s * (1.0 + g * (1.0 - s))).astype(BF16)
        gu = (gi * silu).astype(BF16)
        grad_gates[columns] = gg
        grad_ups[columns] = gu
        grad_part[k] = (
            dot(gg, w_units[:, :PADDED], ((1,), (1,))) + dot(gu, w_units[:, PADDED:], ((1,), (1,)))
        ).astype(BF16).reshape(2, 128, D)
        return [links.start(part.at[k, 1 - core], come.at[k], other) for part, come, _ in both]

    def pair_up(k, copies):
        for trip, (part, come, paired) in zip(copies, both):
            trip.wait_recv()
            paired[k] = (come[k].astype(F32) + part[k, core].astype(F32)).astype(BF16)

    def emit_out(h, value):
        at = pl.ds(64 * h, 64)
        mixed_out[at] = (hidden[at] + value).astype(BF16)

    def emit_grad(h, value):
        grad_sum[pl.ds(64 * h, 64)] = value

    reduces = [
        ring_reduce(
            links, lambda k, h, p=paired: p.at[k, pl.ds(64 * h, 64)], low, high, place, 2, emit
        )
        for paired, low, high, emit in (
            (grad_paired, grad_low, grad_high, emit_grad),
            (out_paired, out_low, out_high, emit_out),
        )
    ]

    def advance():
        for stream in reduces:
            next(stream, None)

    copies[0].wait_recv()
    trips_own = tile(z)
    next(gather)
    next(gather)
    copies[2].wait_recv()
    trips_after = tile(after)
    in_turn(gather)
    copies[3].wait_recv()
    trips_far = tile(far)
    pair_up(far, trips_far)
    advance()
    pair_up(after, trips_after)
    advance()
    copies[1].wait_recv()
    trips_before = tile(before)
    pair_up(before, trips_before)
    advance()
    pair_up(z, trips_own)

    @pl.loop(0, 4)
    def _(k):
        columns = pl.ds(pl.multiple_of(k * 256, 256), 256)
        spread_t[:, columns] = dot(
            owners[...], normed_all[k].reshape(256, D), ((1,), (1,))
        ).astype(BF16)

    @pl.loop(0, 4)
    def _(k):
        lines = spread_t[pl.ds(pl.multiple_of(k * 256, 256), 256)]
        along_x[k, :256] = dot(lines, grad_gates[...]).astype(BF16)
        group, _ = down_group((k, y, z, core))
        lines = inner_t[pl.ds(pl.multiple_of(group * 160, 16), 160)]
        tall = dot(lines, cot_all[...].reshape(1024, D)).astype(BF16)
        along_x[k, 256:416] = tall[:, :PADDED]
        along_x[k, 416:496, :256] = tall[:80, PADDED:]
        along_x[k, 416:496, 256:512] = tall[80:, PADDED:]
        along_x[k, 416:496, 512:] = jnp.zeros((80, 128), BF16)

    def put_x(h, value):
        if h == 0:
            gate_mid[...] = value.astype(BF16).reshape(4, 64, PADDED)
            return
        for k in range(4):
            row, lane = 160 + 40 * (k % 2), 256 * (k // 2)
            down_mid[k, :40, :PADDED] = value[40 * k : 40 * (k + 1)].astype(BF16)
            down_mid[k, :40, PADDED:] = value[row : row + 40, lane : lane + 256].astype(BF16)
            down_mid[k, 40:] = jnp.zeros((8, D), BF16)

    def put_y(h, value):
        up_mid[pl.ds(2 * h, 2)] = value.astype(BF16)

    stream_x = ring_reduce(
        links, lambda k, h: along_x.at[k, pl.ds(256 * h, 256 - 16 * h)], x_low, x_high, place, 0, put_x
    )
    stream_y = ring_reduce(
        links, lambda k, h: up_all.at[pl.ds(2 * h, 2), k], y_low, y_high, place, 1, put_y
    )
    for _ in range(3):
        next(stream_x)
    advance()

    @pl.loop(0, 4)
    def _(k):
        lines = spread_t[pl.ds(pl.multiple_of(k * 256, 256), 256)]
        up_all[k] = dot(lines, grad_ups[...]).astype(BF16).reshape(4, 64, PADDED)

    for _ in range(3):
        next(stream_y)
    spread_o = (
        dot(owners_half[0], mixed_all[0], ((1,), (1,))) + dot(owners_half[1], mixed_all[1], ((1,), (1,)))
    ).astype(BF16)
    for _ in range(8):
        advance()
    field = hidden[...]
    _, inverse = local_norm(field, gain[...])
    through, gains = norm_backward(field, inverse, gain[...], grad_sum[...])
    grad_gain[...] = gains
    total = cot_all[z, core].astype(F32) + through
    grad_hidden[...] = total
    branch_all[core] = total.astype(BF16)
    trip = links.start(branch_all.at[core], branch_all.at[core], other)
    next(stream_x)
    next(stream_y)
    trip.wait_recv()
    branch = branch_all[...].reshape(256, D).astype(F32)
    half = jnp.where(core == 0, branch[:, :HALF], branch[:, HALF:]).astype(BF16)
    part_o[...] = dot(spread_o, half).astype(BF16).reshape(4, 4, 4, 16, HALF)
    in_turn(stream_y, stream_x)
    links.close()


def finish_kernel(
    kv_part_a, kv_part_b, grad_query, table_all, weight_all, normed_all, owners, grad_hidden, tokens, gain,
    gain_mlp_grad, col_pick, gate_mid, up_mid, down_mid, part_o, *rest,
):
    (
        d_tokens, wq_out, wk_out, wv_out, wo_out, gate_out, up_out, down_out, vector_out,
        grad_kv, kv_mid_a, kv_mid_b, kv_land_a, kv_land_b, part_qa, part_qb, grad_normed, half_sum,
        gate_land, up_land, down_land, down_end, down_own, end, rows_all,
        o_first, o_mid, o_land, o_end, o_rows, qa_mid, qa_land, qa_end, qa_rows, qb_mid, qb_land, qb_end, qb_rows,
        vec_now, vec_in,
        a_low, a_high, b_low, b_high, qa_low, qa_high, qb_low, qb_high, send, recv,
    ) = rest
    place = own_place()
    x, y, z, core = place
    f, zh = lax.rem(z, 2), lax.div(z, 2)
    sub = 2 * zh + core
    other = partner(place)
    mine = z * 2 + core
    x_peers, y_peers = around(place, X_STEPS), around(place, Y_STEPS)
    xy_peers, xz_peers, yz_peers = (
        around(place, steps) for steps in (XY_STEPS, XZ_STEPS, YZ_STEPS)
    )
    z_peers = around(place, Z_STEPS)
    ring = []
    for step in range(1, 8):
        at = lax.rem(mine + step, 8)
        ring.append((x, y, lax.div(at, 2), lax.rem(at, 2)))
    first, second = down_group(place)
    to_owner = (sub, first, 2 * lax.div(second, 2) + f, lax.rem(second, 2))
    from_group = (lax.rem(x + y + 3, 4), lax.rem(sub + 4 - x, 4), 2 * lax.div(x, 2) + f, lax.rem(x, 2))
    greet(ring + xy_peers + xz_peers[3:] + yz_peers[3:] + [to_owner, from_group])
    links = Links(send, recv)

    def kv_stream(part, mid, landing, order, low, high, peers, base):
        def put_mid(h, value):
            mid[pl.ds(2 * h, 2)] = value.astype(BF16)

        def put_end(value):
            grad_kv[pl.ds(base, 128)] = value

        if order == 0:
            first = lambda k, h: part.at[k, pl.ds(2 * h, 2)]
        else:
            first = lambda k, h: part.at[pl.ds(2 * h, 2), k]
        yield from ring_reduce(links, first, low, high, place, order, put_mid)
        keep = 1 - order
        yield from direct_reduce(
            links, peers, lambda at: mid.at[at[keep], lax.div(at[2], 2)], landing,
            mid.at[place[keep], zh], put_end,
        )

    def to_rows(end, rows):
        last = links.start(end.at[1 - core], rows.at[core], other)
        rows[core] = end[core]
        yield
        last.wait_recv()

    def q_stream(part, mid, landing, end, rows, order, low, high, peers):
        def put_mid(h, value):
            mid[pl.ds(2 * h, 2)] = value.astype(BF16)

        def put_end(value):
            end[0], end[1] = value[:8], value[8:]

        if order == 0:
            first = lambda k, h: part.at[k, pl.ds(2 * h, 2)]
        else:
            first = lambda k, h: part.at[pl.ds(2 * h, 2), k]
        yield from ring_reduce(links, first, low, high, place, order, put_mid)
        keep = 1 - order
        yield from direct_reduce(
            links, peers, lambda at: mid.at[at[keep], at[2]], landing, mid.at[place[keep], z], put_end
        )
        yield from to_rows(end, rows)

    def o_stream():
        def put_end(value):
            o_end[0], o_end[1] = value[:8], value[8:]

        def put_mid(value):
            o_mid[...] = value.astype(BF16)

        def part(at):
            return part_o.at[pl.ds(0, 4), pl.ds(0, 4), at[2]]

        yield from direct_reduce(links, z_peers, part, o_first, part(place), put_mid)
        yield from direct_reduce(
            links, xy_peers, lambda at: o_mid.at[at[0], at[1]], o_land, o_mid.at[x, y], put_end
        )
        yield from to_rows(o_end, o_rows)

    def wide(mid, landing, axis, peers, column):
        def put_end(value):
            end[:, :, pl.ds(column, PADDED)] = value.reshape(8, 8, PADDED)

        yield from direct_reduce(
            links, peers, lambda at: mid.at[at[axis]], landing, mid.at[place[axis]], put_end
        )

    def tall():
        def put_end(value):
            down_end[...] = value[:40]

        yield from direct_reduce(
            links, y_peers, lambda at: down_mid.at[down_group(at)[1]], down_land, down_mid.at[second], put_end
        )
        copy = links.start(down_end, down_own, to_owner)
        yield
        copy.wait_recv()
        down_out[...] = down_own[:38]

    def hidden_units():
        gates = wide(gate_mid, gate_land, 1, y_peers, 0)
        ups = wide(up_mid, up_land, 0, x_peers, PADDED)
        next(gates)
        next(ups)
        yield
        for stream in (gates, ups):
            for _ in stream:
                pass
        copies = [
            links.start(end.at[to[2] * 2 + to[3]], rows_all.at[mine], to) for to in ring
        ]
        rows_all[mine] = end[mine]
        yield
        line = lax.broadcasted_iota(jnp.int32, (PADDED, SLICE), 1)
        pick = (line == col_pick[...]).astype(F32).astype(BF16)
        for copy in copies:
            copy.wait_recv()
        for which, out in enumerate((gate_out, up_out)):
            values = rows_all[:, :, PADDED * which : PADDED * (which + 1)].reshape(64, PADDED)
            top = values.astype(BF16)
            below = (values - top.astype(F32)).astype(BF16)
            units = dot(top, pick) + dot(below, pick)
            for at in range(8):
                part = 4 * (at // 2 % 2) + 2 * (at // 4) + at % 2
                out[:, SLICE * part : SLICE * (part + 1)] = units[8 * at : 8 * at + 7]

    kv_streams = [
        kv_stream(kv_part_a, kv_mid_a, kv_land_a, 0, a_low, a_high, yz_kv(place), 0),
        kv_stream(kv_part_b, kv_mid_b, kv_land_b, 1, b_low, b_high, xz_kv(place), 128),
    ]
    units, talls, os = hidden_units(), tall(), o_stream()
    for _ in range(3):
        for stream in kv_streams:
            next(stream)
    next(os)
    spread_n = dot(owners[...], normed_all[...].reshape(256, D), ((1,), (1,))).astype(BF16)
    for stream in kv_streams:
        next(stream)
    next(units)
    next(talls)
    in_turn(*kv_streams)
    next(units)
    next(talls)

    table = table_all[...].reshape(256, 128)
    cosine = jnp.concatenate([table[:, :64]] * 8, axis=1)
    sine = jnp.concatenate([table[:, 64:]] * 8, axis=1)
    turn = jnp.concatenate([grad_query[...] * HD**-0.5, grad_kv[:, :64]], axis=1)
    scaled = turn * sine
    lane = lax.broadcasted_iota(jnp.int32, (256, 512), 1)
    swapped = jnp.where(
        lax.rem(lane, 64) < 32, pltpu.roll(scaled, 480, 1), -pltpu.roll(scaled, 32, 1)
    )
    lin = jnp.concatenate(
        [turn * cosine + swapped, grad_kv[:, 64:], jnp.zeros((256, 64), F32)], axis=1
    ).astype(BF16)
    part = dot(spread_n, lin).astype(BF16)
    part_qa[...] = part[:, :384].reshape(4, 4, 4, 16, 384)
    part_qb[...] = part[:, 384:].reshape(4, 4, 4, 16, 256)
    q_streams = [
        q_stream(part_qa, qa_mid, qa_land, qa_end, qa_rows, 0, qa_low, qa_high, yz_peers),
        q_stream(part_qb, qb_mid, qb_land, qb_end, qb_rows, 1, qb_low, qb_high, xz_peers),
    ]
    for _ in range(3):
        for stream in q_streams:
            next(stream)

    def sums():
        grad_normed[...] = dot(lin, weight_all[...], ((1,), (1,))).reshape(2, 128, D)
        copy = links.start(grad_normed.at[1 - core], half_sum, other)
        column = jnp.sum(lin.astype(F32), axis=0, keepdims=True)

        def placed(values):
            empty = jnp.zeros_like(values)
            return jnp.where(
                core == 0,
                jnp.concatenate([values, empty], axis=1),
                jnp.concatenate([empty, values], axis=1),
            )

        biases = [placed(column[:, low:high]) for low, high in ((0, HALF), (HALF, 512), (512, 576))]
        copy.wait_recv()
        grad = grad_normed[core] + half_sum[...]
        field = tokens[...].astype(F32)
        _, inverse = local_norm(field, gain[...])
        through, gains = norm_backward(field, inverse, gain[...], grad)
        d_tokens[...] = grad_hidden[...] + through
        vec_now[0] = jnp.concatenate(
            [gains, gain_mlp_grad[...], *biases, jnp.zeros((1, 128), F32)], axis=1
        )
        trip = links.start(vec_now.at[0], vec_in.at[0], other)
        trip.wait_recv()
        vec_now[1] = vec_now[0] + vec_in[0]
        for stage, axis in enumerate((2, 1, 0)):
            trips = [
                links.start(
                    vec_now.at[1 + stage],
                    vec_in.at[1 + 3 * stage + at],
                    shifted(place, axis, step),
                )
                for at, step in enumerate((1, -1, 2))
            ]
            yield
            for trip in trips:
                trip.wait_recv()
            at = 1 + 3 * stage
            near = vec_in[at] + vec_in[at + 1]
            vec_now[2 + stage] = (vec_now[1 + stage] + vec_in[at + 2]) + near
        vector_out[...] = vec_now[4]

    in_turn(sums(), *q_streams, os, units, talls)

    def row_of(core_at):
        return jnp.concatenate([qa_rows[core_at], qb_rows[core_at]], axis=1)[:7]

    first, second = row_of(0), row_of(1)
    for out, low, high in ((wq_out, 0, HALF), (wk_out, HALF, 512), (wv_out, 512, 576)):
        out[...] = jnp.concatenate([first[:, low:high], second[:, low:high]], axis=1)
    wo_out[...] = jnp.concatenate([o_rows[0][:7], o_rows[1][:7]], axis=1)
    links.close()


AROUND = (0, 1, -1, 2)
X_STEPS = [(d, 0, 0) for d in AROUND[1:]]
Y_STEPS = [(0, d, 0) for d in AROUND[1:]]
Z_STEPS = [(0, 0, d) for d in AROUND[1:]]
XY_STEPS = [(dx, dy, 0) for dy in AROUND for dx in AROUND if dx or dy]
XZ_STEPS = [(dx, 0, dz) for dz in AROUND for dx in AROUND if dx or dz]
YZ_STEPS = [(0, dy, dz) for dz in AROUND for dy in AROUND if dy or dz]


def yz_kv(place):
    return around(place, KV_A_STEPS)


def xz_kv(place):
    return around(place, KV_B_STEPS)


def tidy_kernel(*refs):
    half = len(refs) // 2
    for src, dst in zip(refs[:half], refs[half:]):
        dst[...] = src[...]


def natural_order(order, kv_a, kv_b, kv, kv_t):
    @pl.loop(0, 32)
    def _(chip):
        for t in range(4):
            block = kv_a[chip, pl.ds(64 * t, 64)] if t < 2 else kv_b[chip, pl.ds(64 * (t - 2), 64)]
            at = pl.multiple_of(order[4 * chip + t] * 64, 64)
            kv[pl.ds(at, 64)] = block

    @pl.loop(0, 8192 // CHUNK)
    def _(c):
        kv_t[c] = kv[pl.ds(pl.multiple_of(c * CHUNK, CHUNK), CHUNK)].T


def allowed_at(c, base):
    key = c * CHUNK + lax.broadcasted_iota(jnp.int32, (CHUNK, HALF), 0)
    lane = lax.broadcasted_iota(jnp.int32, (CHUNK, HALF), 1)
    return key <= base + lax.rem(lane, 64)


def by_head(rows):
    return jnp.concatenate([rows[:, 64 * h : 64 * (h + 1)] for h in range(7)], axis=0)


def side_by_side(columns_t):
    stacked = columns_t.T
    return jnp.concatenate([stacked[64 * h : 64 * (h + 1)] for h in range(7)], axis=1)


def attend_kernel(order, owned, kv_a, kv_b, queries, out_t, lse, mixed, kv, kv_t, acc):
    natural_order(order, kv_a, kv_b, kv, kv_t)
    none = jnp.zeros((64, HALF), F32)
    for t in range(4):
        spot = owned[t]
        rows = by_head(queries[64 * t : 64 * (t + 1)].astype(F32))
        q_t = jnp.concatenate([rows.T, none], axis=0).astype(BF16)
        last = lax.div(spot * 64, CHUNK)
        acc[...] = jnp.zeros_like(acc)

        def step(c, carry, masked):
            top, total = carry
            scores = dot(kv[pl.ds(pl.multiple_of(c * CHUNK, CHUNK), CHUNK)], q_t)
            if masked:
                scores = jnp.where(allowed_at(c, spot * 64), scores, MASKED)
            new_top = jnp.maximum(top, jnp.max(scores, axis=0, keepdims=True))
            probs = jnp.exp(scores - new_top)
            scale = jnp.exp(top - new_top)
            total = total * scale + jnp.sum(probs, axis=0, keepdims=True)
            acc[...] = acc[...] * scale + dot(kv_t[c, pl.ds(64, 64)], probs.astype(BF16))
            return new_top, total

        start = (jnp.full((1, HALF), MASKED, F32), jnp.zeros((1, HALF), F32))
        carry = lax.fori_loop(0, last, lambda c, carry: step(c, carry, False), start)
        top, total = step(last, carry, True)
        result = acc[...] / total
        out_t[t] = result
        mixed[64 * t : 64 * (t + 1)] = side_by_side(result).astype(BF16)
        lse[t] = top + jnp.log(total)


def attend_back_kernel(
    order, owned, kv_a, kv_b, queries, branch, w_o, out_t, lse,
    grad_query, grad_a, grad_b, kv, kv_t, acc, acc_q,
):
    natural_order(order, kv_a, kv_b, kv, kv_t)
    acc[...] = jnp.zeros_like(acc)
    grad_mixed = dot(
        branch[...].reshape(256, D), w_o[pl.ds(pl.multiple_of(owned[4] * HALF, HALF), HALF)], ((1,), (1,))
    )
    none_t, none = jnp.zeros((64, HALF), F32), jnp.zeros((HALF, 64), F32)
    for t in range(4):
        spot = owned[t]
        last = lax.div(spot * 64, CHUNK)
        rows = by_head(queries[64 * t : 64 * (t + 1)].astype(F32))
        q = jnp.concatenate([rows, none], axis=1).astype(BF16)
        q_t = jnp.concatenate([rows.T, none_t], axis=0).astype(BF16)
        rows = by_head(grad_mixed[64 * t : 64 * (t + 1)].astype(BF16).astype(F32))
        g = jnp.concatenate([none, rows], axis=1).astype(BF16)
        rows_t = rows.T
        g_t = jnp.concatenate([none_t, rows_t], axis=0).astype(BF16)
        delta = jnp.sum(rows_t * out_t[t], axis=0, keepdims=True)
        norm = lse[t]
        acc_q[...] = jnp.zeros_like(acc_q)

        def step(c, masked):
            rows = pl.ds(pl.multiple_of(c * CHUNK, CHUNK), CHUNK)
            block = kv[rows]
            scores = dot(block, q_t)
            if masked:
                scores = jnp.where(allowed_at(c, spot * 64), scores, MASKED)
            probs = jnp.exp(scores - norm)
            grad_probs = dot(block, g_t)
            grad_scores = (probs * (grad_probs - delta)).astype(BF16)
            acc[rows] += dot(probs.astype(BF16), g) + dot(grad_scores, q)
            acc_q[...] += dot(kv_t[c, pl.ds(0, 64)], grad_scores)

        def body(c, carry):
            step(c, False)
            return carry

        lax.fori_loop(0, last, body, 0)
        step(last, True)
        grad_query[64 * t : 64 * (t + 1)] = side_by_side(acc_q[...])

    @pl.loop(0, 32)
    def _(chip):
        for t in range(4):
            at = pl.multiple_of(order[4 * chip + t] * 64, 64)
            block = acc[pl.ds(at, 64)].astype(BF16)
            if t < 2:
                grad_a[chip, pl.ds(64 * t, 64)] = block
            else:
                grad_b[chip, pl.ds(64 * (t - 2), 64)] = block


def local_call(kernel, outs, scratch, scalars, flops, *args):
    return pl.pallas_call(
        kernel,
        out_shape=outs,
        in_specs=[pl.BlockSpec(memory_space=pltpu.SMEM)] * scalars + whole(len(args) - scalars),
        out_specs=[pl.BlockSpec(memory_space=pltpu.VMEM)] * len(outs),
        scratch_shapes=scratch,
        compiler_params=pltpu.CompilerParams(vmem_limit_bytes=VMEM_LIMIT),
        cost_estimate=pl.CostEstimate(flops=flops, bytes_accessed=8 << 20, transcendentals=1 << 23),
    )(*args)


def padded_columns():
    col = np.arange(PADDED)
    return np.where(col % 40 < 38, col // 40 * 38 + col % 40, -(1 << 20)).astype(np.int32)


def owner_rows():
    row = np.arange(1024)
    i, core, z, y, x = row % 8, row // 8 % 2, row // 16 % 4, row // 64 % 4, row // 256
    at = 7 * (64 * (z % 2) + 16 * x + 4 * y + 2 * (z // 2) + core) + i
    pick = np.zeros((1024, D), np.float32)
    keep = i < 7
    pick[row[keep], at[keep]] = 1.0
    return pick


def index_of(x, y, z, core):
    return (z % 2) * 64 + (x * 4 + y) * 4 + 2 * (z // 2) + core


def permutation(move):
    pairs = []
    for x in range(4):
        for y in range(4):
            for z in range(4):
                for core in range(2):
                    pairs.append((index_of(x, y, z, core), index_of(*move(x, y, z, core))))
    return pairs


BOTH = ("fsdp", "ctx")


def per_device(
    tokens, block_index, positions, cotangent, norm_attn, w_q, b_q, w_k, b_k, w_v, b_v, w_o,
    norm_mlp, w_gate, w_up, w_down,
):
    f, c = lax.axis_index("fsdp"), lax.axis_index("ctx")
    core, zh = c % 2, (c // 2) % 2
    z = 2 * zh + f
    sub = 2 * zh + core
    field, cot = tokens[0], cotangent[0]
    order = block_index[0]
    owned = lax.dynamic_slice_in_dim(order, 4 * (c // 2), 4, 0)
    owned = jnp.concatenate([owned, core[None]])
    gain_attn = norm_attn.astype(F32)[None]
    gain_mlp = norm_mlp.astype(F32)[None]

    freq = THETA ** (-(jnp.arange(HD // 2, dtype=F32) * 2.0 / HD))
    angle = positions[0].astype(F32)[:, None] * freq[None, :]
    cosine, sine = jnp.cos(angle), jnp.sin(angle)
    table = jnp.concatenate([cosine, cosine, sine, sine], -1)

    def core_columns(array):
        half = array.shape[-1] // 2
        return jnp.where(core == 0, array[..., :half], array[..., half:])

    bias = jnp.concatenate(
        [core_columns(b_q), core_columns(b_k), core_columns(b_v), jnp.zeros((64,), BF16)], axis=0
    ).astype(F32)[None]

    picked = padded_columns()
    row_pick, col_pick = jnp.asarray(picked[None]), jnp.asarray(picked[:, None])
    owners = owner_rows()
    owners_half = jnp.asarray(np.stack([owners[:, :HALF], owners[:, HALF:]]), BF16)
    owners = jnp.asarray(owners, BF16)

    (
        normed_all, table_all, weight_all, w_o_all, queries, kv_a, kv_b, cot_all,
        own_units, up_units, down_units, down_weight,
    ) = remote_call(
        enter_kernel,
        0,
        [
            shape((2, 128, D), BF16),
            shape((2, 128, 128), F32),
            shape((D, PADDED), BF16),
            shape((D, D), BF16),
            shape((256, HALF), BF16),
            shape((4, 4, 2, 128, 128), BF16),
            shape((4, 4, 2, 128, 128), BF16),
            shape((4, 2, 128, D), BF16),
            shape((HALF, 2 * PADDED), BF16),
            shape((224, 2 * PADDED), BF16),
            shape((224, 2 * PADDED), BF16),
            shape((PADDED, D), BF16),
        ],
        40,
        [
            pltpu.VMEM((HALF, PADDED), BF16),
            pltpu.VMEM((2, HALF, 768), BF16),
            pltpu.VMEM((2, 224, 768), BF16),
            pltpu.VMEM((2, 224, 768), BF16),
            pltpu.VMEM((SLICE, D), BF16),
            pltpu.SemaphoreType.DMA((7,)),
        ],
        field, gain_attn, table, w_q, w_k, w_v, bias, cot, row_pick, col_pick, w_o, w_gate, w_up, w_down,
        far=3,
    )

    to_up = permutation(lambda x, y, z, core: (x, y, (z + 1) % 4, core))
    to_down = permutation(lambda x, y, z, core: (x, y, (z + 3) % 4, core))
    u_late, u_early = lax.ppermute(up_units, BOTH, to_up), lax.ppermute(down_units, BOTH, to_down)

    kv_a, kv_b = kv_a.reshape(32, 128, 128), kv_b.reshape(32, 128, 128)
    natural = [pltpu.VMEM((8192, 128), BF16), pltpu.VMEM((8192 // CHUNK, 128, CHUNK), BF16)]
    out_t, lse, mixed = local_call(
        attend_kernel,
        [shape((4, 64, HALF), F32), shape((4, 1, HALF), F32), shape((256, HALF), BF16)],
        natural + [pltpu.VMEM((64, HALF), F32)],
        2,
        8 << 30,
        order, owned, kv_a, kv_b, queries,
    )

    def pair(dims, dtype=BF16, other=None):
        return [pltpu.VMEM((3,) + dims, dtype), pltpu.VMEM((3,) + (other or dims), dtype)]

    exchange = [pltpu.VMEM((4, 2, 128, D), BF16)] + [pltpu.VMEM((4, 128, D), BF16)] * 2 + pair((64, D))
    blocks = [
        shape((4, 64, PADDED), BF16),
        shape((4, 64, PADDED), BF16),
        shape((4, 48, D), BF16),
        shape((4, 4, 4, 16, HALF), BF16),
    ]
    mixed_out, grad_hidden, branch_all, grad_gain_mlp, *parts = remote_call(
        feed_kernel,
        1,
        [shape((128, D), BF16), shape((128, D), F32), shape((2, 128, D), BF16), shape((1, D), F32)] + blocks,
        48,
        [
            pltpu.VMEM((2, 256, HALF), BF16),
            pltpu.VMEM((D, 2 * PADDED), BF16),
            pltpu.VMEM((128, D), F32),
            pltpu.VMEM((4, 2, 128, D), BF16),
            pltpu.VMEM((1024, 1024), BF16),
            pltpu.VMEM((PADDED, 1024), BF16),
            pltpu.VMEM((1024, PADDED), BF16),
            pltpu.VMEM((1024, PADDED), BF16),
            pltpu.VMEM((4, 4, 64, PADDED), BF16),
            pltpu.VMEM((4, 496, PADDED), BF16),
        ]
        + pair((256, PADDED), BF16, (240, PADDED))
        + pair((2, 64, PADDED))
        + exchange
        + exchange
        + [pltpu.VMEM((128, D), F32)],
        mixed, w_o_all, own_units, u_early, u_late, down_weight, cot_all, field, gain_mlp, owners, owners_half,
    )

    grad_query, part_a, part_b = local_call(
        attend_back_kernel,
        [shape((256, HALF), F32), shape((32, 128, 128), BF16), shape((32, 128, 128), BF16)],
        natural + [pltpu.VMEM((8192, 128), F32), pltpu.VMEM((64, HALF), F32)],
        2,
        24 << 30,
        order, owned, kv_a, kv_b, queries, branch_all, w_o_all, out_t, lse,
    )

    def rows_of(columns):
        return [
            pltpu.VMEM((4, 4, 16, columns), BF16),
            pltpu.VMEM((15, 16, columns), BF16),
            pltpu.VMEM((2, 8, columns), F32),
            pltpu.VMEM((2, 8, columns), F32),
        ]

    chips = (4, 4, 2, 128, 128)
    finals = [
        shape((128, D), F32),
        shape((7, D), F32),
        shape((7, 128), F32),
        shape((7, 128), F32),
        shape((7, D), F32),
        shape((7, FF), F32),
        shape((7, FF), F32),
        shape((38, D), F32),
        shape((1, 3072), F32),
    ]
    *results, vector = remote_call(
        finish_kernel,
        2,
        finals,
        130,
        [
            pltpu.VMEM((256, 128), F32),
            pltpu.VMEM((4, 2, 128, 128), BF16),
            pltpu.VMEM((4, 2, 128, 128), BF16),
            pltpu.VMEM((7, 128, 128), BF16),
            pltpu.VMEM((7, 128, 128), BF16),
            pltpu.VMEM((4, 4, 4, 16, 384), BF16),
            pltpu.VMEM((4, 4, 4, 16, 256), BF16),
            pltpu.VMEM((2, 128, D), F32),
            pltpu.VMEM((128, D), F32),
        ]
        + [pltpu.VMEM((3, 64, PADDED), BF16)] * 2
        + [pltpu.VMEM((3, 48, D), BF16), pltpu.VMEM((40, D), F32), pltpu.VMEM((40, D), F32)]
        + [pltpu.VMEM((8, 8, 2 * PADDED), F32)] * 2
        + [pltpu.VMEM((3, 4, 4, 16, HALF), BF16)]
        + rows_of(HALF)
        + rows_of(384)
        + rows_of(256)
        + [pltpu.VMEM((5, 1, 3072), F32), pltpu.VMEM((10, 1, 3072), F32)]
        + pair((2, 2, 128, 128)) * 2
        + pair((2, 4, 16, 384))
        + pair((2, 4, 16, 256)),
        part_a.reshape(chips), part_b.reshape(chips), grad_query, table_all, weight_all, normed_all, owners,
        grad_hidden, field, gain_attn, grad_gain_mlp, col_pick, *parts,
    )
    tidied = pl.pallas_call(
        tidy_kernel,
        out_shape=[shape((128, D), BF16)] + finals[:-1],
        in_specs=whole(len(finals)),
        out_specs=whole(len(finals)),
        compiler_params=pltpu.CompilerParams(vmem_limit_bytes=VMEM_LIMIT),
    )(mixed_out, *results)
    mixed_out, d_tokens, *grads = tidied
    sums = vector[0]
    return (
        mixed_out[None],
        d_tokens[None],
        *grads,
        sums[:D],
        sums[D : 2 * D],
        sums[2 * D : 3 * D],
        sums[3 * D : 3 * D + 128],
        sums[3 * D + 128 : 3 * D + 256],
    )


def solution(mesh):
    rows, flat = P("fsdp", None), P(("fsdp", "ctx"), None)
    field = P("fsdp", "ctx", None)
    return jax.shard_map(
        per_device,
        mesh=mesh,
        in_specs=(
            field, rows, P("fsdp", "ctx"), field, P(), rows, P(), rows, P(), rows, P(), rows, P(),
            rows, rows, rows,
        ),
        out_specs=(field, field) + (flat,) * 7 + (P(),) * 5,
        check_vma=False,
    )
```
